32 devices in a mesh: groups: 2 (over x), tensor: 8 (over z, y), pool: 2 (over core).
Axes of the slice: x: 2, y: 2, z: 4, core: 2. Of those that a mesh axis runs over, the one named last changes fastest.
Arguments:
- tokens: bfloat16 [16, 32, 8192], P(('groups', 'pool'), None, 'tensor'), parts along dimension 0, may hold values from -6 to 6
- mamba_in_weight: bfloat16 [8192, 2, 8192], P(None, None, 'tensor'), may hold values from -0.0625 to 0.0625
- state_projection: bfloat16 [8192, 640], P('tensor'), may hold values from -0.0625 to 0.0625
- inner_taps: bfloat16 [4, 8192], P(None, 'tensor'), may hold values from -3 to 3
- state_taps: bfloat16 [4, 512], replicated, may hold values from -3 to 3
- inner_history: bfloat16 [16, 3, 8192], P(('groups', 'pool'), None, 'tensor'), parts along dimension 0, may hold values from -6 to 6
- state_history: float32 [16, 3, 512], P(('groups', 'pool')), parts along dimension 0, may hold values from -6 to 6
- step_size_bias: float32 [128], P('tensor'), may hold values from -3 to 0
- log_decay_rate: float32 [128], P('tensor'), may hold values from -2 to 2
- skip_factor: float32 [128], P('tensor'), may hold values from 0.5 to 1.5
- gated_norm_gain: float32 [8192], P('tensor'), may hold values from 0.5 to 1.5
- mamba_out_weight: bfloat16 [8192, 8192], P('tensor'), may hold values from -0.0625 to 0.0625
- saved_state_pool: float32 [24, 128, 64, 256], P(('groups', 'pool'), 'tensor'), parts along dimension 0, may hold values from -6 to 6
- tenant_state_slot: int32 [16], P(('groups', 'pool')), parts along dimension 0, may hold values from 0 to 11, as said below
- attention_gain: float32 [8192], replicated, may hold values from 0.5 to 1.5
- query_matrix: bfloat16 [8192, 8192], P(None, 'tensor'), may hold values from -1 to 1
- adapter_down: bfloat16 [16, 8192, 64], P(None, 'tensor'), may hold values from -0.0625 to 0.0625
- adapter_up: bfloat16 [16, 64, 8192], P(None, None, 'tensor'), may hold values from -0.75 to 0.75
- tenant_adapter: int32 [16], P(('groups', 'pool')), parts along dimension 0, may hold values from 0 to 15
- key_value_weight: bfloat16 [8192, 2048], P('tensor'), may hold values from -0.0625 to 0.0625
- key_value_pool: bfloat16 [128, 32, 2048], P(('groups', 'tensor')), parts along dimension 0, may hold values from -6 to 6
- tenant_blocks: int32 [16, 8], P(('groups', 'pool')), parts along dimension 0, may hold values from 0 to 63, as said below
- cached_length: int32 [16], P(('groups', 'pool')), parts along dimension 0, may hold values from 1 to 256
- attention_out_weight: bfloat16 [8192, 8192], P('tensor'), may hold values from -0.0625 to 0.0625
Outputs:
- second: bfloat16 [16, 32, 8192], P(('groups', 'pool'), None, 'tensor'), parts along dimension 0
- final_state: float32 [16, 128, 64, 256], P(('groups', 'pool'), 'tensor'), parts along dimension 0
The draws below stay inside these ranges and needn't reach their ends.
There are 2 independent parts, one for each index of `groups`. The reference program is written for one: setup_inputs(seed, part) draws one part's arguments, and reference() takes and returns one part's arrays. A program takes and returns all parts, laid end to end along the dimension named above; an argument that names none is the same for every part. Nothing has to cross between parts.
Inputs may be any that keep to these rules, and one draw needn't show every extreme that they name: `tenant_state_slot`: distinct slots. `tenant_blocks`: every pool block appears exactly once in the table.
All inputs are finite; a program needn't handle non-finite values.
Results may differ from the reference program's by a relative error of at most 0.0095.
Values may be sent and summed in bfloat16 or wider, within the bound.
No kernel may reach another device: no remote copies, remote signals or barrier semaphores. Data moves between devices by JAX's collectives and lax.ppermute only.
A program may use at most 320 MiB of HBM per device.

```python
import jax
import jax.numpy as jnp
from jax import lax

MODEL_WIDTH = 8192
MHEADS = 128
HDIM = 64
STATE = 256
QUERY_HEADS = 64
KEY_HEADS = 8
HEAD_SIZE = 128
ADAPTER_RANK = 64
TEN = 8
SLOTS = 12
ADAPTER_POOL = 16
BLK = 32
SPAN = 32
CTX_BLOCKS = 8
INNER = 8192
BLOCKS = 64
CONTEXT = 256


def with_ends(key, values, smallest, largest):
    places = jax.random.permutation(key, values.shape[0])
    return values.at[places[0]].set(smallest).at[places[1]].set(largest)


def draw_tokens(key, part):
    key = jax.random.fold_in(key, 53)
    shape = (TEN, SPAN, MODEL_WIDTH)
    return jax.random.truncated_normal(key, -6.0, 6.0, shape, jnp.float32).astype(jnp.bfloat16)


def draw_query_matrix(key, part):
    key = jax.random.fold_in(key, 61)
    noise_key = jax.random.fold_in(key, 0)
    shape = (MODEL_WIDTH, QUERY_HEADS * HEAD_SIZE)
    return (jax.random.truncated_normal(noise_key, -6.0, 6.0, shape, jnp.float32) * MODEL_WIDTH ** (-0.5)).astype(jnp.bfloat16)


def draw_key_value_pool(key, part):
    key = jax.random.fold_in(key, 67)
    base_key = jax.random.fold_in(key, 0)
    shape = (BLOCKS, BLK, 2 * KEY_HEADS * HEAD_SIZE)
    return jax.random.truncated_normal(base_key, -6.0, 6.0, shape, jnp.float32).astype(jnp.bfloat16)


def draw_tenant_state_slot(key, part):
    key = jax.random.fold_in(key, 11)
    first_key, second_key = jax.random.split(key)
    middle = jax.random.permutation(first_key, SLOTS - 2)[:TEN - 2].astype(jnp.int32) + 1
    chosen = jnp.concatenate([jnp.array([0, SLOTS - 1], jnp.int32), middle])
    return jax.random.permutation(second_key, chosen).astype(jnp.int32)


def draw_tenant_adapter(key, part):
    key = jax.random.fold_in(key, 23)
    first_key, second_key = jax.random.split(key)
    values = jax.random.randint(first_key, (TEN,), 0, ADAPTER_POOL).astype(jnp.int32)
    return with_ends(second_key, values, 0, ADAPTER_POOL - 1).astype(jnp.int32)


def draw_tenant_blocks(key, part):
    key = jax.random.fold_in(key, 37)
    return jax.random.permutation(key, BLOCKS).astype(jnp.int32).reshape(TEN, CTX_BLOCKS)


def draw_cached_length(key, part):
    key = jax.random.fold_in(key, 41)
    first_key, second_key = jax.random.split(key)
    values = jax.random.randint(first_key, (TEN,), 1, CONTEXT + 1).astype(jnp.int32)
    return with_ends(second_key, values, 1, CONTEXT).astype(jnp.int32)


def block_levels(own_key, shape, cuts, low, high):
    def one(dim, blocks):
        heights = jax.random.uniform(jax.random.fold_in(jax.random.fold_in(own_key, 6), dim), (blocks,), jnp.float32, low / len(cuts), high / len(cuts))
        return jnp.repeat(jnp.exp(heights), shape[dim] // blocks).reshape((-1,) + (1,) * (len(shape) - dim - 1))

    gain = one(*cuts[0])
    for cut in cuts[1:]:
        gain = gain * one(*cut)
    return gain


def centred(key, dims, scale, most, cuts=(), kind=jnp.bfloat16):
    entries = jax.random.normal(key, dims, jnp.float32) * scale
    if len(cuts) > 0:
        entries = block_levels(key, dims, cuts, -0.22, 0.18) * entries
    return jnp.clip(entries, min=-most, max=most).astype(kind)


def setup_inputs(seed: int = 0, part: int = 0) -> dict:
    key_list = jax.random.split(jax.random.key(seed), 25)
    part_keys = jax.random.split(jax.random.fold_in(key_list[24], part), 25)
    tokens = draw_tokens(jax.random.fold_in(jax.random.fold_in(key_list[24], part), 71), part)
    mamba_in_weight = centred(key_list[1], (MODEL_WIDTH, 2, INNER), MODEL_WIDTH ** -0.5, 0.0625, ((2, 8),))
    state_projection = centred(key_list[2], (MODEL_WIDTH, 2 * STATE + MHEADS), MODEL_WIDTH ** -0.5, 0.0625, ((0, 8),))
    inner_taps = centred(key_list[3], (4, INNER), 4 ** -0.5, 3.0, ((1, 8),))
    state_taps = centred(key_list[4], (4, 2 * STATE), 4 ** -0.5, 3.0)
    inner_history = centred(part_keys[5], (TEN, 3, INNER), 1.0, 6.0, ((0, 2), (2, 8)))
    state_history = centred(part_keys[6], (TEN, 3, 2 * STATE), 1.0, 6.0, ((0, 2),), jnp.float32)
    step_size_bias = jnp.clip(-3.0 + 3.0 * jax.random.uniform(key_list[7], (MHEADS,), jnp.float32) ** block_levels(key_list[7], (MHEADS,), ((0, 8),), -0.2, 0.2), -3.0, 0.0)
    log_decay_rate = jnp.clip(jax.random.uniform(key_list[8], (MHEADS,), jnp.float32, -2.0, 2.0) * block_levels(key_list[8], (MHEADS,), ((0, 8),), -0.4, 0.0), -2.0, 2.0)
    skip_factor = jnp.clip(0.5 + 1.0 * jax.random.uniform(key_list[9], (MHEADS,), jnp.float32) ** block_levels(key_list[9], (MHEADS,), ((0, 8),), -0.2, 0.2), 0.5, 1.5)
    gated_norm_gain = jnp.clip(1.0 + 0.1 * jax.random.normal(key_list[10], (INNER,), jnp.float32), 0.5, 1.5)
    mamba_out_weight = centred(key_list[11], (INNER, MODEL_WIDTH), INNER ** -0.5, 0.0625, ((0, 8),))
    saved_state_pool = centred(part_keys[12], (SLOTS, MHEADS, HDIM, STATE), 1.0, 6.0, ((0, 2), (1, 8)), jnp.float32)
    tenant_state_slot = draw_tenant_state_slot(jax.random.fold_in(jax.random.fold_in(key_list[24], part), 71), part)
    attention_gain = jnp.clip(1.0 + 0.1 * jax.random.normal(key_list[14], (MODEL_WIDTH,), jnp.float32), 0.5, 1.5)
    query_matrix = draw_query_matrix(jax.random.fold_in(key_list[24], 71), part)
    adapter_down = centred(key_list[16], (ADAPTER_POOL, MODEL_WIDTH, ADAPTER_RANK), MODEL_WIDTH ** -0.5, 0.0625, ((1, 8),))
    adapter_up = centred(key_list[17], (ADAPTER_POOL, ADAPTER_RANK, QUERY_HEADS * HEAD_SIZE), ADAPTER_RANK ** -0.5, 0.75, ((2, 8),))
    tenant_adapter = draw_tenant_adapter(jax.random.fold_in(jax.random.fold_in(key_list[24], part), 71), part)
    key_value_weight = centred(key_list[19], (MODEL_WIDTH, 2 * KEY_HEADS * HEAD_SIZE), MODEL_WIDTH ** -0.5, 0.0625, ((0, 8),))
    key_value_pool = draw_key_value_pool(jax.random.fold_in(jax.random.fold_in(key_list[24], part), 71), part)
    tenant_blocks = draw_tenant_blocks(jax.random.fold_in(jax.random.fold_in(key_list[24], part), 71), part)
    cached_length = draw_cached_length(jax.random.fold_in(jax.random.fold_in(key_list[24], part), 71), part)
    attention_out_weight = centred(key_list[23], (QUERY_HEADS * HEAD_SIZE, MODEL_WIDTH), (QUERY_HEADS * HEAD_SIZE) ** -0.5, 0.0625, ((0, 8),))
    return {"tokens": tokens, "mamba_in_weight": mamba_in_weight, "state_projection": state_projection, "inner_taps": inner_taps, "state_taps": state_taps, "inner_history": inner_history, "state_history": state_history, "step_size_bias": step_size_bias, "log_decay_rate": log_decay_rate, "skip_factor": skip_factor, "gated_norm_gain": gated_norm_gain, "mamba_out_weight": mamba_out_weight, "saved_state_pool": saved_state_pool, "tenant_state_slot": tenant_state_slot, "attention_gain": attention_gain, "query_matrix": query_matrix, "adapter_down": adapter_down, "adapter_up": adapter_up, "tenant_adapter": tenant_adapter, "key_value_weight": key_value_weight, "key_value_pool": key_value_pool, "tenant_blocks": tenant_blocks, "cached_length": cached_length, "attention_out_weight": attention_out_weight}


epsilon = 1e-05
adapter_scale = 2.0
highest = lax.Precision.HIGHEST

def causal_conv(series, history, kernel):
    joined = jnp.concatenate([history.astype(jnp.float32), series.astype(jnp.float32)], axis=1)
    token_length = series.shape[1]
    summed_taps = kernel[0].astype(jnp.float32) * joined[:, 0:token_length]
    for offset in range(1, 4):
        summed_taps = summed_taps + kernel[offset].astype(jnp.float32) * joined[:, offset:offset + token_length]
    return jax.nn.silu(summed_taps)

def state_space(values, in_state, out_state, step_sizes, decay_rates, skip_terms, initial):
    log_decay = -step_sizes * decay_rates
    running = jnp.cumsum(log_decay, axis=1)
    token_length = values.shape[1]
    places = jnp.arange(token_length)
    lower_part = (places[:, None] >= places[None, :])[None, :, :, None]
    spread = running[:, :, None, :] - running[:, None, :, :]
    decays = jnp.where(lower_part, jnp.exp(jnp.where(lower_part, spread, 0.0)), 0.0)
    intersection = jnp.einsum('btn,bsn->bts', out_state, in_state, precision=highest)
    mixing = intersection[:, :, :, None] * decays * step_sizes[:, None, :, :]
    within = jnp.einsum('btsh,bshp->bthp', mixing, values, precision=highest)
    carried = jnp.einsum('btn,bhpn->bthp', out_state, initial, precision=highest) * jnp.exp(running)[:, :, :, None]
    result = within + carried + skip_terms[None, None, :, None] * values
    remain = jnp.exp(running[:, -1:, :] - running) * step_sizes
    final_state = jnp.exp(running[:, -1, :])[:, :, None, None] * initial + jnp.einsum('bsh,bshp,bsn->bhpn', remain, values, in_state, precision=highest)
    return (result, final_state)

def reference(tokens, mamba_in_weight, state_projection, inner_taps, state_taps, inner_history, state_history, step_size_bias, log_decay_rate, skip_factor, gated_norm_gain, mamba_out_weight, saved_state_pool, tenant_state_slot, attention_gain, query_matrix, adapter_down, adapter_up, tenant_adapter, key_value_weight, key_value_pool, tenant_blocks, cached_length, attention_out_weight):
    tenant_count, token_length, width = tokens.shape
    flat_tokens = tokens.reshape(tenant_count * token_length, width)
    inner = jnp.dot(flat_tokens, mamba_in_weight.reshape(width, 2 * INNER), preferred_element_type=jnp.float32)
    inner = inner.astype(jnp.bfloat16).reshape(tenant_count, token_length, 2, INNER)
    projected = jnp.dot(flat_tokens, state_projection, preferred_element_type=jnp.float32).reshape(tenant_count, token_length, -1)
    conv_values = causal_conv(inner[:, :, 0], inner_history, inner_taps).reshape(tenant_count, token_length, MHEADS, HDIM)
    conv_bc = causal_conv(projected[:, :, :2 * STATE], state_history, state_taps)
    step_sizes = jax.nn.softplus(projected[:, :, 2 * STATE:] + step_size_bias)
    initial = jnp.take(saved_state_pool, tenant_state_slot, axis=0)
    result, final_state = state_space(conv_values, conv_bc[:, :, :STATE], conv_bc[:, :, STATE:], step_sizes, jnp.exp(log_decay_rate), skip_factor, initial)
    gated = result.reshape(tenant_count, token_length, INNER) * jax.nn.silu(inner[:, :, 1].astype(jnp.float32))
    normed = (gated * lax.rsqrt(lax.optimization_barrier(jnp.mean(gated * gated, axis=-1, keepdims=True)) + epsilon) * gated_norm_gain).astype(jnp.bfloat16)
    mamba_out = jnp.dot(normed.reshape(-1, INNER), mamba_out_weight, preferred_element_type=jnp.float32)
    first = (flat_tokens.astype(jnp.float32) + mamba_out).astype(jnp.bfloat16)
    wide_first = lax.optimization_barrier(first).astype(jnp.float32)
    attn_in = (wide_first * lax.rsqrt(lax.optimization_barrier(jnp.mean(wide_first * wide_first, axis=-1, keepdims=True)) + epsilon) * attention_gain).astype(jnp.bfloat16)
    query_rows = jnp.dot(attn_in, query_matrix, preferred_element_type=jnp.float32).reshape(tenant_count, token_length, QUERY_HEADS * HEAD_SIZE)
    picked_down = jnp.take(adapter_down, tenant_adapter, axis=0)
    low_rank = jnp.einsum('bld,bdr->blr', attn_in.reshape(tenant_count, token_length, width).astype(jnp.float32), picked_down.astype(jnp.float32)).astype(jnp.bfloat16)
    picked_up = jnp.take(adapter_up, tenant_adapter, axis=0)
    raised_rows = jnp.einsum('blr,brc->blc', low_rank.astype(jnp.float32), picked_up.astype(jnp.float32))
    query_rows = (query_rows + adapter_scale * raised_rows).astype(jnp.bfloat16).reshape(tenant_count, token_length, KEY_HEADS, QUERY_HEADS // KEY_HEADS, HEAD_SIZE)
    fresh = jnp.dot(attn_in, key_value_weight, preferred_element_type=jnp.float32).astype(jnp.bfloat16).reshape(tenant_count, token_length, 2, KEY_HEADS, HEAD_SIZE)
    cached = jnp.take(key_value_pool, tenant_blocks, axis=0).reshape(tenant_count, -1, 2, KEY_HEADS, HEAD_SIZE)
    context = cached.shape[1]
    keys_all = jnp.concatenate([cached[:, :, 0], fresh[:, :, 0]], axis=1)
    values_all = jnp.concatenate([cached[:, :, 1], fresh[:, :, 1]], axis=1)

    def attend(packed):
        query_one, key_one, value_one, limit = packed
        scores = jnp.einsum('tkgd,jkd->kgtj', query_one.astype(jnp.float32), key_one.astype(jnp.float32)) * HEAD_SIZE ** (-0.5)
        places = jnp.arange(context + token_length)
        positions = jnp.arange(token_length)
        visible = jnp.where(places[None, :] < context, places[None, :] < limit, places[None, :] - context <= positions[:, None])
        masked = jnp.where(visible[None, None], scores, -jnp.inf)
        highest_score = lax.optimization_barrier(jnp.max(masked, axis=-1, keepdims=True))
        raised = jnp.where(visible[None, None], jnp.exp(masked - highest_score), 0.0)
        weights = (raised / lax.optimization_barrier(jnp.sum(raised, axis=-1, keepdims=True))).astype(jnp.bfloat16)
        return jnp.einsum('kgtj,jkd->tkgd', weights.astype(jnp.float32), value_one.astype(jnp.float32)).astype(jnp.bfloat16)
    heads_out = lax.map(attend, (query_rows, keys_all, values_all, cached_length))
    attn_out = jnp.dot(heads_out.reshape(-1, QUERY_HEADS * HEAD_SIZE), attention_out_weight, preferred_element_type=jnp.float32)
    second = (wide_first + attn_out).astype(jnp.bfloat16).reshape(tenant_count, token_length, width)
    return (second, final_state)
```

```python
import functools

import jax
import jax.numpy as jnp
from jax import lax
from jax.experimental import pallas as pl
from jax.experimental.pallas import tpu as pltpu
from jax.sharding import PartitionSpec as P

HDIM = 64
STATE = 256
QUERY_HEADS = 64
KEY_HEADS = 8
HEAD_SIZE = 128

epsilon = 1e-05
adapter_scale = 2.0
highest = lax.Precision.HIGHEST
f32 = jnp.float32
bf16 = jnp.bfloat16
VMEM_BYTES = 56 << 20


def ring_order(n):
    cols = 1
    for c in range(2, n):
        if n % c == 0 and (n // c) % 2 == 0 and c <= n // c:
            cols = c
    if cols == 1:
        return list(range(n))
    rows = n // cols
    order = [r * cols for r in range(rows)]
    for k, r in enumerate(reversed(range(rows))):
        across = list(range(1, cols))
        order += [r * cols + c for c in (across if k % 2 == 0 else across[::-1])]
    return order


class Ring:
    def __init__(self, n):
        self.n = n
        self.order = ring_order(n)
        place = {d: i for i, d in enumerate(self.order)}
        self.table = [[self.order[(place[d] + s) % n] for s in range(n)] for d in range(n)]
        self.cw = [(self.order[i], self.order[(i + 1) % n]) for i in range(n)]
        self.ccw = [(self.order[i], self.order[(i - 1) % n]) for i in range(n)]

    def near(self):
        me = lax.axis_index("tensor")
        return lax.dynamic_slice_in_dim(jnp.array(self.table, jnp.int32), me, 1, 0)[0]

    def right(self, x):
        return lax.ppermute(x, "tensor", self.cw)

    def left(self, x):
        return lax.ppermute(x, "tensor", self.ccw)

    def gather(self, x):
        n, half = self.n, self.n // 2
        h = x.shape[0] // 2
        stages = [[(0, x)]]
        a = b = x
        for s in range(1, half):
            a, b = self.right(a), self.left(b)
            stages.append([(n - s, a), (s, b)])
        last = jnp.concatenate([self.right(a[:h]), self.left(b[h:])], axis=0)
        stages.append([(half, last)])
        return stages

    def reduce(self, part):
        n, half = self.n, self.n // 2
        p = part(half).astype(bf16)
        h = p.shape[0] // 2
        a, b = self.right(p[:h]), self.left(p[h:])
        for d in range(half - 1, 0, -1):
            pa, pb = part(d), part(n - d)
            if d == half - 1:
                pa = jnp.concatenate([pa[:h] + a.astype(f32), pa[h:]], axis=0)
                pb = jnp.concatenate([pb[:h], pb[h:] + b.astype(f32)], axis=0)
            else:
                pa, pb = pa + a.astype(f32), pb + b.astype(f32)
            a, b = self.right(pa.astype(bf16)), self.left(pb.astype(bf16))
        own = part(0)
        if half == 1:
            return own + jnp.concatenate([a, b], axis=0).astype(f32)
        return own + a.astype(f32) + b.astype(f32)

    def masks(self):
        m, found = 1, []
        while m < self.n:
            found.append([(i, i ^ m) for i in range(self.n)])
            m *= 2
        return found

    def total(self, x):
        for pairs in self.masks():
            x = x + lax.ppermute(x, "tensor", pairs)
        return x

    def total_halves(self, x):
        pairs = self.masks()
        me = lax.axis_index("tensor")
        h = x.shape[0] // 2
        odd = (me % 2) == 1
        keep = jnp.where(odd, x[h:], x[:h])
        give = jnp.where(odd, x[:h], x[h:])
        keep = keep + lax.ppermute(give, "tensor", pairs[0])
        for p in pairs[1:]:
            keep = keep + lax.ppermute(keep, "tensor", p)
        other = lax.ppermute(keep, "tensor", pairs[0])
        return jnp.where(
            odd, jnp.concatenate([other, keep], axis=0), jnp.concatenate([keep, other], axis=0)
        )


def in_kernel(count, steps, first_call, which, *refs):
    blocks = refs[:count]
    w_ref = refs[count]
    o_ref = refs[-2]
    spread = refs[-1]
    j, k = pl.program_id(0), pl.program_id(1)
    kb = w_ref.shape[0]
    rows = blocks[0].shape[0]

    @pl.when((j == 0) & (k == 0))
    def _():
        if first_call:
            o_ref[...] = jnp.zeros_like(o_ref)
        else:
            o_ref[...] = refs[count + 1][...]

    lane = lax.broadcasted_iota(jnp.int32, (128, 512), 1)
    sub = lax.broadcasted_iota(jnp.int32, (128, 512), 0)
    target = jnp.where(lane < 256, 2 * sub, 2 * sub + 257)
    widen = jnp.where(lane == target, 1.0, 0.0).astype(bf16)

    for b in range(count):
        for s in range(steps):

            @pl.when((j == b) & (k == s))
            def _():
                for p in range(kb // 128):
                    piece = blocks[b][:, s * kb + p * 128 : s * kb + (p + 1) * 128]
                    both = jnp.dot(piece, widen, preferred_element_type=f32).astype(bf16)
                    spread[:rows, p * 256 : (p + 1) * 256] = both[:, :256]
                    spread[rows:, p * 256 : (p + 1) * 256] = both[:, 256:]

    w = w_ref[...].reshape(2 * kb, w_ref.shape[2])
    o_ref[...] += jnp.dot(spread[...], w, preferred_element_type=f32)


def in_product(ids, blocks, weight, acc):
    count = len(blocks)
    rows, depth = blocks[0].shape
    cols = weight.shape[2]
    kb = min(512, depth)
    steps = depth // kb
    in_specs = [pl.BlockSpec((rows, depth), lambda j, k, w: (0, 0)) for _ in blocks]
    in_specs.append(pl.BlockSpec((kb, 2, cols), lambda j, k, w: (w[j] * steps + k, 0, 0)))
    operands = [ids, *blocks, weight]
    aliases = {}
    if acc is not None:
        in_specs.append(pl.BlockSpec((2 * rows, cols), lambda j, k, w: (0, 0)))
        operands.append(acc)
        aliases = {len(operands) - 1: 0}
    return pl.pallas_call(
        functools.partial(in_kernel, count, steps, acc is None),
        grid_spec=pltpu.PrefetchScalarGridSpec(
            num_scalar_prefetch=1,
            grid=(count, steps),
            in_specs=in_specs,
            out_specs=pl.BlockSpec((2 * rows, cols), lambda j, k, w: (0, 0)),
            scratch_shapes=[pltpu.VMEM((2 * rows, 2 * kb), bf16)],
        ),
        out_shape=jax.ShapeDtypeStruct((2 * rows, cols), f32),
        input_output_aliases=aliases,
        compiler_params=pltpu.CompilerParams(vmem_limit_bytes=VMEM_BYTES),
        cost_estimate=pl.CostEstimate(
            flops=count * 8 * rows * depth * cols,
            bytes_accessed=count * depth * cols * 8,
            transcendentals=0,
        ),
        name="in_product",
    )(*operands)


def shifted(history, x, k):
    if k == 3:
        return x
    return jnp.concatenate([history[k:3], x[: x.shape[0] - 3 + k]], axis=0)


def conv_silu(history, x, taps):
    total = taps[0:1] * shifted(history, x, 0)
    for k in range(1, 4):
        total = total + taps[k : k + 1] * shifted(history, x, k)
    return total * jax.nn.sigmoid(total)


def spans(heads, width):
    lane = lax.broadcasted_iota(jnp.int32, (heads, heads * width), 1)
    row = lax.broadcasted_iota(jnp.int32, (heads, heads * width), 0)
    return jnp.where(lane // width == row, 1.0, 0.0).astype(f32)


def state_kernel(
    own_id,
    far_id,
    is_own,
    x_ref,
    z_ref,
    bc_ref,
    raw_ref,
    hx_ref,
    hbc_ref,
    tx_ref,
    tbc_ref,
    bias_ref,
    rate_ref,
    skip_ref,
    gain_ref,
    own_ref,
    far_ref,
    gated_ref,
    energy_ref,
    final_ref,
    initial,
):
    i = pl.program_id(0)

    @pl.when(is_own[i] == 1)
    def _():
        initial[...] = own_ref[0]

    @pl.when(is_own[i] == 0)
    def _():
        initial[...] = far_ref[0].astype(f32)

    length = x_ref.shape[0]
    heads = raw_ref.shape[1]
    values = conv_silu(hx_ref[0], x_ref[...].astype(bf16).astype(f32), tx_ref[...])
    bc = conv_silu(hbc_ref[0], bc_ref[...], tbc_ref[...])
    in_state = bc[:, :STATE].astype(bf16)
    out_state = bc[:, STATE:].astype(bf16)
    raw = raw_ref[...] + bias_ref[...]
    steps = jnp.maximum(raw, 0.0) + jnp.log1p(jnp.exp(-jnp.abs(raw)))
    log_decay = -steps * jnp.exp(rate_ref[...])
    row = lax.broadcasted_iota(jnp.int32, (length, length), 0)
    col = lax.broadcasted_iota(jnp.int32, (length, length), 1)
    lower = jnp.where(row >= col, 1.0, 0.0).astype(f32)
    running = jnp.dot(lower, log_decay, precision=highest, preferred_element_type=f32)
    last = running[length - 1 : length]

    wide = spans(heads, length)
    both = jnp.dot(
        jnp.concatenate([running, steps], axis=0), wide, precision=highest, preferred_element_type=f32
    )
    run_t, step_t = both[:length], both[length:]
    lane = lax.broadcasted_iota(jnp.int32, (length, heads * length), 1) % length
    place = lax.broadcasted_iota(jnp.int32, (length, heads * length), 0)
    diagonal = lane == place
    run_s = jnp.sum(jnp.where(diagonal, run_t, 0.0), axis=0, keepdims=True)
    step_s = jnp.sum(jnp.where(diagonal, step_t, 0.0), axis=0, keepdims=True)
    seen = place >= lane
    decays = jnp.where(seen, jnp.exp(jnp.where(seen, run_t - run_s, 0.0)), 0.0)
    overlap = lax.dot_general(
        out_state,
        jnp.concatenate([in_state] * heads, axis=0),
        (((1,), (1,)), ((), ())),
        preferred_element_type=f32,
    )
    mixing = (overlap * decays * step_s).astype(bf16)
    short = values.astype(bf16)
    group = min(4, heads)
    gl, gw = group * length, group * HDIM
    own_block = (
        lax.broadcasted_iota(jnp.int32, (gl, gw), 0) // length
        == lax.broadcasted_iota(jnp.int32, (gl, gw), 1) // HDIM
    )
    within = []
    for g in range(heads // group):
        v = jnp.concatenate([values[:, g * gw : (g + 1) * gw]] * group, axis=0)
        v = jnp.where(own_block, v, 0.0).astype(bf16)
        within.append(jnp.dot(mixing[:, g * gl : (g + 1) * gl], v, preferred_element_type=f32))
    within = within[0] if len(within) == 1 else jnp.concatenate(within, axis=1)

    narrow = spans(heads, HDIM)
    scales = jnp.dot(
        jnp.concatenate([jnp.exp(running), jnp.exp(last - running) * steps], axis=0),
        narrow,
        precision=highest,
        preferred_element_type=f32,
    )
    start = initial[...]
    carried = lax.dot_general(
        out_state, start.astype(bf16), (((1,), (1,)), ((), ())), preferred_element_type=f32
    )
    result = within + carried * scales[:length] + skip_ref[...] * values
    z = z_ref[...].astype(bf16).astype(f32)
    gated = result * (z * jax.nn.sigmoid(z))
    energy_ref[...] = jnp.sum(gated * gated, axis=1, keepdims=True)
    gated_ref[...] = (gated * gain_ref[...]).astype(bf16)

    kept = jnp.exp(
        lax.dot_general(
            log_decay,
            jnp.ones((length, STATE), f32),
            (((0,), (0,)), ((), ())),
            precision=highest,
            preferred_element_type=f32,
        )
    )
    update = lax.dot_general(
        (values * scales[length:]).astype(bf16),
        in_state,
        (((0,), (0,)), ((), ())),
        preferred_element_type=f32,
    )
    for h in range(heads):
        at = slice(h * HDIM, (h + 1) * HDIM)
        final_ref[0, at, :] = update[at] + start[at] * kept[h : h + 1]


def state_pass(
    inner, bc, raw, hx, hbc, tx, tbc, bias, rate, skip, gain, own_pool, far_pool, own_id, far_id, is_own
):
    tenants = own_id.shape[0]
    length = raw.shape[0] // tenants
    heads = raw.shape[1]
    cols = inner.shape[1]

    def rows(width):
        return pl.BlockSpec((length, width), lambda i, *s: (i, 0))

    def whole(a):
        return pl.BlockSpec(a.shape, lambda i, *s: (0,) * a.ndim)

    pooled = (1, cols, STATE)
    return pl.pallas_call(
        state_kernel,
        grid_spec=pltpu.PrefetchScalarGridSpec(
            num_scalar_prefetch=3,
            grid=(tenants,),
            in_specs=[
                rows(cols),
                pl.BlockSpec((length, cols), lambda i, *s: (tenants + i, 0)),
                rows(2 * STATE),
                rows(heads),
                pl.BlockSpec((1, 3, cols), lambda i, *s: (i, 0, 0)),
                pl.BlockSpec((1, 3, 2 * STATE), lambda i, *s: (i, 0, 0)),
                whole(tx),
                whole(tbc),
                whole(bias),
                whole(rate),
                whole(skip),
                whole(gain),
                pl.BlockSpec(pooled, lambda i, own, far, is_own: (own[i], 0, 0)),
                pl.BlockSpec(pooled, lambda i, own, far, is_own: (far[i], 0, 0)),
            ],
            out_specs=[
                rows(cols),
                rows(1),
                pl.BlockSpec(pooled, lambda i, *s: (i, 0, 0)),
            ],
            scratch_shapes=[pltpu.VMEM((cols, STATE), f32)],
        ),
        out_shape=[
            jax.ShapeDtypeStruct((tenants * length, cols), bf16),
            jax.ShapeDtypeStruct((tenants * length, 1), f32),
            jax.ShapeDtypeStruct((tenants, cols, STATE), f32),
        ],
        compiler_params=pltpu.CompilerParams(vmem_limit_bytes=VMEM_BYTES),
        cost_estimate=pl.CostEstimate(
            flops=tenants * 6 * length * cols * STATE,
            bytes_accessed=tenants * cols * STATE * 10,
            transcendentals=0,
        ),
        name="state_pass",
    )(
        own_id, far_id, is_own, inner, inner, bc, raw, hx, hbc, tx, tbc, bias, rate, skip, gain,
        own_pool, far_pool,
    )


def attend_kernel(
    table, limit, adapter, core, q_ref, low_ref, fresh_ref, norm_ref, up_ref, near_ref, far_ref, o_ref
):
    i = pl.program_id(0)
    length = q_ref.shape[0]
    heads = q_ref.shape[1] // HEAD_SIZE
    blocks = table.shape[1]
    part = near_ref.shape[1]
    norm = norm_ref[...]
    low = (low_ref[...] * norm).astype(bf16)
    raised = jnp.dot(low, up_ref[0], preferred_element_type=f32)
    q = (q_ref[...] * norm + adapter_scale * raised).astype(bf16)
    q = jnp.concatenate([q[:, h * HEAD_SIZE : (h + 1) * HEAD_SIZE] for h in range(heads)], axis=0)
    fresh = (fresh_ref[...] * norm).astype(bf16)
    pieces = []
    for j in range(blocks):
        at = table[i, j]
        pieces += [near_ref[at], far_ref[at]]
    cached = jnp.concatenate(pieces, axis=0)
    context = cached.shape[0]
    nt = (((1,), (1,)), ((), ()))
    scale = HEAD_SIZE ** (-0.5)
    old = lax.dot_general(q, cached[:, :HEAD_SIZE], nt, preferred_element_type=f32) * scale
    new = lax.dot_general(q, fresh[:, :HEAD_SIZE], nt, preferred_element_type=f32) * scale
    lane = lax.broadcasted_iota(jnp.int32, old.shape, 1)
    inside = lane % (2 * part)
    far_side = jnp.where(inside >= part, 1, 0)
    half = jnp.where(core[0] == 0, far_side, 1 - far_side)
    place = (lane // (2 * part)) * (2 * part) + half * part + inside % part
    old_seen = place < limit[i]
    token = lax.broadcasted_iota(jnp.int32, new.shape, 0) % length
    new_seen = lax.broadcasted_iota(jnp.int32, new.shape, 1) <= token
    old = jnp.where(old_seen, old, -jnp.inf)
    new = jnp.where(new_seen, new, -jnp.inf)
    top = jnp.maximum(jnp.max(old, axis=1, keepdims=True), jnp.max(new, axis=1, keepdims=True))
    old = jnp.where(old_seen, jnp.exp(old - top), 0.0)
    new = jnp.where(new_seen, jnp.exp(new - top), 0.0)
    share = 1.0 / (jnp.sum(old, axis=1, keepdims=True) + jnp.sum(new, axis=1, keepdims=True))
    out = jnp.dot((old * share).astype(bf16), cached[:, HEAD_SIZE:], preferred_element_type=f32)
    out += jnp.dot((new * share).astype(bf16), fresh[:, HEAD_SIZE:], preferred_element_type=f32)
    out = out.astype(bf16)
    for h in range(heads):
        o_ref[:, h * HEAD_SIZE : (h + 1) * HEAD_SIZE] = out[h * length : (h + 1) * length]


def attend(table, limit, adapter, core, q, low, fresh, norm, up, near, far):
    tenants = table.shape[0]
    length = q.shape[0] // tenants
    cols = q.shape[1]

    def rows(a):
        return pl.BlockSpec((length, a.shape[1]), lambda i, *s: (i, 0))

    def whole(a):
        return pl.BlockSpec(a.shape, lambda i, *s: (0,) * a.ndim)

    return pl.pallas_call(
        attend_kernel,
        grid_spec=pltpu.PrefetchScalarGridSpec(
            num_scalar_prefetch=4,
            grid=(tenants,),
            in_specs=[
                rows(q),
                rows(low),
                rows(fresh),
                rows(norm),
                pl.BlockSpec((1, *up.shape[1:]), lambda i, t, n, a, c: (a[i], 0, 0)),
                whole(near),
                whole(far),
            ],
            out_specs=rows(q),
        ),
        out_shape=jax.ShapeDtypeStruct(q.shape, bf16),
        compiler_params=pltpu.CompilerParams(vmem_limit_bytes=VMEM_BYTES),
        cost_estimate=pl.CostEstimate(
            flops=tenants * 4 * length * cols * 288,
            bytes_accessed=near.size * 4 + q.size * 6 + up.size,
            transcendentals=0,
        ),
        name="attend",
    )(table, limit, adapter, core, q, low, fresh, norm, up, near, far)


def per_device(
    ring,
    pools,
    tokens,
    mamba_in_weight,
    state_projection,
    inner_taps,
    state_taps,
    inner_history,
    state_history,
    step_size_bias,
    log_decay_rate,
    skip_factor,
    gated_norm_gain,
    mamba_out_weight,
    saved_state_pool,
    tenant_state_slot,
    attention_gain,
    query_matrix,
    adapter_down,
    adapter_up,
    tenant_adapter,
    key_value_weight,
    key_value_pool,
    tenant_blocks,
    cached_length,
    attention_out_weight,
):
    n = ring.n
    tenants, length, depth = tokens.shape
    me = lax.axis_index("tensor")
    core = lax.axis_index("pool")
    rows = tenants * length
    width = depth * n
    own_tokens = tokens.reshape(rows, depth)
    near = ring.near()
    heads = step_size_bias.shape[0]
    cols = mamba_in_weight.shape[2]

    stages = ring.gather(own_tokens)
    projected = ring.total_halves(
        jnp.dot(own_tokens, state_projection, preferred_element_type=f32)
    )
    inner = None
    for stage in stages:
        ids = jnp.stack([near[s] for s, _ in stage])
        inner = in_product(ids, [x for _, x in stage], mamba_in_weight, inner)

    slots = saved_state_pool.shape[0]
    flat_pool = saved_state_pool.reshape(slots, heads * HDIM, STATE)
    far_pool = lax.ppermute(
        flat_pool.astype(bf16), "pool", [(i, (i + 1) % pools) for i in range(pools)]
    )
    local_slot = tenant_state_slot - core * slots
    is_own = ((local_slot >= 0) & (local_slot < slots)).astype(jnp.int32)
    own_id = jnp.clip(local_slot, 0, slots - 1)
    far_id = jnp.clip(tenant_state_slot - (1 - core) * slots, 0, slots - 1)

    local_heads = query_matrix.shape[1] // HEAD_SIZE
    group_size = QUERY_HEADS // KEY_HEADS
    count, block_len, _ = key_value_pool.shape
    part = block_len // pools
    mine = lax.dynamic_slice_in_dim(key_value_pool, core * part, part, 1)
    mine = mine.reshape(count, part, 2, KEY_HEADS, HEAD_SIZE).transpose(3, 0, 1, 2, 4)
    mine = mine.reshape(KEY_HEADS, count, part, 2 * HEAD_SIZE)

    def for_device(d):
        return lax.dynamic_index_in_dim(mine, d * local_heads // group_size, 0, keepdims=False)

    if n <= 8:
        got = [for_device(me)]
        for s in range(1, n):
            got.append(
                lax.ppermute(
                    for_device((me + s) % n), "tensor", [(i, (i + s) % n) for i in range(n)]
                )
            )
        cache = jnp.concatenate(got, axis=0)
        owner = (me - tenant_blocks // count) % n
    else:
        every = jnp.stack([mine[d * local_heads // group_size] for d in range(n)])
        cache = lax.all_to_all(every, "tensor", 0, 0, tiled=True)
        cache = cache.reshape(n * count, part, 2 * HEAD_SIZE)
        owner = tenant_blocks // count
    table = owner * count + tenant_blocks % count
    far_cache = lax.ppermute(cache, "pool", [(i, (i + 1) % pools) for i in range(pools)])

    raw = lax.dynamic_slice_in_dim(projected, 2 * STATE + me * heads, heads, 1)
    gated, energy, final_state = state_pass(
        inner,
        projected,
        raw,
        inner_history.astype(f32),
        state_history,
        inner_taps.astype(f32),
        state_taps.astype(f32),
        step_size_bias[None],
        log_decay_rate[None],
        jnp.repeat(skip_factor, HDIM)[None],
        gated_norm_gain[None],
        flat_pool,
        far_pool,
        own_id,
        far_id,
        is_own,
    )
    energy = ring.total(energy)

    def out_part(left_side, weight):
        def part(s):
            block = lax.dynamic_slice_in_dim(weight, near[s] * depth, depth, 1)
            return jnp.dot(left_side, block, preferred_element_type=f32)

        return part

    mixed = ring.reduce(out_part(gated, mamba_out_weight))
    scale = lax.rsqrt(energy / (cols * n) + epsilon)
    first = (own_tokens.astype(f32) + mixed * scale).astype(bf16)
    wide_first = lax.optimization_barrier(first).astype(f32)
    gain = lax.dynamic_slice_in_dim(attention_gain, me * depth, depth, 0)
    attn_own = (wide_first * gain).astype(bf16)

    stages = ring.gather(attn_own)
    picked_down = jnp.take(adapter_down, tenant_adapter, axis=0)
    low = jnp.einsum(
        "bld,bdr->blr",
        attn_own.reshape(tenants, length, depth),
        picked_down,
        preferred_element_type=f32,
    ).reshape(rows, -1)
    rank = low.shape[1]
    square = jnp.sum(wide_first * wide_first, axis=-1, keepdims=True)
    sums = ring.total(jnp.concatenate([low, square], axis=1))
    kv = jnp.dot(attn_own, key_value_weight, preferred_element_type=f32)

    def kv_part(s):
        head = near[s] * local_heads // group_size
        key = lax.dynamic_slice_in_dim(kv, head * HEAD_SIZE, HEAD_SIZE, 1)
        value = lax.dynamic_slice_in_dim(kv, (KEY_HEADS + head) * HEAD_SIZE, HEAD_SIZE, 1)
        return jnp.concatenate([key, value], axis=1)

    fresh = ring.reduce(kv_part)
    query = None
    for stage in stages:
        for s, x in stage:
            block = lax.dynamic_slice_in_dim(query_matrix, near[s] * depth, depth, 0)
            term = jnp.dot(x, block, preferred_element_type=f32)
            query = term if query is None else query + term
    norm = lax.rsqrt(sums[:, rank:] / width + epsilon)
    heads_out = attend(
        table,
        cached_length,
        tenant_adapter,
        core[None].astype(jnp.int32),
        query,
        sums[:, :rank],
        fresh,
        norm,
        adapter_up,
        cache,
        far_cache,
    )
    out = ring.reduce(out_part(heads_out, attention_out_weight))
    second = (lax.optimization_barrier(first).astype(f32) + out).astype(bf16)
    return (
        second.reshape(tenants, length, depth),
        final_state.reshape(tenants, heads, HDIM, STATE),
    )


def solution(mesh):
    in_specs = (
        P(("groups", "pool"), None, "tensor"),
        P(None, None, "tensor"),
        P("tensor", None),
        P(None, "tensor"),
        P(),
        P(("groups", "pool"), None, "tensor"),
        P(("groups", "pool"), None, None),
        P("tensor"),
        P("tensor"),
        P("tensor"),
        P("tensor"),
        P("tensor", None),
        P(("groups", "pool"), "tensor", None, None),
        P(("groups", "pool")),
        P(),
        P(None, "tensor"),
        P(None, "tensor", None),
        P(None, None, "tensor"),
        P(("groups", "pool")),
        P("tensor", None),
        P(("groups", "tensor"), None, None),
        P(("groups", "pool"), None),
        P(("groups", "pool")),
        P("tensor", None),
    )
    out_specs = (P(("groups", "pool"), None, "tensor"), P(("groups", "pool"), "tensor", None, None))
    ring = Ring(mesh.shape["tensor"])
    return jax.shard_map(
        functools.partial(per_device, ring, mesh.shape["pool"]),
        mesh=mesh,
        in_specs=in_specs,
        out_specs=out_specs,
        check_vma=False,
    )
```

```python
import functools

import jax
import jax.numpy as jnp
from jax import lax
from jax.experimental import pallas as pl
from jax.experimental.pallas import tpu as pltpu
from jax.sharding import PartitionSpec as P

HDIM = 64
STATE = 256
QUERY_HEADS = 64
KEY_HEADS = 8
HEAD_SIZE = 128

epsilon = 1e-05
adapter_scale = 2.0
highest = lax.Precision.HIGHEST
f32 = jnp.float32
bf16 = jnp.bfloat16
VMEM_BYTES = 56 << 20


def ring_order(n):
    cols = 1
    for c in range(2, n):
        if n % c == 0 and (n // c) % 2 == 0 and c <= n // c:
            cols = c
    if cols == 1:
        return list(range(n))
    rows = n // cols
    order = [r * cols for r in range(rows)]
    for k, r in enumerate(reversed(range(rows))):
        across = list(range(1, cols))
        order += [r * cols + c for c in (across if k % 2 == 0 else across[::-1])]
    return order


class Ring:
    def __init__(self, n, pools):
        self.n = n
        self.half = n // 2
        self.pools = pools
        order = ring_order(n)
        place = {d: i for i, d in enumerate(order)}
        self.table = [
            [order[(place[d] + s) % n] for s in range(n)] + [d, c] for d in range(n) for c in range(pools)
        ]
        self.cw = [(order[i], order[(i + 1) % n]) for i in range(n)]
        self.ccw = [(order[i], order[(i - 1) % n]) for i in range(n)]

    def info(self):
        at = lax.axis_index("tensor") * self.pools + lax.axis_index("pool")
        return lax.dynamic_slice_in_dim(jnp.array(self.table, jnp.int32), at, 1, 0)[0]

    def right(self, x):
        return lax.ppermute(x, "tensor", self.cw)

    def left(self, x):
        return lax.ppermute(x, "tensor", self.ccw)

    def gather(self, x):
        n, half = self.n, self.half
        h = x.shape[0] // 2
        stages = [([0], [x])]
        a = b = x
        for s in range(1, half):
            a, b = self.right(a), self.left(b)
            stages.append(([n - s, s], [a, b]))
        stages.append(([half], [self.right(a[:h]), self.left(b[h:])]))
        return stages


def split(x):
    high = x.astype(bf16)
    return high, (x - high.astype(f32)).astype(bf16)


def in_kernel(offsets, count, first_call, info, *refs):
    blocks = refs[:count]
    w_ref = refs[count]
    o_ref, p_ref, spread = refs[-3:]
    j = pl.program_id(0)
    depth = w_ref.shape[0]
    rows = o_ref.shape[0] // 2

    @pl.when(j == 0)
    def _():
        if first_call:
            o_ref[...] = jnp.zeros_like(o_ref)
            p_ref[...] = jnp.zeros_like(p_ref)
        else:
            o_ref[...] = refs[count + 1][...]
            p_ref[...] = refs[count + 2][...]

    lane = lax.broadcasted_iota(jnp.int32, (128, 512), 1)
    sub = lax.broadcasted_iota(jnp.int32, (128, 512), 0)
    target = jnp.where(lane < 256, 2 * sub, 2 * sub + 257)
    widen = jnp.where(lane == target, 1.0, 0.0).astype(bf16)

    for b in range(len(offsets)):

        @pl.when(j == b)
        def _():
            base = 0
            for block in [blocks[b]] if count == len(offsets) else blocks:
                r = block.shape[0]
                for p in range(depth // 128):
                    piece = block[:, p * 128 : (p + 1) * 128]
                    both = jnp.dot(piece, widen, preferred_element_type=f32).astype(bf16)
                    spread[base : base + r, p * 256 : (p + 1) * 256] = both[:, :256]
                    spread[rows + base : rows + base + r, p * 256 : (p + 1) * 256] = both[:, 256:]
                p_ref[base : base + r] += block[:, depth:].astype(f32)
                base += r

    w = w_ref[...].reshape(2 * depth, w_ref.shape[2])
    o_ref[...] += jnp.dot(spread[...], w, preferred_element_type=f32)


def in_product(info, offsets, blocks, weight, depth, accs):
    count = len(blocks)
    rows = sum(b.shape[0] for b in blocks) // len(offsets)
    cols = weight.shape[2]
    extra = blocks[0].shape[1] - depth

    def row_block(j, info):
        at = info[offsets[0]]
        for b in range(1, len(offsets)):
            at = jnp.where(j == b, info[offsets[b]], at)
        return (at, 0, 0)

    def fixed(shape):
        return pl.BlockSpec(shape, lambda j, info: (0, 0))

    in_specs = [fixed(b.shape) for b in blocks]
    in_specs.append(pl.BlockSpec((depth, 2, cols), row_block))
    operands = [info, *blocks, weight]
    aliases = {}
    shapes = [(2 * rows, cols), (rows, extra)]
    if accs is not None:
        in_specs += [fixed(s) for s in shapes]
        aliases = {len(operands): 0, len(operands) + 1: 1}
        operands += accs
    return pl.pallas_call(
        functools.partial(in_kernel, offsets, count, accs is None),
        grid_spec=pltpu.PrefetchScalarGridSpec(
            num_scalar_prefetch=1,
            grid=(len(offsets),),
            in_specs=in_specs,
            out_specs=[fixed(s) for s in shapes],
            scratch_shapes=[pltpu.VMEM((2 * rows, 2 * depth), bf16)],
        ),
        out_shape=[jax.ShapeDtypeStruct(s, f32) for s in shapes],
        input_output_aliases=aliases,
        compiler_params=pltpu.CompilerParams(vmem_limit_bytes=VMEM_BYTES),
        cost_estimate=pl.CostEstimate(
            flops=len(offsets) * 8 * rows * depth * cols,
            bytes_accessed=len(offsets) * depth * cols * 8,
            transcendentals=0,
        ),
        name="in_product",
    )(*operands)


def lanes_of(columns, rows):
    lane = lax.broadcasted_iota(jnp.int32, (rows, 128), 1)
    out = jnp.zeros((rows, 128), f32)
    for at, value in columns:
        out = jnp.where(lane == at, value.astype(f32), out)
    return out.astype(bf16)


def energy_lanes(energy):
    high, low = split(energy)
    return lanes_of([(0, high), (1, low)], energy.shape[0])


def energy_of(lanes):
    wide = lanes.astype(f32)
    return wide[:, 0:1] + wide[:, 1:2]


def send_kernel(kind, dests, steps, with_energy, info, lhs_ref, w_ref, *refs):
    refs = list(refs)
    e_ref = refs.pop(0) if with_energy else None
    outs = refs[-2:]
    got = refs[:-2]
    j, c = pl.program_id(0), pl.program_id(1)
    ct = w_ref.shape[1]
    rows = lhs_ref.shape[0]
    h = rows // 2
    depth = steps * ct
    term = jnp.dot(lhs_ref[...], w_ref[...], preferred_element_type=f32)
    sides = [slice(0, h), slice(h, rows)]
    tail = slice(depth, depth + 128)

    for jj in range(dests):
        for cc in range(steps):

            @pl.when((j == jj) & (c == cc))
            def _():
                at = slice(cc * ct, (cc + 1) * ct)
                if kind == "first":
                    for out, side in zip(outs, sides):
                        out[:, at] = term[side].astype(bf16)
                elif kind == "second":
                    mine, other = sides[jj], sides[1 - jj]
                    outs[jj][mine, at] = (term[mine] + got[jj][:, at].astype(f32)).astype(bf16)
                    outs[jj][other, at] = term[other].astype(bf16)
                else:
                    outs[jj][:, at] = (term + got[jj][:, at].astype(f32)).astype(bf16)
                if with_energy and cc == 0:
                    e = e_ref[...]
                    if kind == "first":
                        for out, side in zip(outs, sides):
                            out[:, tail] = energy_lanes(e[side])
                    elif kind == "second":
                        came = e[mine] + energy_of(got[jj][:, tail])
                        outs[jj][mine, tail] = energy_lanes(came)
                        outs[jj][other, tail] = energy_lanes(e[other])
                    else:
                        outs[jj][:, tail] = energy_lanes(e + energy_of(got[jj][:, tail]))


def tile_of(depth):
    return min(512, depth)


def column_block(offsets, steps):
    def at(j, c, info, *more):
        device = info[offsets[0]]
        for b in range(1, len(offsets)):
            device = jnp.where(j == b, info[offsets[b]], device)
        return (0, device * steps + c)

    return at


def fixed_block(shape):
    return pl.BlockSpec(shape, lambda j, c, *s: (0,) * len(shape))


def send_step(info, kind, offsets, lhs, weight, depth, energy, got):
    rows = lhs.shape[0]
    ct = tile_of(depth)
    steps = depth // ct
    wide = depth + (0 if energy is None else 128)
    high = rows // 2 if kind == "first" else rows
    operands = [lhs, weight] + ([] if energy is None else [energy]) + got
    in_specs = [fixed_block(a.shape) for a in operands]
    in_specs[1] = pl.BlockSpec((weight.shape[0], ct), column_block(offsets, steps))
    return pl.pallas_call(
        functools.partial(send_kernel, kind, len(offsets), steps, energy is not None),
        grid_spec=pltpu.PrefetchScalarGridSpec(
            num_scalar_prefetch=1,
            grid=(len(offsets), steps),
            in_specs=in_specs,
            out_specs=[fixed_block((high, wide))] * 2,
        ),
        out_shape=[jax.ShapeDtypeStruct((high, wide), bf16)] * 2,
        compiler_params=pltpu.CompilerParams(vmem_limit_bytes=VMEM_BYTES),
        cost_estimate=pl.CostEstimate(
            flops=len(offsets) * 2 * rows * depth * weight.shape[0],
            bytes_accessed=len(offsets) * depth * weight.shape[0] * 2,
            transcendentals=0,
        ),
        name="send_step",
    )(info, *operands)


def ring_sum(ring, info, lhs, weight, depth, energy=None):
    n, half = ring.n, ring.half
    a, b = send_step(info, "first", [half], lhs, weight, depth, energy, [])
    a, b = ring.right(a), ring.left(b)
    for d in range(half - 1, 0, -1):
        kind = "second" if d == half - 1 else "later"
        a, b = send_step(info, kind, [d, n - d], lhs, weight, depth, energy, [a, b])
        a, b = ring.right(a), ring.left(b)
    return [a, b] if half > 1 else [jnp.concatenate([a, b], axis=0)]


def mixer_kernel(arrived, steps, tenants, inner_size, info, adapter, lhs_ref, w_ref, *refs):
    got = refs[:arrived]
    e_ref, tok_ref, gain_ref = refs[arrived : arrived + 3]
    downs = refs[arrived + 3 : arrived + 3 + tenants]
    first_ref, message_ref, square = refs[-3:]
    c = pl.program_id(1)
    ct = w_ref.shape[1]
    rows = lhs_ref.shape[0]
    depth = steps * ct
    length = rows // tenants
    tail = slice(depth, depth + 128)
    energy = e_ref[...]
    for g in got:
        energy = energy + energy_of(g[:, tail])
    scale = lax.rsqrt(energy / inner_size + epsilon)
    term = jnp.dot(lhs_ref[...], w_ref[...], preferred_element_type=f32)

    @pl.when(c == 0)
    def _():
        square[...] = jnp.zeros_like(square)

    for cc in range(steps):

        @pl.when(c == cc)
        def _():
            at = slice(cc * ct, (cc + 1) * ct)
            total = term
            for g in got:
                total = total + g[:, at].astype(f32)
            first = (tok_ref[:, at].astype(f32) + total * scale).astype(bf16)
            wide = first.astype(f32)
            square[...] += jnp.sum(wide * wide, axis=1, keepdims=True)
            first_ref[:, at] = first
            message_ref[:, at] = (wide * gain_ref[:, at]).astype(bf16)

    @pl.when(c == steps - 1)
    def _():
        high, low = split(square[...])
        rank = downs[0].shape[1]
        parts = []
        for i in range(tenants):
            x = message_ref[i * length : (i + 1) * length, :depth]
            parts.append(
                lax.dot_general(x, downs[i][0], (((1,), (1,)), ((), ())), preferred_element_type=f32)
            )
        small = jnp.concatenate(parts, axis=0).astype(bf16)
        message_ref[:, tail] = lanes_of([(rank, high), (rank + 1, low)], rows)
        message_ref[:, depth : depth + rank] = small


def mixer_step(info, adapter, lhs, weight, depth, energy, got, own_tokens, gain, down, inner_size):
    rows = lhs.shape[0]
    tenants = adapter.shape[0]
    ct = tile_of(depth)
    steps = depth // ct
    operands = [lhs, weight, *got, energy, own_tokens, gain] + [down] * tenants
    in_specs = [fixed_block(a.shape) for a in operands]
    in_specs[1] = pl.BlockSpec((weight.shape[0], ct), column_block([0], steps))
    in_specs[4 + len(got)] = pl.BlockSpec(
        (1, depth), lambda j, c, info, adapter: (0, info[info.shape[0] - 2])
    )
    for i in range(tenants):
        in_specs[5 + len(got) + i] = pl.BlockSpec(
            (1, *down.shape[1:]), functools.partial(lambda i, j, c, info, adapter: (adapter[i], 0, 0), i)
        )
    shapes = [(rows, depth), (rows, depth + 128)]
    return pl.pallas_call(
        functools.partial(mixer_kernel, len(got), steps, tenants, inner_size),
        grid_spec=pltpu.PrefetchScalarGridSpec(
            num_scalar_prefetch=2,
            grid=(1, steps),
            in_specs=in_specs,
            out_specs=[fixed_block(s) for s in shapes],
            scratch_shapes=[pltpu.VMEM((rows, 1), f32)],
        ),
        out_shape=[jax.ShapeDtypeStruct(s, bf16) for s in shapes],
        compiler_params=pltpu.CompilerParams(vmem_limit_bytes=VMEM_BYTES),
        cost_estimate=pl.CostEstimate(
            flops=2 * rows * depth * weight.shape[0],
            bytes_accessed=depth * weight.shape[0] * 2,
            transcendentals=0,
        ),
        name="mixer_step",
    )(info, adapter, *operands)


def final_kernel(arrived, info, lhs_ref, w_ref, *refs):
    total = jnp.dot(lhs_ref[...], w_ref[...], preferred_element_type=f32)
    for g in refs[:arrived]:
        total = total + g[...].astype(f32)
    refs[-1][...] = (refs[arrived][...].astype(f32) + total).astype(bf16)


def final_step(info, lhs, weight, depth, got, first):
    rows = lhs.shape[0]
    ct = tile_of(depth)
    steps = depth // ct
    operands = [lhs, weight, *got, first]
    tiles = pl.BlockSpec((rows, ct), lambda j, c, info: (0, c))
    return pl.pallas_call(
        functools.partial(final_kernel, len(got)),
        grid_spec=pltpu.PrefetchScalarGridSpec(
            num_scalar_prefetch=1,
            grid=(1, steps),
            in_specs=[
                fixed_block(lhs.shape),
                pl.BlockSpec((weight.shape[0], ct), column_block([0], steps)),
            ]
            + [tiles] * (len(got) + 1),
            out_specs=tiles,
        ),
        out_shape=jax.ShapeDtypeStruct((rows, depth), bf16),
        compiler_params=pltpu.CompilerParams(vmem_limit_bytes=VMEM_BYTES),
        name="final_step",
    )(info, *operands)


def query_kernel(offsets, count, first_call, info, *refs):
    blocks = refs[:count]
    w_ref = refs[count]
    q_ref, l_ref = refs[-2:]
    j, k = pl.program_id(0), pl.program_id(1)
    kb = w_ref.shape[0]
    steps = pl.num_programs(1)
    depth = blocks[0].shape[1] - 128

    @pl.when((j == 0) & (k == 0))
    def _():
        if first_call:
            q_ref[...] = jnp.zeros_like(q_ref)
            l_ref[...] = jnp.zeros_like(l_ref)
        else:
            q_ref[...] = refs[count + 1][...]
            l_ref[...] = refs[count + 2][...]

    for b in range(len(offsets)):
        for kk in range(depth // kb):

            @pl.when((j == b) & (k == kk))
            def _():
                pieces = [blocks[b]] if count == len(offsets) else blocks
                base = 0
                for block in pieces:
                    at = slice(base, base + block.shape[0])
                    q_ref[at] += jnp.dot(
                        block[:, kk * kb : (kk + 1) * kb], w_ref[...], preferred_element_type=f32
                    )
                    if kk == 0:
                        l_ref[at] += block[:, depth:].astype(f32)
                    base += block.shape[0]


def query_step(info, offsets, blocks, weight, depth, accs):
    count = len(blocks)
    rows = sum(b.shape[0] for b in blocks) // len(offsets)
    cols = weight.shape[1]
    kb = tile_of(depth)
    steps = depth // kb

    def row_block(j, k, info):
        at = info[offsets[0]]
        for b in range(1, len(offsets)):
            at = jnp.where(j == b, info[offsets[b]], at)
        return (at * steps + k, 0)

    shapes = [(rows, cols), (rows, 128)]
    in_specs = [fixed_block(b.shape) for b in blocks] + [pl.BlockSpec((kb, cols), row_block)]
    operands = [info, *blocks, weight]
    aliases = {}
    if accs is not None:
        in_specs += [fixed_block(s) for s in shapes]
        aliases = {len(operands): 0, len(operands) + 1: 1}
        operands += accs
    return pl.pallas_call(
        functools.partial(query_kernel, offsets, count, accs is None),
        grid_spec=pltpu.PrefetchScalarGridSpec(
            num_scalar_prefetch=1,
            grid=(len(offsets), steps),
            in_specs=in_specs,
            out_specs=[fixed_block(s) for s in shapes],
        ),
        out_shape=[jax.ShapeDtypeStruct(s, f32) for s in shapes],
        input_output_aliases=aliases,
        compiler_params=pltpu.CompilerParams(vmem_limit_bytes=VMEM_BYTES),
        cost_estimate=pl.CostEstimate(
            flops=len(offsets) * 2 * rows * depth * cols,
            bytes_accessed=len(offsets) * depth * cols * 2,
            transcendentals=0,
        ),
        name="query_step",
    )(*operands)


def shifted(history, x, k):
    if k == 3:
        return x
    return jnp.concatenate([history[k:3], x[: x.shape[0] - 3 + k]], axis=0)


def conv_silu(history, x, taps):
    total = taps[0:1] * shifted(history, x, 0)
    for k in range(1, 4):
        total = total + taps[k : k + 1] * shifted(history, x, k)
    return total * jax.nn.sigmoid(total)


def spans(heads, width):
    lane = lax.broadcasted_iota(jnp.int32, (heads, heads * width), 1)
    row = lax.broadcasted_iota(jnp.int32, (heads, heads * width), 0)
    return jnp.where(lane // width == row, 1.0, 0.0).astype(f32)


def state_kernel(
    slot,
    info,
    x_ref,
    z_ref,
    bc_ref,
    hx_ref,
    hbc_ref,
    tx_ref,
    tbc_ref,
    bias_ref,
    rate_ref,
    skip_ref,
    gain_ref,
    own_ref,
    far_ref,
    gated_ref,
    energy_ref,
    final_ref,
    initial,
    *,
    slots,
):
    i = pl.program_id(0)
    count = info.shape[0]
    is_own = slot[i] // slots == info[count - 1]

    @pl.when(is_own)
    def _():
        initial[...] = own_ref[0]

    @pl.when(jnp.logical_not(is_own))
    def _():
        initial[...] = far_ref[0].astype(f32)

    length = x_ref.shape[0]
    heads = bias_ref.shape[1]
    values = conv_silu(hx_ref[0], x_ref[...].astype(bf16).astype(f32), tx_ref[...])
    bc = conv_silu(hbc_ref[0], bc_ref[:, : 2 * STATE], tbc_ref[...])
    all_raw = bc_ref[:, 2 * STATE :]
    pick = (all_raw.shape[1], heads)
    chosen = lax.broadcasted_iota(jnp.int32, pick, 0) == (
        lax.broadcasted_iota(jnp.int32, pick, 1) + info[count - 2] * heads
    )
    chosen = jnp.where(chosen, 1.0, 0.0).astype(f32)
    in_state = bc[:, :STATE].astype(bf16)
    out_state = bc[:, STATE:].astype(bf16)
    raw = jnp.dot(all_raw, chosen, precision=highest, preferred_element_type=f32) + bias_ref[...]
    steps = jnp.maximum(raw, 0.0) + jnp.log1p(jnp.exp(-jnp.abs(raw)))
    log_decay = -steps * jnp.exp(rate_ref[...])
    row = lax.broadcasted_iota(jnp.int32, (length, length), 0)
    col = lax.broadcasted_iota(jnp.int32, (length, length), 1)
    lower = jnp.where(row >= col, 1.0, 0.0).astype(f32)
    running = jnp.dot(lower, log_decay, precision=highest, preferred_element_type=f32)
    last = running[length - 1 : length]

    wide = spans(heads, length)
    both = jnp.dot(
        jnp.concatenate([running, steps], axis=0), wide, precision=highest, preferred_element_type=f32
    )
    run_t, step_t = both[:length], both[length:]
    lane = lax.broadcasted_iota(jnp.int32, (length, heads * length), 1) % length
    place = lax.broadcasted_iota(jnp.int32, (length, heads * length), 0)
    diagonal = lane == place
    run_s = jnp.sum(jnp.where(diagonal, run_t, 0.0), axis=0, keepdims=True)
    step_s = jnp.sum(jnp.where(diagonal, step_t, 0.0), axis=0, keepdims=True)
    seen = place >= lane
    decays = jnp.where(seen, jnp.exp(jnp.where(seen, run_t - run_s, 0.0)), 0.0)
    overlap = lax.dot_general(
        out_state,
        jnp.concatenate([in_state] * heads, axis=0),
        (((1,), (1,)), ((), ())),
        preferred_element_type=f32,
    )
    mixing = (overlap * decays * step_s).astype(bf16)
    short = values.astype(bf16)
    group = min(4, heads)
    gl, gw = group * length, group * HDIM
    own_block = (
        lax.broadcasted_iota(jnp.int32, (gl, gw), 0) // length
        == lax.broadcasted_iota(jnp.int32, (gl, gw), 1) // HDIM
    )
    within = []
    for g in range(heads // group):
        v = jnp.concatenate([values[:, g * gw : (g + 1) * gw]] * group, axis=0)
        v = jnp.where(own_block, v, 0.0).astype(bf16)
        within.append(jnp.dot(mixing[:, g * gl : (g + 1) * gl], v, preferred_element_type=f32))
    within = within[0] if len(within) == 1 else jnp.concatenate(within, axis=1)

    narrow = spans(heads, HDIM)
    scales = jnp.dot(
        jnp.concatenate(
            [
                jnp.exp(running),
                jnp.exp(last - running) * steps,
                jnp.broadcast_to(skip_ref[...], (8, heads)),
            ],
            axis=0,
        ),
        narrow,
        precision=highest,
        preferred_element_type=f32,
    )
    start = initial[...]
    carried = lax.dot_general(
        out_state, start.astype(bf16), (((1,), (1,)), ((), ())), preferred_element_type=f32
    )
    result = within + carried * scales[:length] + scales[2 * length : 2 * length + 1] * values
    z = z_ref[...].astype(bf16).astype(f32)
    gated = result * (z * jax.nn.sigmoid(z))
    energy_ref[...] = jnp.sum(gated * gated, axis=1, keepdims=True)
    gated_ref[...] = (gated * gain_ref[...]).astype(bf16)

    kept = jnp.exp(
        lax.dot_general(
            log_decay,
            jnp.ones((length, STATE), f32),
            (((0,), (0,)), ((), ())),
            precision=highest,
            preferred_element_type=f32,
        )
    )
    update = lax.dot_general(
        (values * scales[length : 2 * length]).astype(bf16),
        in_state,
        (((0,), (0,)), ((), ())),
        preferred_element_type=f32,
    )
    for h in range(heads):
        at = slice(h * HDIM, (h + 1) * HDIM)
        final_ref[0, at, :] = update[at] + start[at] * kept[h : h + 1]


def state_pass(
    info, slot, inner, projected, hx, hbc, tx, tbc, bias, rate, skip, gain, own_pool, far_pool
):
    tenants = slot.shape[0]
    length = projected.shape[0] // tenants
    cols = inner.shape[1]
    slots = own_pool.shape[0]

    def rows(width):
        return pl.BlockSpec((length, width), lambda i, *s: (i, 0))

    def whole(a):
        return pl.BlockSpec(a.shape, lambda i, *s: (0,) * a.ndim)

    def own_slot(i, slot, info):
        return (jnp.clip(slot[i] - info[info.shape[0] - 1] * slots, 0, slots - 1), 0, 0)

    def far_slot(i, slot, info):
        return (jnp.clip(slot[i] - (1 - info[info.shape[0] - 1]) * slots, 0, slots - 1), 0, 0)

    pooled = (1, cols, STATE)
    return pl.pallas_call(
        functools.partial(state_kernel, slots=slots),
        grid_spec=pltpu.PrefetchScalarGridSpec(
            num_scalar_prefetch=2,
            grid=(tenants,),
            in_specs=[
                rows(cols),
                pl.BlockSpec((length, cols), lambda i, *s: (tenants + i, 0)),
                rows(projected.shape[1]),
                pl.BlockSpec((1, 3, cols), lambda i, *s: (i, 0, 0)),
                pl.BlockSpec((1, 3, 2 * STATE), lambda i, *s: (i, 0, 0)),
                whole(tx),
                whole(tbc),
                whole(bias),
                whole(rate),
                whole(skip),
                whole(gain),
                pl.BlockSpec(pooled, own_slot),
                pl.BlockSpec(pooled, far_slot),
            ],
            out_specs=[
                rows(cols),
                rows(1),
                pl.BlockSpec(pooled, lambda i, *s: (i, 0, 0)),
            ],
            scratch_shapes=[pltpu.VMEM((cols, STATE), f32)],
        ),
        out_shape=[
            jax.ShapeDtypeStruct((tenants * length, cols), bf16),
            jax.ShapeDtypeStruct((tenants * length, 1), f32),
            jax.ShapeDtypeStruct((tenants, cols, STATE), f32),
        ],
        compiler_params=pltpu.CompilerParams(vmem_limit_bytes=VMEM_BYTES),
        cost_estimate=pl.CostEstimate(
            flops=tenants * 6 * length * cols * STATE,
            bytes_accessed=tenants * cols * STATE * 10,
            transcendentals=0,
        ),
        name="state_pass",
    )(slot, info, inner, inner, projected, hx, hbc, tx, tbc, bias, rate, skip, gain, own_pool, far_pool)


def attend_kernel(
    size, width, table, limit, adapter, info, q_ref, low_ref, up_ref, near_ref, far_ref, *refs
):
    o_ref = refs[-1]
    i = pl.program_id(0)
    length = q_ref.shape[0]
    heads = q_ref.shape[1] // HEAD_SIZE
    blocks = table.shape[1]
    part = near_ref.shape[1]
    me, core = info[info.shape[0] - 2], info[info.shape[0] - 1]
    count = near_ref.shape[0] // size
    rank = up_ref.shape[1]
    square = low_ref[:, rank : rank + 1] + low_ref[:, rank + 1 : rank + 2]
    norm = lax.rsqrt(square / width + epsilon)
    low = (low_ref[:, :rank] * norm).astype(bf16)
    raised = jnp.dot(low, up_ref[0], preferred_element_type=f32)
    q = (q_ref[...] * norm + adapter_scale * raised).astype(bf16)
    q = jnp.concatenate([q[:, h * HEAD_SIZE : (h + 1) * HEAD_SIZE] for h in range(heads)], axis=0)
    fresh = jnp.concatenate([refs[0][...], refs[1][...]], axis=1)
    for came in refs[2:-1]:
        fresh = fresh + came[...].astype(f32)
    fresh = (fresh * norm).astype(bf16)
    pieces = []
    for j in range(blocks):
        owner = table[i, j] // count
        if size <= 8:
            owner = lax.rem(me - owner + size, size)
        at = owner * count + lax.rem(table[i, j], count)
        pieces += [near_ref[at], far_ref[at]]
    cached = jnp.concatenate(pieces, axis=0)
    context = cached.shape[0]
    nt = (((1,), (1,)), ((), ()))
    scale = HEAD_SIZE ** (-0.5)
    old = lax.dot_general(q, cached[:, :HEAD_SIZE], nt, preferred_element_type=f32) * scale
    new = lax.dot_general(q, fresh[:, :HEAD_SIZE], nt, preferred_element_type=f32) * scale
    lane = lax.broadcasted_iota(jnp.int32, old.shape, 1)
    inside = lane % (2 * part)
    far_side = jnp.where(inside >= part, 1, 0)
    half = jnp.where(core == 0, far_side, 1 - far_side)
    place = (lane // (2 * part)) * (2 * part) + half * part + inside % part
    old_seen = place < limit[i]
    token = lax.broadcasted_iota(jnp.int32, new.shape, 0) % length
    new_seen = lax.broadcasted_iota(jnp.int32, new.shape, 1) <= token
    old = jnp.where(old_seen, old, -jnp.inf)
    new = jnp.where(new_seen, new, -jnp.inf)
    top = jnp.maximum(jnp.max(old, axis=1, keepdims=True), jnp.max(new, axis=1, keepdims=True))
    old = jnp.where(old_seen, jnp.exp(old - top), 0.0)
    new = jnp.where(new_seen, jnp.exp(new - top), 0.0)
    share = 1.0 / (jnp.sum(old, axis=1, keepdims=True) + jnp.sum(new, axis=1, keepdims=True))
    out = jnp.dot((old * share).astype(bf16), cached[:, HEAD_SIZE:], preferred_element_type=f32)
    out += jnp.dot((new * share).astype(bf16), fresh[:, HEAD_SIZE:], preferred_element_type=f32)
    out = out.astype(bf16)
    for h in range(heads):
        o_ref[:, h * HEAD_SIZE : (h + 1) * HEAD_SIZE] = out[h * length : (h + 1) * length]


def attend(ring, width, table, limit, adapter, info, q, low, up, near, far, kv, kv_came, head_of):
    tenants = table.shape[0]
    length = q.shape[0] // tenants

    def rows(a):
        return pl.BlockSpec((length, a.shape[1]), lambda i, *s: (i, 0))

    def whole(a):
        return pl.BlockSpec(a.shape, lambda i, *s: (0,) * a.ndim)

    def own(base):
        return pl.BlockSpec(
            (length, HEAD_SIZE), lambda i, t, n, a, info: (i, base + head_of(info[info.shape[0] - 2]))
        )

    return pl.pallas_call(
        functools.partial(attend_kernel, ring.n, width),
        grid_spec=pltpu.PrefetchScalarGridSpec(
            num_scalar_prefetch=4,
            grid=(tenants,),
            in_specs=[
                rows(q),
                rows(low),
                pl.BlockSpec((1, *up.shape[1:]), lambda i, t, n, a, info: (a[i], 0, 0)),
                whole(near),
                whole(far),
                own(0),
                own(KEY_HEADS),
            ]
            + [rows(a) for a in kv_came],
            out_specs=rows(q),
        ),
        out_shape=jax.ShapeDtypeStruct(q.shape, bf16),
        compiler_params=pltpu.CompilerParams(vmem_limit_bytes=VMEM_BYTES),
        cost_estimate=pl.CostEstimate(
            flops=tenants * 4 * length * q.shape[1] * 288,
            bytes_accessed=near.size * 4 + q.size * 6 + up.size,
            transcendentals=0,
        ),
        name="attend",
    )(table, limit, adapter, info, q, low, up, near, far, kv, kv, *kv_came)


def per_device(
    ring,
    tokens,
    mamba_in_weight,
    state_projection,
    inner_taps,
    state_taps,
    inner_history,
    state_history,
    step_size_bias,
    log_decay_rate,
    skip_factor,
    gated_norm_gain,
    mamba_out_weight,
    saved_state_pool,
    tenant_state_slot,
    attention_gain,
    query_matrix,
    adapter_down,
    adapter_up,
    tenant_adapter,
    key_value_weight,
    key_value_pool,
    tenant_blocks,
    cached_length,
    attention_out_weight,
):
    n, half, pools = ring.n, ring.half, ring.pools
    tenants, length, depth = tokens.shape
    rows = tenants * length
    width = depth * n
    info = ring.info()
    me, core = info[n], info[n + 1]
    own_tokens = tokens.reshape(rows, depth)
    heads = step_size_bias.shape[0]
    cols = mamba_in_weight.shape[2]
    swap = [(i, (i + 1) % pools) for i in range(pools)]

    partial = jnp.dot(own_tokens, state_projection, preferred_element_type=f32)
    stages = ring.gather(jnp.concatenate([own_tokens, partial.astype(bf16)], axis=1))
    accs = None
    for offsets, blocks in stages:
        accs = in_product(info, offsets, blocks, mamba_in_weight, depth, accs)
    inner, projected = accs

    slots = saved_state_pool.shape[0]
    flat_pool = saved_state_pool.reshape(slots, heads * HDIM, STATE)
    far_pool = lax.ppermute(flat_pool.astype(bf16), "pool", swap)

    local_heads = query_matrix.shape[1] // HEAD_SIZE
    group_size = QUERY_HEADS // KEY_HEADS

    def head_of(device):
        return device * local_heads // group_size

    count, block_len, _ = key_value_pool.shape
    part = block_len // pools
    mine = lax.dynamic_slice_in_dim(key_value_pool, core * part, part, 1)
    mine = mine.reshape(count, part, 2, KEY_HEADS, HEAD_SIZE).transpose(3, 0, 1, 2, 4)
    mine = mine.reshape(KEY_HEADS, count, part, 2 * HEAD_SIZE)
    mine, _ = lax.optimization_barrier((mine, stages[-1][1]))

    if n <= 8:
        got = []
        for s in range(n):
            block = lax.dynamic_index_in_dim(mine, head_of((me + s) % n), 0, keepdims=False)
            if s > 0:
                block = lax.ppermute(block, "tensor", [(i, (i + s) % n) for i in range(n)])
            got.append(block)
        cache = jnp.concatenate(got, axis=0)
    else:
        every = jnp.stack([mine[head_of(d)] for d in range(n)])
        cache = lax.all_to_all(every, "tensor", 0, 0, tiled=True)
        cache = cache.reshape(n * count, part, 2 * HEAD_SIZE)
    far_cache = lax.ppermute(cache, "pool", swap)

    gated, energy, final_state = state_pass(
        info,
        tenant_state_slot,
        inner,
        projected,
        inner_history.astype(f32),
        state_history,
        inner_taps.astype(f32),
        state_taps.astype(f32),
        step_size_bias[None],
        log_decay_rate[None],
        skip_factor[None],
        gated_norm_gain[None],
        flat_pool,
        far_pool,
    )
    got = ring_sum(ring, info, gated, mamba_out_weight, depth, energy)
    first, message = mixer_step(
        info,
        tenant_adapter,
        gated,
        mamba_out_weight,
        depth,
        energy,
        got,
        own_tokens,
        attention_gain[None],
        adapter_down.transpose(0, 2, 1),
        cols * n,
    )

    kv = jnp.dot(message[:, :depth], key_value_weight, preferred_element_type=f32)

    def kv_part(s):
        head = head_of(info[s])
        key = lax.dynamic_slice_in_dim(kv, head * HEAD_SIZE, HEAD_SIZE, 1)
        value = lax.dynamic_slice_in_dim(kv, (KEY_HEADS + head) * HEAD_SIZE, HEAD_SIZE, 1)
        return jnp.concatenate([key, value], axis=1)

    h = rows // 2
    stages = [([0], [message])]
    a, b = message, message
    ka, kb = kv_part(half)[:h].astype(bf16), kv_part(half)[h:].astype(bf16)
    for s in range(1, half):
        a, b, ka, kb = ring.right(a), ring.left(b), ring.right(ka), ring.left(kb)
        a, b, ka, kb = lax.optimization_barrier((a, b, ka, kb))
        stages.append(([n - s, s], [a, b]))
        pa, pb = kv_part(half - s), kv_part(n - half + s)
        if s == 1:
            pa = jnp.concatenate([pa[:h] + ka.astype(f32), pa[h:]], axis=0)
            pb = jnp.concatenate([pb[:h], pb[h:] + kb.astype(f32)], axis=0)
        else:
            pa, pb = pa + ka.astype(f32), pb + kb.astype(f32)
        ka, kb = pa.astype(bf16), pb.astype(bf16)
    stages.append(([half], [ring.right(a[:h]), ring.left(b[h:])]))
    ka, kb = ring.right(ka), ring.left(kb)
    kv_came = [ka, kb] if half > 1 else [jnp.concatenate([ka, kb], axis=0)]
    accs = None
    for offsets, blocks in stages:
        accs = query_step(info, offsets, blocks, query_matrix, depth, accs)
    query, low = accs
    heads_out = attend(
        ring,
        width,
        tenant_blocks,
        cached_length,
        tenant_adapter,
        info,
        query,
        low,
        adapter_up,
        cache,
        far_cache,
        kv,
        kv_came,
        head_of,
    )
    got = ring_sum(ring, info, heads_out, attention_out_weight, depth)
    second = final_step(info, heads_out, attention_out_weight, depth, got, first)
    return (
        second.reshape(tenants, length, depth),
        final_state.reshape(tenants, heads, HDIM, STATE),
    )


def solution(mesh):
    in_specs = (
        P(("groups", "pool"), None, "tensor"),
        P(None, None, "tensor"),
        P("tensor", None),
        P(None, "tensor"),
        P(),
        P(("groups", "pool"), None, "tensor"),
        P(("groups", "pool"), None, None),
        P("tensor"),
        P("tensor"),
        P("tensor"),
        P("tensor"),
        P("tensor", None),
        P(("groups", "pool"), "tensor", None, None),
        P(("groups", "pool")),
        P(),
        P(None, "tensor"),
        P(None, "tensor", None),
        P(None, None, "tensor"),
        P(("groups", "pool")),
        P("tensor", None),
        P(("groups", "tensor"), None, None),
        P(("groups", "pool"), None),
        P(("groups", "pool")),
        P("tensor", None),
    )
    out_specs = (P(("groups", "pool"), None, "tensor"), P(("groups", "pool"), "tensor", None, None))
    ring = Ring(mesh.shape["tensor"], mesh.shape["pool"])
    return jax.shard_map(
        functools.partial(per_device, ring),
        mesh=mesh,
        in_specs=in_specs,
        out_specs=out_specs,
        check_vma=False,
    )
```

```python
import functools

import jax
import jax.numpy as jnp
from jax import lax
from jax.experimental import pallas as pl
from jax.experimental.pallas import tpu as pltpu
from jax.sharding import PartitionSpec as P

HDIM = 64
STATE = 256
QUERY_HEADS = 64
KEY_HEADS = 8
HEAD_SIZE = 128

epsilon = 1e-05
adapter_scale = 2.0
highest = lax.Precision.HIGHEST
f32 = jnp.float32
bf16 = jnp.bfloat16


def ring_order(n):
    cols = 1
    for c in range(2, n):
        if n % c == 0 and (n // c) % 2 == 0 and c <= n // c:
            cols = c
    if cols == 1:
        return list(range(n))
    rows = n // cols
    order = [r * cols for r in range(rows)]
    for k, r in enumerate(reversed(range(rows))):
        across = list(range(1, cols))
        order += [r * cols + c for c in (across if k % 2 == 0 else across[::-1])]
    return order


class Ring:
    def __init__(self, n, pools):
        self.n = n
        heads = [d * QUERY_HEADS // n // (QUERY_HEADS // KEY_HEADS) for d in range(n)]
        self.half = n // 2
        self.pools = pools
        order = ring_order(n)
        place = {d: i for i, d in enumerate(order)}
        self.table = [
            [order[(place[d] + s) % n] for s in range(n)]
            + [heads[order[(place[d] + s) % n]] for s in range(n)]
            + [d, c]
            for d in range(n)
            for c in range(pools)
        ]
        self.cw = [(order[i], order[(i + 1) % n]) for i in range(n)]
        self.ccw = [(order[i], order[(i - 1) % n]) for i in range(n)]

    def info(self):
        at = lax.axis_index("tensor") * self.pools + lax.axis_index("pool")
        return lax.dynamic_slice_in_dim(jnp.array(self.table, jnp.int32), at, 1, 0)[0]

    def right(self, x):
        return lax.ppermute(x, "tensor", self.cw)

    def left(self, x):
        return lax.ppermute(x, "tensor", self.ccw)

    def masks(self):
        found, m = [], 1
        while m < self.n:
            found.append([(i, i ^ m) for i in range(self.n)])
            m *= 2
        return found

    def gather(self, x, weigh, keep, give):
        n, half = self.n, self.half
        h = x.shape[0] // 2
        pairs = self.masks()
        exchange = pairs + pairs[:1]
        sums, ready = None, ([0], [x])
        a = b = x
        for s in range(1, max(half, len(exchange)) + 1):
            if s == half:
                a, b = a[:h], b[h:]
            if s <= half:
                a, b = self.right(a), self.left(b)
            if s <= len(exchange):
                came = lax.ppermute(give, "tensor", exchange[s - 1])
            if s <= half:
                sums = weigh(*ready, sums)
            if s <= len(exchange):
                a, b, sums, came = lax.optimization_barrier((a, b, sums, came))
            else:
                a, b, sums = lax.optimization_barrier((a, b, sums))
            if s < len(exchange):
                keep = keep + came.astype(f32)
                give = keep.astype(bf16)
            if s <= half:
                ready = ([n - s, s], [a, b]) if s < half else ([half], [a, b])
        return weigh(*ready, sums), keep, came


def split(x):
    high = x.astype(bf16)
    return high, (x - high.astype(f32)).astype(bf16)


def partial_kernel(info, x_ref, w_ref, keep_ref, give_ref, whole):
    whole[...] = jnp.dot(x_ref[...], w_ref[...], preferred_element_type=f32)
    h = keep_ref.shape[0]
    odd = lax.rem(info[info.shape[0] - 2], 2)
    keep_ref[...] = whole[pl.ds(pl.multiple_of(odd * h, 8), h), :]
    give_ref[...] = whole[pl.ds(pl.multiple_of((1 - odd) * h, 8), h), :].astype(bf16)


def partial_product(info, x, weight):
    shape = (x.shape[0] // 2, weight.shape[1])
    return pl.pallas_call(
        partial_kernel,
        grid_spec=pltpu.PrefetchScalarGridSpec(
            num_scalar_prefetch=1,
            grid=(1,),
            in_specs=[
                pl.BlockSpec(x.shape, lambda j, info: (0, 0)),
                pl.BlockSpec(weight.shape, lambda j, info: (0, 0)),
            ],
            out_specs=[pl.BlockSpec(shape, lambda j, info: (0, 0))] * 2,
            scratch_shapes=[pltpu.VMEM((x.shape[0], weight.shape[1]), f32)],
        ),
        out_shape=[jax.ShapeDtypeStruct(shape, f32), jax.ShapeDtypeStruct(shape, bf16)],
        compiler_params=pltpu.CompilerParams(vmem_limit_bytes=12 << 20),
        name="partial_product",
    )(info, x, weight)


def in_kernel(offsets, count, chunks, first_call, info, *refs):
    blocks = refs[:count]
    w_ref = refs[count]
    o_ref, spread, held, arrived = refs[-4:]
    depth = held.shape[1] * chunks
    rows = o_ref.shape[0] // 2
    part = depth // chunks
    copies = []
    for b, offset in enumerate(offsets):
        for c in range(chunks):
            at = pl.multiple_of(info[offset] * depth + c * part, part)
            slot = b * chunks + c
            copies.append(
                pltpu.make_async_copy(w_ref.at[pl.ds(at, part)], held.at[slot], arrived.at[slot])
            )
    for copy in copies:
        copy.start()

    lane = lax.broadcasted_iota(jnp.int32, (128, 512), 1)
    sub = lax.broadcasted_iota(jnp.int32, (128, 512), 0)
    target = jnp.where(lane < 256, 2 * sub, 2 * sub + 257)
    widen = jnp.where(lane == target, 1.0, 0.0).astype(bf16)
    for b in range(len(offsets)):
        base = 0
        for block in [blocks[b]] if count == len(offsets) else blocks:
            r = block.shape[0]
            for p in range(depth // 128):
                piece = block[:, p * 128 : (p + 1) * 128]
                both = jnp.dot(piece, widen, preferred_element_type=f32).astype(bf16)
                spread[b, base : base + r, p * 256 : (p + 1) * 256] = both[:, :256]
                spread[b, rows + base : rows + base + r, p * 256 : (p + 1) * 256] = both[:, 256:]
            base += r

    for slot, copy in enumerate(copies):
        b, c = slot // chunks, slot % chunks
        copy.wait()
        w = held[slot].reshape(2 * part, held.shape[3])
        x = spread[b, :, c * 2 * part : (c + 1) * 2 * part]
        term = jnp.dot(x, w, preferred_element_type=f32)
        if slot == 0:
            o_ref[...] = term if first_call else refs[count + 1][...] + term
        else:
            o_ref[...] += term


def in_product(info, offsets, blocks, weight, depth, acc):
    count = len(blocks)
    rows = sum(b.shape[0] for b in blocks) // len(offsets)
    cols = weight.shape[2]
    chunks = 2 if depth % 512 == 0 else 1
    slots = chunks * len(offsets)

    def fixed(shape):
        return pl.BlockSpec(shape, lambda j, info: (0, 0))

    in_specs = [fixed(b.shape) for b in blocks]
    in_specs.append(pl.BlockSpec(memory_space=pl.ANY))
    operands = [info, *blocks, weight]
    aliases = {}
    shape = (2 * rows, cols)
    if acc is not None:
        in_specs.append(fixed(shape))
        aliases = {len(operands): 0}
        operands.append(acc)
    return pl.pallas_call(
        functools.partial(in_kernel, offsets, count, chunks, acc is None),
        grid_spec=pltpu.PrefetchScalarGridSpec(
            num_scalar_prefetch=1,
            grid=(1,),
            in_specs=in_specs,
            out_specs=fixed(shape),
            scratch_shapes=[
                pltpu.VMEM((len(offsets), 2 * rows, 2 * depth), bf16),
                pltpu.VMEM((slots, depth // chunks, 2, cols), bf16),
                pltpu.SemaphoreType.DMA((slots,)),
            ],
        ),
        out_shape=jax.ShapeDtypeStruct(shape, f32),
        input_output_aliases=aliases,
        compiler_params=pltpu.CompilerParams(vmem_limit_bytes=30 << 20),
        cost_estimate=pl.CostEstimate(
            flops=len(offsets) * 8 * rows * depth * cols,
            bytes_accessed=len(offsets) * depth * cols * 8,
            transcendentals=0,
        ),
        name="in_product",
    )(*operands)


def lanes_of(columns, rows):
    lane = lax.broadcasted_iota(jnp.int32, (rows, 128), 1)
    out = jnp.zeros((rows, 128), f32)
    for at, value in columns:
        out = jnp.where(lane == at, value.astype(f32), out)
    return out.astype(bf16)


def energy_lanes(energy):
    high, low = split(energy)
    return lanes_of([(0, high), (1, low)], energy.shape[0])


def energy_of(lanes):
    wide = lanes.astype(f32)
    return wide[:, 0:1] + wide[:, 1:2]


def join_kernel(kind, depth, with_energy, *refs):
    refs = list(refs)
    e_ref = refs.pop(0) if with_energy else None
    term_ref = refs.pop(0)
    outs = refs[-2:]
    got = refs[:-2]
    rows = term_ref.shape[0] if kind == "first" else term_ref.shape[0] // 2
    h = rows // 2
    sides = [slice(0, h), slice(h, rows)]
    main, tail = slice(0, depth), slice(depth, depth + 128)
    for j in range(2):
        mine, other = sides[j], sides[1 - j]
        out = outs[j]
        if kind == "first":
            out[:, main] = term_ref[mine].astype(bf16)
            if with_energy:
                out[:, tail] = energy_lanes(e_ref[mine])
            continue
        base = j * rows
        if kind == "second":
            own = slice(base + mine.start, base + mine.stop)
            rest = slice(base + other.start, base + other.stop)
            out[mine, main] = (term_ref[own] + got[j][:, main].astype(f32)).astype(bf16)
            out[other, main] = term_ref[rest].astype(bf16)
            if with_energy:
                out[mine, tail] = energy_lanes(e_ref[mine] + energy_of(got[j][:, tail]))
                out[other, tail] = energy_lanes(e_ref[other])
        else:
            whole = slice(base, base + rows)
            out[:, main] = (term_ref[whole] + got[j][:, main].astype(f32)).astype(bf16)
            if with_energy:
                out[:, tail] = energy_lanes(e_ref[...] + energy_of(got[j][:, tail]))


def join(kind, rows, depth, energy, terms, got):
    wide = depth + (0 if energy is None else 128)
    high = rows // 2 if kind == "first" else rows
    operands = ([] if energy is None else [energy]) + [terms] + got
    return pl.pallas_call(
        functools.partial(join_kernel, kind, depth, energy is not None),
        out_shape=[jax.ShapeDtypeStruct((high, wide), bf16)] * 2,
        compiler_params=pltpu.CompilerParams(vmem_limit_bytes=12 << 20),
        cost_estimate=pl.CostEstimate(flops=0, bytes_accessed=rows * wide * 8, transcendentals=0),
        name="join",
    )(*operands)


def term_kernel(info, lhs_ref, w_ref, o_ref):
    o_ref[...] = jnp.dot(lhs_ref[...], w_ref[...], preferred_element_type=f32)


def terms_of(info, offsets, lhs, weight, depth):
    rows = lhs.shape[0]
    return pl.pallas_call(
        term_kernel,
        grid_spec=pltpu.PrefetchScalarGridSpec(
            num_scalar_prefetch=1,
            grid=(len(offsets), 1),
            in_specs=[
                fixed_block(lhs.shape),
                pl.BlockSpec((weight.shape[0], depth), column_block(offsets, 1)),
            ],
            out_specs=pl.BlockSpec((rows, depth), lambda j, c, info: (j, 0)),
        ),
        out_shape=jax.ShapeDtypeStruct((len(offsets) * rows, depth), f32),
        compiler_params=pltpu.CompilerParams(vmem_limit_bytes=46 << 20),
        cost_estimate=pl.CostEstimate(
            flops=len(offsets) * 2 * rows * depth * weight.shape[0],
            bytes_accessed=len(offsets) * depth * weight.shape[0] * 2,
            transcendentals=0,
        ),
        name="terms",
    )(info, lhs, weight)


def tile_of(depth):
    return min(1024, depth)


def column_block(offsets, steps):
    def at(j, c, info, *more):
        device = info[offsets[0]]
        for b in range(1, len(offsets)):
            device = jnp.where(j == b, info[offsets[b]], device)
        return (0, device * steps + c)

    return at


def fixed_block(shape):
    return pl.BlockSpec(shape, lambda j, c, *s: (0,) * len(shape))


def ring_sum(ring, info, lhs, weight, depth, energy=None):
    n, half = ring.n, ring.half
    rows = lhs.shape[0]
    terms = terms_of(info, [half], lhs, weight, depth)
    a, b = join("first", rows, depth, energy, terms, [])
    for d in range(half - 1, -1, -1):
        lhs, a, b = lax.optimization_barrier((lhs, a, b))
        a, b = ring.right(a), ring.left(b)
        terms = terms_of(info, [d, n - d] if d > 0 else [0], lhs, weight, depth)
        terms, a, b = lax.optimization_barrier((terms, a, b))
        if d > 0:
            kind = "second" if d == half - 1 else "later"
            a, b = join(kind, rows, depth, energy, terms, [a, b])
    return terms, ([a, b] if half > 1 else [jnp.concatenate([a, b], axis=0)])


def mixer_kernel(arrived, tenants, inner_size, info, adapter, term_ref, *refs):
    got = refs[:arrived]
    e_ref, tok_ref, gain_ref = refs[arrived : arrived + 3]
    downs = refs[arrived + 3 : arrived + 3 + tenants]
    first_ref, message_ref = refs[-2:]
    rows, depth = term_ref.shape
    length = rows // tenants
    tail = slice(depth, depth + 128)
    energy = e_ref[...]
    total = term_ref[...]
    for g in got:
        energy = energy + energy_of(g[:, tail])
        total = total + g[:, :depth].astype(f32)
    scale = lax.rsqrt(energy / inner_size + epsilon)
    first = (tok_ref[...].astype(f32) + total * scale).astype(bf16)
    wide = first.astype(f32)
    high, low = split(jnp.sum(wide * wide, axis=1, keepdims=True))
    first_ref[...] = first
    attn = (wide * gain_ref[...]).astype(bf16)
    message_ref[:, :depth] = attn
    rank = downs[0].shape[1]
    parts = []
    for i in range(tenants):
        x = attn[i * length : (i + 1) * length]
        parts.append(
            lax.dot_general(x, downs[i][0], (((1,), (1,)), ((), ())), preferred_element_type=f32)
        )
    small = jnp.concatenate(parts, axis=0).astype(bf16)
    message_ref[:, tail] = lanes_of([(rank, high), (rank + 1, low)], rows)
    message_ref[:, depth : depth + rank] = small


def mixer_step(info, adapter, terms, got, energy, own_tokens, gain, down, inner_size):
    rows, depth = terms.shape
    tenants = adapter.shape[0]
    operands = [terms, *got, energy, own_tokens, gain] + [down] * tenants

    def whole(a):
        return pl.BlockSpec(a.shape, lambda j, *s: (0,) * a.ndim)

    in_specs = [whole(a) for a in operands]
    in_specs[3 + len(got)] = pl.BlockSpec(
        (1, depth), lambda j, info, adapter: (0, info[info.shape[0] - 2])
    )
    for i in range(tenants):
        in_specs[4 + len(got) + i] = pl.BlockSpec(
            (1, *down.shape[1:]), functools.partial(lambda i, j, info, adapter: (adapter[i], 0, 0), i)
        )
    shapes = [jax.ShapeDtypeStruct((rows, depth), bf16), jax.ShapeDtypeStruct((rows, depth + 128), bf16)]
    return pl.pallas_call(
        functools.partial(mixer_kernel, len(got), tenants, inner_size),
        grid_spec=pltpu.PrefetchScalarGridSpec(
            num_scalar_prefetch=2,
            grid=(1,),
            in_specs=in_specs,
            out_specs=[whole(s) for s in shapes],
        ),
        out_shape=shapes,
        compiler_params=pltpu.CompilerParams(vmem_limit_bytes=16 << 20),
        cost_estimate=pl.CostEstimate(
            flops=2 * rows * depth * 64, bytes_accessed=rows * depth * 16, transcendentals=0
        ),
        name="mixer_step",
    )(info, adapter, *operands)


def query_kernel(offsets, count, first_call, info, *refs):
    blocks = refs[:count]
    w_ref = refs[count]
    q_ref, l_ref = refs[-2:]
    j, k = pl.program_id(0), pl.program_id(1)
    kb = w_ref.shape[0]
    steps = pl.num_programs(1)
    depth = blocks[0].shape[1] - 128

    @pl.when((j == 0) & (k == 0))
    def _():
        if first_call:
            q_ref[...] = jnp.zeros_like(q_ref)
            l_ref[...] = jnp.zeros_like(l_ref)
        else:
            q_ref[...] = refs[count + 1][...]
            l_ref[...] = refs[count + 2][...]

    for b in range(len(offsets)):
        for kk in range(depth // kb):

            @pl.when((j == b) & (k == kk))
            def _():
                pieces = [blocks[b]] if count == len(offsets) else blocks
                base = 0
                for block in pieces:
                    at = slice(base, base + block.shape[0])
                    q_ref[at] += jnp.dot(
                        block[:, kk * kb : (kk + 1) * kb], w_ref[...], preferred_element_type=f32
                    )
                    if kk == 0:
                        l_ref[at] += block[:, depth:].astype(f32)
                    base += block.shape[0]


def query_step(info, offsets, blocks, weight, depth, accs):
    count = len(blocks)
    rows = sum(b.shape[0] for b in blocks) // len(offsets)
    cols = weight.shape[1]
    kb = tile_of(depth)
    steps = depth // kb

    def row_block(j, k, info):
        at = info[offsets[0]]
        for b in range(1, len(offsets)):
            at = jnp.where(j == b, info[offsets[b]], at)
        return (at * steps + k, 0)

    shapes = [(rows, cols), (rows, 128)]
    in_specs = [fixed_block(b.shape) for b in blocks] + [pl.BlockSpec((kb, cols), row_block)]
    operands = [info, *blocks, weight]
    aliases = {}
    if accs is not None:
        in_specs += [fixed_block(s) for s in shapes]
        aliases = {len(operands): 0, len(operands) + 1: 1}
        operands += accs
    return pl.pallas_call(
        functools.partial(query_kernel, offsets, count, accs is None),
        grid_spec=pltpu.PrefetchScalarGridSpec(
            num_scalar_prefetch=1,
            grid=(len(offsets), steps),
            in_specs=in_specs,
            out_specs=[fixed_block(s) for s in shapes],
        ),
        out_shape=[jax.ShapeDtypeStruct(s, f32) for s in shapes],
        input_output_aliases=aliases,
        compiler_params=pltpu.CompilerParams(vmem_limit_bytes=16 << 20),
        cost_estimate=pl.CostEstimate(
            flops=len(offsets) * 2 * rows * depth * cols,
            bytes_accessed=len(offsets) * depth * cols * 2,
            transcendentals=0,
        ),
        name="query_step",
    )(*operands)


def shifted(history, x, k):
    if k == 3:
        return x
    return jnp.concatenate([history[k:3], x[: x.shape[0] - 3 + k]], axis=0)


def conv_silu(history, x, taps):
    total = taps[0:1] * shifted(history, x, 0)
    for k in range(1, 4):
        total = total + taps[k : k + 1] * shifted(history, x, k)
    return total * jax.nn.sigmoid(total)


def spans(heads, width):
    lane = lax.broadcasted_iota(jnp.int32, (heads, heads * width), 1)
    row = lax.broadcasted_iota(jnp.int32, (heads, heads * width), 0)
    return jnp.where(lane // width == row, 1.0, 0.0).astype(f32)


def state_kernel(
    slot,
    info,
    x_ref,
    z_ref,
    kept_ref,
    came_ref,
    hx_ref,
    hbc_ref,
    tx_ref,
    tbc_ref,
    bias_ref,
    rate_ref,
    skip_ref,
    gain_ref,
    own_ref,
    far_ref,
    gated_ref,
    energy_ref,
    final_ref,
    initial,
    *,
    slots,
):
    i = pl.program_id(0)
    count = info.shape[0]
    is_own = slot[i] // slots == info[count - 1]

    @pl.when(is_own)
    def _():
        initial[...] = own_ref[0]

    @pl.when(jnp.logical_not(is_own))
    def _():
        initial[...] = far_ref[0]

    length = x_ref.shape[0]
    heads = bias_ref.shape[1]
    values = conv_silu(hx_ref[0], x_ref[...].astype(bf16).astype(f32), tx_ref[...])
    shared = i // (pl.num_programs(0) // 2) == lax.rem(info[count - 2], 2)
    projected = jnp.where(shared, kept_ref[...], came_ref[...].astype(f32))
    bc = conv_silu(hbc_ref[0], projected[:, : 2 * STATE], tbc_ref[...])
    all_raw = projected[:, 2 * STATE :]
    pick = (all_raw.shape[1], heads)
    chosen = lax.broadcasted_iota(jnp.int32, pick, 0) == (
        lax.broadcasted_iota(jnp.int32, pick, 1) + info[count - 2] * heads
    )
    chosen = jnp.where(chosen, 1.0, 0.0).astype(f32)
    in_state = bc[:, :STATE].astype(bf16)
    out_state = bc[:, STATE:].astype(bf16)
    raw = jnp.dot(all_raw, chosen, precision=highest, preferred_element_type=f32) + bias_ref[...]
    steps = jnp.maximum(raw, 0.0) + jnp.log1p(jnp.exp(-jnp.abs(raw)))
    log_decay = -steps * jnp.exp(rate_ref[...])
    row = lax.broadcasted_iota(jnp.int32, (length, length), 0)
    col = lax.broadcasted_iota(jnp.int32, (length, length), 1)
    lower = jnp.where(row >= col, 1.0, 0.0).astype(f32)
    running = jnp.dot(lower, log_decay, precision=highest, preferred_element_type=f32)
    last = running[length - 1 : length]

    wide = spans(heads, length)
    both = jnp.dot(
        jnp.concatenate([running, steps], axis=0), wide, precision=highest, preferred_element_type=f32
    )
    run_t, step_t = both[:length], both[length:]
    lane = lax.broadcasted_iota(jnp.int32, (length, heads * length), 1) % length
    place = lax.broadcasted_iota(jnp.int32, (length, heads * length), 0)
    diagonal = lane == place
    run_s = jnp.sum(jnp.where(diagonal, run_t, 0.0), axis=0, keepdims=True)
    step_s = jnp.sum(jnp.where(diagonal, step_t, 0.0), axis=0, keepdims=True)
    seen = place >= lane
    decays = jnp.where(seen, jnp.exp(jnp.where(seen, run_t - run_s, 0.0)), 0.0)
    overlap = lax.dot_general(
        out_state,
        jnp.concatenate([in_state] * heads, axis=0),
        (((1,), (1,)), ((), ())),
        preferred_element_type=f32,
    )
    mixing = (overlap * decays * step_s).astype(bf16)
    short = values.astype(bf16)
    group = min(4, heads)
    gl, gw = group * length, group * HDIM
    own_block = (
        lax.broadcasted_iota(jnp.int32, (gl, gw), 0) // length
        == lax.broadcasted_iota(jnp.int32, (gl, gw), 1) // HDIM
    )
    within = []
    for g in range(heads // group):
        v = jnp.concatenate([values[:, g * gw : (g + 1) * gw]] * group, axis=0)
        v = jnp.where(own_block, v, 0.0).astype(bf16)
        within.append(jnp.dot(mixing[:, g * gl : (g + 1) * gl], v, preferred_element_type=f32))
    within = within[0] if len(within) == 1 else jnp.concatenate(within, axis=1)

    narrow = spans(heads, HDIM)
    scales = jnp.dot(
        jnp.concatenate(
            [
                jnp.exp(running),
                jnp.exp(last - running) * steps,
                jnp.broadcast_to(skip_ref[...], (8, heads)),
            ],
            axis=0,
        ),
        narrow,
        precision=highest,
        preferred_element_type=f32,
    )
    start = initial[...]
    carried = lax.dot_general(
        out_state, start.astype(bf16), (((1,), (1,)), ((), ())), preferred_element_type=f32
    )
    result = within + carried * scales[:length] + scales[2 * length : 2 * length + 1] * values
    z = z_ref[...].astype(bf16).astype(f32)
    gated = result * (z * jax.nn.sigmoid(z))
    energy_ref[...] = jnp.sum(gated * gated, axis=1, keepdims=True)
    gated_ref[...] = (gated * gain_ref[...]).astype(bf16)

    kept = jnp.exp(
        lax.dot_general(
            log_decay,
            jnp.ones((length, STATE), f32),
            (((0,), (0,)), ((), ())),
            precision=highest,
            preferred_element_type=f32,
        )
    )
    update = lax.dot_general(
        (values * scales[length : 2 * length]).astype(bf16),
        in_state,
        (((0,), (0,)), ((), ())),
        preferred_element_type=f32,
    )
    for h in range(heads):
        at = slice(h * HDIM, (h + 1) * HDIM)
        final_ref[0, at, :] = update[at] + start[at] * kept[h : h + 1]


def state_pass(
    info, slot, inner, kept, came, hx, hbc, tx, tbc, bias, rate, skip, gain, own_pool, far_pool
):
    tenants = slot.shape[0]
    length = inner.shape[0] // 2 // tenants
    cols = inner.shape[1]
    slots = own_pool.shape[0]

    def rows(width):
        return pl.BlockSpec((length, width), lambda i, *s: (i, 0))

    def whole(a):
        return pl.BlockSpec(a.shape, lambda i, *s: (0,) * a.ndim)

    def own_slot(i, slot, info):
        return (jnp.clip(slot[i] - info[info.shape[0] - 1] * slots, 0, slots - 1), 0, 0)

    def far_slot(i, slot, info):
        return (jnp.clip(slot[i] - (1 - info[info.shape[0] - 1]) * slots, 0, slots - 1), 0, 0)

    pooled = (1, cols, STATE)
    return pl.pallas_call(
        functools.partial(state_kernel, slots=slots),
        grid_spec=pltpu.PrefetchScalarGridSpec(
            num_scalar_prefetch=2,
            grid=(tenants,),
            in_specs=[
                rows(cols),
                pl.BlockSpec((length, cols), lambda i, *s: (tenants + i, 0)),
                pl.BlockSpec((length, kept.shape[1]), lambda i, *s: (i % (tenants // 2), 0)),
                pl.BlockSpec((length, kept.shape[1]), lambda i, *s: (i % (tenants // 2), 0)),
                pl.BlockSpec((1, 3, cols), lambda i, *s: (i, 0, 0)),
                pl.BlockSpec((1, 3, 2 * STATE), lambda i, *s: (i, 0, 0)),
                whole(tx),
                whole(tbc),
                whole(bias),
                whole(rate),
                whole(skip),
                whole(gain),
                pl.BlockSpec(pooled, own_slot),
                pl.BlockSpec(pooled, far_slot),
            ],
            out_specs=[
                rows(cols),
                rows(1),
                pl.BlockSpec(pooled, lambda i, *s: (i, 0, 0)),
            ],
            scratch_shapes=[pltpu.VMEM((cols, STATE), f32)],
        ),
        out_shape=[
            jax.ShapeDtypeStruct((tenants * length, cols), bf16),
            jax.ShapeDtypeStruct((tenants * length, 1), f32),
            jax.ShapeDtypeStruct((tenants, cols, STATE), f32),
        ],
        compiler_params=pltpu.CompilerParams(vmem_limit_bytes=28 << 20),
        cost_estimate=pl.CostEstimate(
            flops=tenants * 6 * length * cols * STATE,
            bytes_accessed=tenants * cols * STATE * 10,
            transcendentals=0,
        ),
        name="state_pass",
    )(slot, info, inner, inner, kept, came, hx, hbc, tx, tbc, bias, rate, skip, gain, own_pool, far_pool)


def attend_kernel(
    width, table, limit, adapter, info, q_ref, low_ref, up_ref, near_ref, far_ref, *refs
):
    o_ref = refs[-1]
    i = pl.program_id(0)
    length = q_ref.shape[0]
    heads = q_ref.shape[1] // HEAD_SIZE
    blocks = table.shape[1]
    part = near_ref.shape[1]
    core = info[info.shape[0] - 1]
    rank = up_ref.shape[1]
    square = low_ref[:, rank : rank + 1] + low_ref[:, rank + 1 : rank + 2]
    norm = lax.rsqrt(square / width + epsilon)
    low = (low_ref[:, :rank] * norm).astype(bf16)
    raised = jnp.dot(low, up_ref[0], preferred_element_type=f32)
    q = (q_ref[...] * norm + adapter_scale * raised).astype(bf16)
    q = jnp.concatenate([q[:, h * HEAD_SIZE : (h + 1) * HEAD_SIZE] for h in range(heads)], axis=0)
    fresh = jnp.concatenate([refs[0][...], refs[1][...]], axis=1)
    for came in refs[2:-1]:
        fresh = fresh + came[...].astype(f32)
    fresh = (fresh * norm).astype(bf16)
    pieces = []
    for j in range(blocks):
        at = table[i, j]
        pieces += [near_ref[at], far_ref[at]]
    cached = jnp.concatenate(pieces, axis=0)
    context = cached.shape[0]
    nt = (((1,), (1,)), ((), ()))
    scale = HEAD_SIZE ** (-0.5)
    old = lax.dot_general(q, cached[:, :HEAD_SIZE], nt, preferred_element_type=f32) * scale
    new = lax.dot_general(q, fresh[:, :HEAD_SIZE], nt, preferred_element_type=f32) * scale
    lane = lax.broadcasted_iota(jnp.int32, old.shape, 1)
    inside = lane % (2 * part)
    far_side = jnp.where(inside >= part, 1, 0)
    half = jnp.where(core == 0, far_side, 1 - far_side)
    place = (lane // (2 * part)) * (2 * part) + half * part + inside % part
    old_seen = place < limit[i]
    token = lax.broadcasted_iota(jnp.int32, new.shape, 0) % length
    new_seen = lax.broadcasted_iota(jnp.int32, new.shape, 1) <= token
    old = jnp.where(old_seen, old, -jnp.inf)
    new = jnp.where(new_seen, new, -jnp.inf)
    top = jnp.maximum(jnp.max(old, axis=1, keepdims=True), jnp.max(new, axis=1, keepdims=True))
    old = jnp.where(old_seen, jnp.exp(old - top), 0.0)
    new = jnp.where(new_seen, jnp.exp(new - top), 0.0)
    share = 1.0 / (jnp.sum(old, axis=1, keepdims=True) + jnp.sum(new, axis=1, keepdims=True))
    out = jnp.dot((old * share).astype(bf16), cached[:, HEAD_SIZE:], preferred_element_type=f32)
    out += jnp.dot((new * share).astype(bf16), fresh[:, HEAD_SIZE:], preferred_element_type=f32)
    out = out.astype(bf16)
    for h in range(heads):
        o_ref[:, h * HEAD_SIZE : (h + 1) * HEAD_SIZE] = out[h * length : (h + 1) * length]


def attend(ring, width, table, limit, adapter, info, q, low, up, near, far, kv, kv_came):
    tenants = table.shape[0]
    length = q.shape[0] // tenants

    def rows(a):
        return pl.BlockSpec((length, a.shape[1]), lambda i, *s: (i, 0))

    def whole(a):
        return pl.BlockSpec(a.shape, lambda i, *s: (0,) * a.ndim)

    def own(base):
        return pl.BlockSpec(
            (length, HEAD_SIZE), lambda i, t, n, a, info: (i, base + info[ring.n])
        )

    return pl.pallas_call(
        functools.partial(attend_kernel, width),
        grid_spec=pltpu.PrefetchScalarGridSpec(
            num_scalar_prefetch=4,
            grid=(tenants,),
            in_specs=[
                rows(q),
                rows(low),
                pl.BlockSpec((1, *up.shape[1:]), lambda i, t, n, a, info: (a[i], 0, 0)),
                whole(near),
                whole(far),
                own(0),
                own(KEY_HEADS),
            ]
            + [rows(a) for a in kv_came],
            out_specs=rows(q),
        ),
        out_shape=jax.ShapeDtypeStruct(q.shape, bf16),
        compiler_params=pltpu.CompilerParams(vmem_limit_bytes=24 << 20),
        cost_estimate=pl.CostEstimate(
            flops=tenants * 4 * length * q.shape[1] * 288,
            bytes_accessed=near.size * 4 + q.size * 6 + up.size,
            transcendentals=0,
        ),
        name="attend",
    )(table, limit, adapter, info, q, low, up, near, far, kv, kv, *kv_came)


def pick_kernel(info, key_ref, value_ref, o_ref):
    o_ref[0, :, :, :HEAD_SIZE] = key_ref[...]
    o_ref[0, :, :, HEAD_SIZE:] = value_ref[...]


def pick_heads(info, pool, devices, pools):
    count, block_len, _ = pool.shape
    part = block_len // pools
    each = QUERY_HEADS // devices
    group = QUERY_HEADS // KEY_HEADS

    def lanes(base):
        return pl.BlockSpec(
            (count, part, HEAD_SIZE),
            lambda d, info: (0, info[info.shape[0] - 1], base + lax.div(d * each, group)),
        )

    shape = (devices, count, part, 2 * HEAD_SIZE)
    return pl.pallas_call(
        pick_kernel,
        grid_spec=pltpu.PrefetchScalarGridSpec(
            num_scalar_prefetch=1,
            grid=(devices,),
            in_specs=[lanes(0), lanes(KEY_HEADS)],
            out_specs=pl.BlockSpec((1, *shape[1:]), lambda d, info: (d, 0, 0, 0)),
        ),
        out_shape=jax.ShapeDtypeStruct(shape, bf16),
        compiler_params=pltpu.CompilerParams(vmem_limit_bytes=8 << 20),
        name="pick_heads",
    )(info, pool, pool)


def fresh_kernel(kind, offsets, heads_at, info, kv_ref, *refs):
    outs = refs[-2:]
    got = refs[:-2]
    rows = kv_ref.shape[0]
    h = rows // 2
    sides = [slice(0, h), slice(h, rows)]
    for j in range(2):
        offset = offsets[0] if kind == "first" else offsets[j]
        head = info[heads_at + offset]
        for k in range(2):
            at = pl.ds(pl.multiple_of((head + k * KEY_HEADS) * HEAD_SIZE, HEAD_SIZE), HEAD_SIZE)
            to = slice(k * HEAD_SIZE, (k + 1) * HEAD_SIZE)
            if kind == "first":
                outs[j][:, to] = kv_ref[sides[j], at].astype(bf16)
            elif kind == "second":
                mine, other = sides[j], sides[1 - j]
                outs[j][mine, to] = (kv_ref[mine, at] + got[j][:, to].astype(f32)).astype(bf16)
                outs[j][other, to] = kv_ref[other, at].astype(bf16)
            else:
                outs[j][:, to] = (kv_ref[:, at] + got[j][:, to].astype(f32)).astype(bf16)


def fresh_join(info, kind, offsets, heads_at, kv, got):
    rows = kv.shape[0]
    shape = (rows // 2 if kind == "first" else rows, 2 * HEAD_SIZE)
    operands = [kv, *got]
    return pl.pallas_call(
        functools.partial(fresh_kernel, kind, offsets, heads_at),
        grid_spec=pltpu.PrefetchScalarGridSpec(
            num_scalar_prefetch=1,
            grid=(1,),
            in_specs=[pl.BlockSpec(a.shape, lambda j, info: (0, 0)) for a in operands],
            out_specs=[pl.BlockSpec(shape, lambda j, info: (0, 0))] * 2,
        ),
        out_shape=[jax.ShapeDtypeStruct(shape, bf16)] * 2,
        compiler_params=pltpu.CompilerParams(vmem_limit_bytes=8 << 20),
        name="fresh_join",
    )(info, *operands)


def per_device(
    ring,
    tokens,
    mamba_in_weight,
    state_projection,
    inner_taps,
    state_taps,
    inner_history,
    state_history,
    step_size_bias,
    log_decay_rate,
    skip_factor,
    gated_norm_gain,
    mamba_out_weight,
    saved_state_pool,
    tenant_state_slot,
    attention_gain,
    query_matrix,
    adapter_down,
    adapter_up,
    tenant_adapter,
    key_value_weight,
    key_value_pool,
    tenant_blocks,
    cached_length,
    attention_out_weight,
):
    n, half, pools = ring.n, ring.half, ring.pools
    tenants, length, depth = tokens.shape
    rows = tenants * length
    width = depth * n
    info = ring.info()
    own_tokens = tokens.reshape(rows, depth)
    heads = step_size_bias.shape[0]
    cols = mamba_in_weight.shape[2]
    swap = [(i, (i + 1) % pools) for i in range(pools)]

    slots = saved_state_pool.shape[0]
    flat_pool = saved_state_pool.reshape(slots, heads * HDIM, STATE)
    far_pool = lax.ppermute(flat_pool, "pool", swap)

    keep, give = partial_product(info, own_tokens, state_projection)
    inner, kept, came = ring.gather(
        own_tokens,
        lambda offsets, blocks, acc: in_product(info, offsets, blocks, mamba_in_weight, depth, acc),
        keep,
        give,
    )

    mine = pick_heads(info, key_value_pool, n, pools)
    mine, inner = lax.optimization_barrier((mine, inner))
    cache = lax.all_to_all(mine, "tensor", 0, 0, tiled=True)
    cache = cache.reshape(-1, *cache.shape[2:])
    far_cache = lax.ppermute(cache, "pool", swap)

    gated, energy, final_state = state_pass(
        info,
        tenant_state_slot,
        inner,
        kept,
        came,
        inner_history.astype(f32),
        state_history,
        inner_taps.astype(f32),
        state_taps.astype(f32),
        step_size_bias[None],
        log_decay_rate[None],
        skip_factor[None],
        gated_norm_gain[None],
        flat_pool,
        far_pool,
    )
    terms, got = ring_sum(ring, info, gated, mamba_out_weight, depth, energy)
    first, message = mixer_step(
        info,
        tenant_adapter,
        terms,
        got,
        energy,
        own_tokens,
        attention_gain[None],
        adapter_down.transpose(0, 2, 1),
        cols * n,
    )

    kv = jnp.dot(message[:, :depth], key_value_weight, preferred_element_type=f32)

    h = rows // 2
    a, b = message, message
    ka, kb = fresh_join(info, "first", [half], n, kv, [])
    accs, ready = None, ([0], [message])
    for s in range(1, half + 1):
        if s == half:
            a, b = a[:h], b[h:]
        a, b, ka, kb = ring.right(a), ring.left(b), ring.right(ka), ring.left(kb)
        accs = query_step(info, *ready, query_matrix, depth, accs)
        a, b, ka, kb, accs = lax.optimization_barrier((a, b, ka, kb, accs))
        ready = ([n - s, s], [a, b]) if s < half else ([half], [a, b])
        if s < half:
            kind = "second" if s == 1 else "later"
            ka, kb = fresh_join(info, kind, [half - s, n - half + s], n, kv, [ka, kb])
    kv_came = [ka, kb] if half > 1 else [jnp.concatenate([ka, kb], axis=0)]
    query, low = query_step(info, *ready, query_matrix, depth, accs)
    heads_out = attend(
        ring,
        width,
        tenant_blocks,
        cached_length,
        tenant_adapter,
        info,
        query,
        low,
        adapter_up,
        cache,
        far_cache,
        kv,
        kv_came,
    )
    terms, got = ring_sum(ring, info, heads_out, attention_out_weight, depth)
    second = terms + first.astype(f32)
    for g in got:
        second = second + g.astype(f32)
    second = second.astype(bf16)
    return (
        second.reshape(tenants, length, depth),
        final_state.reshape(tenants, heads, HDIM, STATE),
    )


def solution(mesh):
    in_specs = (
        P(("groups", "pool"), None, "tensor"),
        P(None, None, "tensor"),
        P("tensor", None),
        P(None, "tensor"),
        P(),
        P(("groups", "pool"), None, "tensor"),
        P(("groups", "pool"), None, None),
        P("tensor"),
        P("tensor"),
        P("tensor"),
        P("tensor"),
        P("tensor", None),
        P(("groups", "pool"), "tensor", None, None),
        P(("groups", "pool")),
        P(),
        P(None, "tensor"),
        P(None, "tensor", None),
        P(None, None, "tensor"),
        P(("groups", "pool")),
        P("tensor", None),
        P(("groups", "tensor"), None, None),
        P(("groups", "pool"), None),
        P(("groups", "pool")),
        P("tensor", None),
    )
    out_specs = (P(("groups", "pool"), None, "tensor"), P(("groups", "pool"), "tensor", None, None))
    ring = Ring(mesh.shape["tensor"], mesh.shape["pool"])
    return jax.shard_map(
        functools.partial(per_device, ring),
        mesh=mesh,
        in_specs=in_specs,
        out_specs=out_specs,
        check_vma=False,
    )
```

```python
import functools

import jax
import jax.numpy as jnp
from jax import lax
from jax.experimental import pallas as pl
from jax.experimental.pallas import tpu as pltpu
from jax.sharding import PartitionSpec as P

HDIM = 64
STATE = 256
QUERY_HEADS = 64
KEY_HEADS = 8
HEAD_SIZE = 128

epsilon = 1e-05
adapter_scale = 2.0
highest = lax.Precision.HIGHEST
f32 = jnp.float32
bf16 = jnp.bfloat16


def ring_order(n):
    cols = 1
    for c in range(2, n):
        if n % c == 0 and (n // c) % 2 == 0 and c <= n // c:
            cols = c
    if cols == 1:
        return list(range(n))
    rows = n // cols
    order = [r * cols for r in range(rows)]
    for k, r in enumerate(reversed(range(rows))):
        across = list(range(1, cols))
        order += [r * cols + c for c in (across if k % 2 == 0 else across[::-1])]
    return order


class Ring:
    def __init__(self, n, pools):
        self.n = n
        heads = [d * QUERY_HEADS // n // (QUERY_HEADS // KEY_HEADS) for d in range(n)]
        self.half = n // 2
        self.pools = pools
        order = ring_order(n)
        place = {d: i for i, d in enumerate(order)}
        self.table = [
            [order[(place[d] + s) % n] for s in range(n)]
            + [heads[order[(place[d] + s) % n]] for s in range(n)]
            + [d, c]
            for d in range(n)
            for c in range(pools)
        ]
        self.heads = heads
        self.cw = [(order[i], order[(i + 1) % n]) for i in range(n)]
        self.ccw = [(order[i], order[(i - 1) % n]) for i in range(n)]

    def info(self):
        at = lax.axis_index("tensor") * self.pools + lax.axis_index("pool")
        return lax.dynamic_slice_in_dim(jnp.array(self.table, jnp.int32), at, 1, 0)[0]

    def right(self, x):
        return lax.ppermute(x, "tensor", self.cw)

    def left(self, x):
        return lax.ppermute(x, "tensor", self.ccw)

    def masks(self):
        found, m = [], 1
        while m < self.n:
            found.append([(i, i ^ m) for i in range(self.n)])
            m *= 2
        return found

    def gather(self, x, weigh, project, aside):
        n, half = self.n, self.half
        h = x.shape[0] // 2
        pairs = self.masks()
        exchange = pairs + pairs[:1]
        sums, ready = None, ([0], [x])
        a = b = x
        for s in range(1, max(half, len(exchange)) + 1):
            if s == half:
                a, b, aside = lax.optimization_barrier((a[:h], b[h:], aside))
                aside = lax.all_to_all(aside, "tensor", 0, 0, tiled=True)
            if s <= half:
                a, b = self.right(a), self.left(b)
            if s == 1:
                sums = weigh(*ready, sums)
                x, sums = lax.optimization_barrier((x, sums))
                keep, give = project(x)
            if s <= len(exchange):
                came = lax.ppermute(give, "tensor", exchange[s - 1])
            if 1 < s <= half:
                sums = weigh(*ready, sums)
            if s <= len(exchange):
                a, b, sums, came = lax.optimization_barrier((a, b, sums, came))
            else:
                a, b, sums = lax.optimization_barrier((a, b, sums))
            if s < len(exchange):
                keep = keep + came.astype(f32)
                give = keep.astype(bf16)
            if s <= half:
                ready = ([n - s, s], [a, b]) if s < half else ([half], [a, b])
        return weigh(*ready, sums), keep, came, aside


def split(x):
    high = x.astype(bf16)
    return high, (x - high.astype(f32)).astype(bf16)


def partial_kernel(info, x_ref, w_ref, keep_ref, give_ref, whole):
    whole[...] = jnp.dot(x_ref[...], w_ref[...], preferred_element_type=f32)
    h = keep_ref.shape[0]
    odd = lax.rem(info[info.shape[0] - 2], 2)
    keep_ref[...] = whole[pl.ds(pl.multiple_of(odd * h, 8), h), :]
    give_ref[...] = whole[pl.ds(pl.multiple_of((1 - odd) * h, 8), h), :].astype(bf16)


def partial_product(info, x, weight):
    shape = (x.shape[0] // 2, weight.shape[1])
    return pl.pallas_call(
        partial_kernel,
        grid_spec=pltpu.PrefetchScalarGridSpec(
            num_scalar_prefetch=1,
            grid=(1,),
            in_specs=[
                pl.BlockSpec(x.shape, lambda j, info: (0, 0)),
                pl.BlockSpec(weight.shape, lambda j, info: (0, 0)),
            ],
            out_specs=[pl.BlockSpec(shape, lambda j, info: (0, 0))] * 2,
            scratch_shapes=[pltpu.VMEM((x.shape[0], weight.shape[1]), f32)],
        ),
        out_shape=[jax.ShapeDtypeStruct(shape, f32), jax.ShapeDtypeStruct(shape, bf16)],
        compiler_params=pltpu.CompilerParams(vmem_limit_bytes=12 << 20),
        name="partial_product",
    )(info, x, weight)


def in_kernel(offsets, count, chunks, first_call, info, *refs):
    blocks = refs[:count]
    w_ref = refs[count]
    o_ref, spread, held, arrived = refs[-4:]
    depth = held.shape[1] * chunks
    rows = o_ref.shape[0] // 2
    part = depth // chunks
    copies = []
    for b, offset in enumerate(offsets):
        for c in range(chunks):
            at = pl.multiple_of(info[offset] * depth + c * part, part)
            slot = b * chunks + c
            copies.append(
                pltpu.make_async_copy(w_ref.at[pl.ds(at, part)], held.at[slot], arrived.at[slot])
            )
    for copy in copies:
        copy.start()

    lane = lax.broadcasted_iota(jnp.int32, (128, 512), 1)
    sub = lax.broadcasted_iota(jnp.int32, (128, 512), 0)
    target = jnp.where(lane < 256, 2 * sub, 2 * sub + 257)
    widen = jnp.where(lane == target, 1.0, 0.0).astype(bf16)
    for b in range(len(offsets)):
        base = 0
        for block in [blocks[b]] if count == len(offsets) else blocks:
            r = block.shape[0]
            for p in range(depth // 128):
                piece = block[:, p * 128 : (p + 1) * 128]
                both = jnp.dot(piece, widen, preferred_element_type=f32).astype(bf16)
                spread[b, base : base + r, p * 256 : (p + 1) * 256] = both[:, :256]
                spread[b, rows + base : rows + base + r, p * 256 : (p + 1) * 256] = both[:, 256:]
            base += r

    for slot, copy in enumerate(copies):
        b, c = slot // chunks, slot % chunks
        copy.wait()
        w = held[slot].reshape(2 * part, held.shape[3])
        x = spread[b, :, c * 2 * part : (c + 1) * 2 * part]
        term = jnp.dot(x, w, preferred_element_type=f32)
        if slot == 0:
            o_ref[...] = term if first_call else refs[count + 1][...] + term
        else:
            o_ref[...] += term


def in_product(info, offsets, blocks, weight, depth, acc):
    count = len(blocks)
    rows = sum(b.shape[0] for b in blocks) // len(offsets)
    cols = weight.shape[2]
    chunks = 2 if depth % 512 == 0 else 1
    slots = chunks * len(offsets)

    def fixed(shape):
        return pl.BlockSpec(shape, lambda j, info: (0, 0))

    in_specs = [fixed(b.shape) for b in blocks]
    in_specs.append(pl.BlockSpec(memory_space=pl.ANY))
    operands = [info, *blocks, weight]
    aliases = {}
    shape = (2 * rows, cols)
    if acc is not None:
        in_specs.append(fixed(shape))
        aliases = {len(operands): 0}
        operands.append(acc)
    return pl.pallas_call(
        functools.partial(in_kernel, offsets, count, chunks, acc is None),
        grid_spec=pltpu.PrefetchScalarGridSpec(
            num_scalar_prefetch=1,
            grid=(1,),
            in_specs=in_specs,
            out_specs=fixed(shape),
            scratch_shapes=[
                pltpu.VMEM((len(offsets), 2 * rows, 2 * depth), bf16),
                pltpu.VMEM((slots, depth // chunks, 2, cols), bf16),
                pltpu.SemaphoreType.DMA((slots,)),
            ],
        ),
        out_shape=jax.ShapeDtypeStruct(shape, f32),
        input_output_aliases=aliases,
        compiler_params=pltpu.CompilerParams(vmem_limit_bytes=30 << 20),
        cost_estimate=pl.CostEstimate(
            flops=len(offsets) * 8 * rows * depth * cols,
            bytes_accessed=len(offsets) * depth * cols * 8,
            transcendentals=0,
        ),
        name="in_product",
    )(*operands)


def lanes_of(columns, rows):
    lane = lax.broadcasted_iota(jnp.int32, (rows, 128), 1)
    out = jnp.zeros((rows, 128), f32)
    for at, value in columns:
        out = jnp.where(lane == at, value.astype(f32), out)
    return out.astype(bf16)


def energy_lanes(energy):
    high, low = split(energy)
    return lanes_of([(0, high), (1, low)], energy.shape[0])


def energy_of(lanes):
    wide = lanes.astype(f32)
    return wide[:, 0:1] + wide[:, 1:2]


def join_kernel(kind, depth, with_energy, *refs):
    refs = list(refs)
    e_ref = refs.pop(0) if with_energy else None
    term_ref = refs.pop(0)
    outs = refs[-2:]
    got = refs[:-2]
    rows = term_ref.shape[0] // 2
    h = rows // 2
    sides = [slice(0, h), slice(h, rows)]
    main, tail = slice(0, depth), slice(depth, depth + 128)
    for j in range(2):
        mine, other = sides[j], sides[1 - j]
        out = outs[j]
        base = j * rows
        if kind == "second":
            own = slice(base + mine.start, base + mine.stop)
            rest = slice(base + other.start, base + other.stop)
            out[mine, main] = (term_ref[own] + got[j][:, main].astype(f32)).astype(bf16)
            out[other, main] = term_ref[rest].astype(bf16)
            if with_energy:
                out[mine, tail] = energy_lanes(e_ref[mine] + energy_of(got[j][:, tail]))
                out[other, tail] = energy_lanes(e_ref[other])
        else:
            whole = slice(base, base + rows)
            out[:, main] = (term_ref[whole] + got[j][:, main].astype(f32)).astype(bf16)
            if with_energy:
                out[:, tail] = energy_lanes(e_ref[...] + energy_of(got[j][:, tail]))


def join(kind, rows, depth, energy, terms, got):
    wide = depth + (0 if energy is None else 128)
    operands = ([] if energy is None else [energy]) + [terms] + got
    return pl.pallas_call(
        functools.partial(join_kernel, kind, depth, energy is not None),
        out_shape=[jax.ShapeDtypeStruct((rows, wide), bf16)] * 2,
        compiler_params=pltpu.CompilerParams(vmem_limit_bytes=12 << 20),
        cost_estimate=pl.CostEstimate(flops=0, bytes_accessed=rows * wide * 8, transcendentals=0),
        name="join",
    )(*operands)


def term_kernel(info, lhs_ref, w_ref, o_ref):
    o_ref[...] = jnp.dot(lhs_ref[...], w_ref[...], preferred_element_type=f32)


def terms_of(info, offsets, lhs, weight, depth):
    rows = lhs.shape[0]
    return pl.pallas_call(
        term_kernel,
        grid_spec=pltpu.PrefetchScalarGridSpec(
            num_scalar_prefetch=1,
            grid=(len(offsets), 1),
            in_specs=[
                fixed_block(lhs.shape),
                pl.BlockSpec((weight.shape[0], depth), column_block(offsets, 1)),
            ],
            out_specs=pl.BlockSpec((rows, depth), lambda j, c, info: (j, 0)),
        ),
        out_shape=jax.ShapeDtypeStruct((len(offsets) * rows, depth), f32),
        compiler_params=pltpu.CompilerParams(vmem_limit_bytes=46 << 20),
        cost_estimate=pl.CostEstimate(
            flops=len(offsets) * 2 * rows * depth * weight.shape[0],
            bytes_accessed=len(offsets) * depth * weight.shape[0] * 2,
            transcendentals=0,
        ),
        name="terms",
    )(info, lhs, weight)


def tile_of(depth):
    return min(1024, depth)


def column_block(offsets, steps):
    def at(j, c, info, *more):
        device = info[offsets[0]]
        for b in range(1, len(offsets)):
            device = jnp.where(j == b, info[offsets[b]], device)
        return (0, device * steps + c)

    return at


def fixed_block(shape):
    return pl.BlockSpec(shape, lambda j, c, *s: (0,) * len(shape))


def ring_sum(ring, info, a, b, lhs, weight, depth, energy=None, aside=None):
    n, half = ring.n, ring.half
    rows = lhs.shape[0]
    for d in range(half - 1, -1, -1):
        lhs, a, b = lax.optimization_barrier((lhs, a, b))
        a, b = ring.right(a), ring.left(b)
        terms = terms_of(info, [d, n - d] if d > 0 else [0], lhs, weight, depth)
        if d == max(half - 2, 0) and aside is not None:
            terms, a, b, aside = lax.optimization_barrier((terms, a, b, aside))
        else:
            terms, a, b = lax.optimization_barrier((terms, a, b))
        if d > 0:
            kind = "second" if d == half - 1 else "later"
            a, b = join(kind, rows, depth, energy, terms, [a, b])
    return terms, ([a, b] if half > 1 else [jnp.concatenate([a, b], axis=0)]), aside


def mixer_kernel(arrived, tenants, inner_size, info, adapter, term_ref, *refs):
    got = refs[:arrived]
    e_ref, tok_ref, gain_ref = refs[arrived : arrived + 3]
    downs = refs[arrived + 3 : arrived + 3 + tenants]
    first_ref, message_ref = refs[-2:]
    rows, depth = term_ref.shape
    length = rows // tenants
    tail = slice(depth, depth + 128)
    energy = e_ref[...]
    total = term_ref[...]
    for g in got:
        energy = energy + energy_of(g[:, tail])
        total = total + g[:, :depth].astype(f32)
    scale = lax.rsqrt(energy / inner_size + epsilon)
    first = (tok_ref[...].astype(f32) + total * scale).astype(bf16)
    wide = first.astype(f32)
    high, low = split(jnp.sum(wide * wide, axis=1, keepdims=True))
    first_ref[...] = first
    attn = (wide * gain_ref[...]).astype(bf16)
    message_ref[:, :depth] = attn
    rank = downs[0].shape[1]
    parts = []
    for i in range(tenants):
        x = attn[i * length : (i + 1) * length]
        parts.append(
            lax.dot_general(x, downs[i][0], (((1,), (1,)), ((), ())), preferred_element_type=f32)
        )
    small = jnp.concatenate(parts, axis=0).astype(bf16)
    message_ref[:, tail] = lanes_of([(rank, high), (rank + 1, low)], rows)
    message_ref[:, depth : depth + rank] = small


def mixer_step(info, adapter, terms, got, energy, own_tokens, gain, down, inner_size):
    rows, depth = terms.shape
    tenants = adapter.shape[0]
    operands = [terms, *got, energy, own_tokens, gain] + [down] * tenants

    def whole(a):
        return pl.BlockSpec(a.shape, lambda j, *s: (0,) * a.ndim)

    in_specs = [whole(a) for a in operands]
    in_specs[3 + len(got)] = pl.BlockSpec(
        (1, depth), lambda j, info, adapter: (0, info[info.shape[0] - 2])
    )
    for i in range(tenants):
        in_specs[4 + len(got) + i] = pl.BlockSpec(
            (1, *down.shape[1:]), functools.partial(lambda i, j, info, adapter: (adapter[i], 0, 0), i)
        )
    shapes = [jax.ShapeDtypeStruct((rows, depth), bf16), jax.ShapeDtypeStruct((rows, depth + 128), bf16)]
    return pl.pallas_call(
        functools.partial(mixer_kernel, len(got), tenants, inner_size),
        grid_spec=pltpu.PrefetchScalarGridSpec(
            num_scalar_prefetch=2,
            grid=(1,),
            in_specs=in_specs,
            out_specs=[whole(s) for s in shapes],
        ),
        out_shape=shapes,
        compiler_params=pltpu.CompilerParams(vmem_limit_bytes=16 << 20),
        cost_estimate=pl.CostEstimate(
            flops=2 * rows * depth * 64, bytes_accessed=rows * depth * 16, transcendentals=0
        ),
        name="mixer_step",
    )(info, adapter, *operands)


def query_kernel(offsets, count, first_call, info, *refs):
    blocks = refs[:count]
    w_ref = refs[count]
    q_ref, l_ref = refs[-2:]
    j, k = pl.program_id(0), pl.program_id(1)
    kb = w_ref.shape[0]
    steps = pl.num_programs(1)
    depth = blocks[0].shape[1] - 128

    @pl.when((j == 0) & (k == 0))
    def _():
        if first_call:
            q_ref[...] = jnp.zeros_like(q_ref)
            l_ref[...] = jnp.zeros_like(l_ref)
        else:
            q_ref[...] = refs[count + 1][...]
            l_ref[...] = refs[count + 2][...]

    for b in range(len(offsets)):
        for kk in range(depth // kb):

            @pl.when((j == b) & (k == kk))
            def _():
                pieces = [blocks[b]] if count == len(offsets) else blocks
                base = 0
                for block in pieces:
                    at = slice(base, base + block.shape[0])
                    q_ref[at] += jnp.dot(
                        block[:, kk * kb : (kk + 1) * kb], w_ref[...], preferred_element_type=f32
                    )
                    if kk == 0:
                        l_ref[at] += block[:, depth:].astype(f32)
                    base += block.shape[0]


def query_step(info, offsets, blocks, weight, depth, accs):
    count = len(blocks)
    rows = sum(b.shape[0] for b in blocks) // len(offsets)
    cols = weight.shape[1]
    kb = tile_of(depth)
    steps = depth // kb

    def row_block(j, k, info):
        at = info[offsets[0]]
        for b in range(1, len(offsets)):
            at = jnp.where(j == b, info[offsets[b]], at)
        return (at * steps + k, 0)

    shapes = [(rows, cols), (rows, 128)]
    in_specs = [fixed_block(b.shape) for b in blocks] + [pl.BlockSpec((kb, cols), row_block)]
    operands = [info, *blocks, weight]
    aliases = {}
    if accs is not None:
        in_specs += [fixed_block(s) for s in shapes]
        aliases = {len(operands): 0, len(operands) + 1: 1}
        operands += accs
    return pl.pallas_call(
        functools.partial(query_kernel, offsets, count, accs is None),
        grid_spec=pltpu.PrefetchScalarGridSpec(
            num_scalar_prefetch=1,
            grid=(len(offsets), steps),
            in_specs=in_specs,
            out_specs=[fixed_block(s) for s in shapes],
        ),
        out_shape=[jax.ShapeDtypeStruct(s, f32) for s in shapes],
        input_output_aliases=aliases,
        compiler_params=pltpu.CompilerParams(vmem_limit_bytes=46 << 20),
        cost_estimate=pl.CostEstimate(
            flops=len(offsets) * 2 * rows * depth * cols,
            bytes_accessed=len(offsets) * depth * cols * 2,
            transcendentals=0,
        ),
        name="query_step",
    )(*operands)


def shifted(history, x, k):
    if k == 3:
        return x
    return jnp.concatenate([history[k:3], x[: x.shape[0] - 3 + k]], axis=0)


def conv_silu(history, x, taps):
    total = taps[0:1] * shifted(history, x, 0)
    for k in range(1, 4):
        total = total + taps[k : k + 1] * shifted(history, x, k)
    return total * jax.nn.sigmoid(total)


def spans(heads, width):
    lane = lax.broadcasted_iota(jnp.int32, (heads, heads * width), 1)
    row = lax.broadcasted_iota(jnp.int32, (heads, heads * width), 0)
    return jnp.where(lane // width == row, 1.0, 0.0).astype(f32)


def far_columns(info, half, w_ref, held, arrived):
    depth = held.shape[1]
    at = pl.multiple_of(info[half] * depth, 128)
    return pltpu.make_async_copy(w_ref.at[:, pl.ds(at, depth)], held, arrived)


def first_messages(lhs_ref, held, energy_ref, left_ref, right_ref):
    term = jnp.dot(lhs_ref[...], held[...], preferred_element_type=f32)
    h, depth = left_ref.shape[0], held.shape[1]
    for j, out in enumerate((left_ref, right_ref)):
        side = slice(j * h, (j + 1) * h)
        out[:, :depth] = term[side].astype(bf16)
        if energy_ref is not None:
            out[:, depth : depth + 128] = energy_lanes(energy_ref[side])


def state_kernel(
    slot,
    info,
    x_ref,
    z_ref,
    kept_ref,
    came_ref,
    w_ref,
    hx_ref,
    hbc_ref,
    tx_ref,
    tbc_ref,
    bias_ref,
    rate_ref,
    skip_ref,
    gain_ref,
    own_ref,
    far_ref,
    gated_ref,
    energy_ref,
    final_ref,
    left_ref,
    right_ref,
    initial,
    held,
    arrived,
    *,
    slots,
    half,
):
    i = pl.program_id(0)
    count = info.shape[0]
    copy = far_columns(info, half, w_ref, held, arrived)

    @pl.when(i == 0)
    def _():
        copy.start()

    is_own = slot[i] // slots == info[count - 1]

    @pl.when(is_own)
    def _():
        initial[...] = own_ref[0]

    @pl.when(jnp.logical_not(is_own))
    def _():
        initial[...] = far_ref[0]

    length = x_ref.shape[0]
    heads = bias_ref.shape[1]
    values = conv_silu(hx_ref[0], x_ref[...].astype(bf16).astype(f32), tx_ref[...])
    shared = i // (pl.num_programs(0) // 2) == lax.rem(info[count - 2], 2)
    projected = jnp.where(shared, kept_ref[...], came_ref[...].astype(f32))
    bc = conv_silu(hbc_ref[0], projected[:, : 2 * STATE], tbc_ref[...])
    all_raw = projected[:, 2 * STATE :]
    pick = (all_raw.shape[1], heads)
    chosen = lax.broadcasted_iota(jnp.int32, pick, 0) == (
        lax.broadcasted_iota(jnp.int32, pick, 1) + info[count - 2] * heads
    )
    chosen = jnp.where(chosen, 1.0, 0.0).astype(f32)
    in_state = bc[:, :STATE].astype(bf16)
    out_state = bc[:, STATE:].astype(bf16)
    raw = jnp.dot(all_raw, chosen, precision=highest, preferred_element_type=f32) + bias_ref[...]
    steps = jnp.maximum(raw, 0.0) + jnp.log1p(jnp.exp(-jnp.abs(raw)))
    log_decay = -steps * jnp.exp(rate_ref[...])
    row = lax.broadcasted_iota(jnp.int32, (length, length), 0)
    col = lax.broadcasted_iota(jnp.int32, (length, length), 1)
    lower = jnp.where(row >= col, 1.0, 0.0).astype(f32)
    running = jnp.dot(lower, log_decay, precision=highest, preferred_element_type=f32)
    last = running[length - 1 : length]

    wide = spans(heads, length)
    both = jnp.dot(
        jnp.concatenate([running, steps], axis=0), wide, precision=highest, preferred_element_type=f32
    )
    run_t, step_t = both[:length], both[length:]
    lane = lax.broadcasted_iota(jnp.int32, (length, heads * length), 1) % length
    place = lax.broadcasted_iota(jnp.int32, (length, heads * length), 0)
    diagonal = lane == place
    run_s = jnp.sum(jnp.where(diagonal, run_t, 0.0), axis=0, keepdims=True)
    step_s = jnp.sum(jnp.where(diagonal, step_t, 0.0), axis=0, keepdims=True)
    seen = place >= lane
    decays = jnp.where(seen, jnp.exp(jnp.where(seen, run_t - run_s, 0.0)), 0.0)
    overlap = lax.dot_general(
        out_state,
        jnp.concatenate([in_state] * heads, axis=0),
        (((1,), (1,)), ((), ())),
        preferred_element_type=f32,
    )
    mixing = (overlap * decays * step_s).astype(bf16)
    short = values.astype(bf16)
    group = min(4, heads)
    gl, gw = group * length, group * HDIM
    own_block = (
        lax.broadcasted_iota(jnp.int32, (gl, gw), 0) // length
        == lax.broadcasted_iota(jnp.int32, (gl, gw), 1) // HDIM
    )
    within = []
    for g in range(heads // group):
        v = jnp.concatenate([values[:, g * gw : (g + 1) * gw]] * group, axis=0)
        v = jnp.where(own_block, v, 0.0).astype(bf16)
        within.append(jnp.dot(mixing[:, g * gl : (g + 1) * gl], v, preferred_element_type=f32))
    within = within[0] if len(within) == 1 else jnp.concatenate(within, axis=1)

    narrow = spans(heads, HDIM)
    scales = jnp.dot(
        jnp.concatenate(
            [
                jnp.exp(running),
                jnp.exp(last - running) * steps,
                jnp.broadcast_to(skip_ref[...], (8, heads)),
            ],
            axis=0,
        ),
        narrow,
        precision=highest,
        preferred_element_type=f32,
    )
    start = initial[...]
    carried = lax.dot_general(
        out_state, start.astype(bf16), (((1,), (1,)), ((), ())), preferred_element_type=f32
    )
    result = within + carried * scales[:length] + scales[2 * length : 2 * length + 1] * values
    z = z_ref[...].astype(bf16).astype(f32)
    gated = result * (z * jax.nn.sigmoid(z))
    at = pl.ds(pl.multiple_of(i * length, length), length)
    energy_ref[at, :] = jnp.sum(gated * gated, axis=1, keepdims=True)
    gated_ref[at, :] = (gated * gain_ref[...]).astype(bf16)

    kept = jnp.exp(
        lax.dot_general(
            log_decay,
            jnp.ones((length, STATE), f32),
            (((0,), (0,)), ((), ())),
            precision=highest,
            preferred_element_type=f32,
        )
    )
    update = lax.dot_general(
        (values * scales[length : 2 * length]).astype(bf16),
        in_state,
        (((0,), (0,)), ((), ())),
        preferred_element_type=f32,
    )
    for h in range(heads):
        at = slice(h * HDIM, (h + 1) * HDIM)
        final_ref[0, at, :] = update[at] + start[at] * kept[h : h + 1]

    @pl.when(i == pl.num_programs(0) - 1)
    def _():
        copy.wait()
        first_messages(gated_ref, held, energy_ref, left_ref, right_ref)


def state_pass(
    half, info, slot, inner, kept, came, weight, hx, hbc, tx, tbc, bias, rate, skip, gain, own_pool, far_pool
):
    tenants = slot.shape[0]
    length = inner.shape[0] // 2 // tenants
    cols = inner.shape[1]
    slots = own_pool.shape[0]

    def rows(width):
        return pl.BlockSpec((length, width), lambda i, *s: (i, 0))

    def whole(a):
        return pl.BlockSpec(a.shape, lambda i, *s: (0,) * a.ndim)

    def own_slot(i, slot, info):
        return (jnp.clip(slot[i] - info[info.shape[0] - 1] * slots, 0, slots - 1), 0, 0)

    def far_slot(i, slot, info):
        return (jnp.clip(slot[i] - (1 - info[info.shape[0] - 1]) * slots, 0, slots - 1), 0, 0)

    pooled = (1, cols, STATE)
    message = (tenants * length // 2, weight.shape[1] // (2 * half) + 128)

    def fixed(shape):
        return pl.BlockSpec(shape, lambda i, *s: (0, 0))

    return pl.pallas_call(
        functools.partial(state_kernel, slots=slots, half=half),
        grid_spec=pltpu.PrefetchScalarGridSpec(
            num_scalar_prefetch=2,
            grid=(tenants,),
            in_specs=[
                rows(cols),
                pl.BlockSpec((length, cols), lambda i, *s: (tenants + i, 0)),
                pl.BlockSpec((length, kept.shape[1]), lambda i, *s: (i % (tenants // 2), 0)),
                pl.BlockSpec((length, kept.shape[1]), lambda i, *s: (i % (tenants // 2), 0)),
                pl.BlockSpec(memory_space=pl.ANY),
                pl.BlockSpec((1, 3, cols), lambda i, *s: (i, 0, 0)),
                pl.BlockSpec((1, 3, 2 * STATE), lambda i, *s: (i, 0, 0)),
                whole(tx),
                whole(tbc),
                whole(bias),
                whole(rate),
                whole(skip),
                whole(gain),
                pl.BlockSpec(pooled, own_slot),
                pl.BlockSpec(pooled, far_slot),
            ],
            out_specs=[
                fixed((tenants * length, cols)),
                fixed((tenants * length, 1)),
                pl.BlockSpec(pooled, lambda i, *s: (i, 0, 0)),
                fixed(message),
                fixed(message),
            ],
            scratch_shapes=[
                pltpu.VMEM((cols, STATE), f32),
                pltpu.VMEM((weight.shape[0], message[1] - 128), bf16),
                pltpu.SemaphoreType.DMA,
            ],
        ),
        out_shape=[
            jax.ShapeDtypeStruct((tenants * length, cols), bf16),
            jax.ShapeDtypeStruct((tenants * length, 1), f32),
            jax.ShapeDtypeStruct((tenants, cols, STATE), f32),
            jax.ShapeDtypeStruct(message, bf16),
            jax.ShapeDtypeStruct(message, bf16),
        ],
        compiler_params=pltpu.CompilerParams(vmem_limit_bytes=48 << 20),
        cost_estimate=pl.CostEstimate(
            flops=tenants * 6 * length * cols * STATE,
            bytes_accessed=tenants * cols * STATE * 10,
            transcendentals=0,
        ),
        name="state_pass",
    )(slot, info, inner, inner, kept, came, weight, hx, hbc, tx, tbc, bias, rate, skip, gain, own_pool, far_pool)


def attend_kernel(
    half, width, table, limit, adapter, info, q_ref, low_ref, up_ref, near_ref, far_ref, w_ref, *refs
):
    o_ref, left_ref, right_ref, held, arrived = refs[-5:]
    copy = far_columns(info, half, w_ref, held, arrived)

    @pl.when(pl.program_id(0) == 0)
    def _():
        copy.start()

    i = pl.program_id(0)
    length = q_ref.shape[0]
    heads = q_ref.shape[1] // HEAD_SIZE
    blocks = table.shape[1]
    part = near_ref.shape[1]
    core = info[info.shape[0] - 1]
    rank = up_ref.shape[1]
    square = low_ref[:, rank : rank + 1] + low_ref[:, rank + 1 : rank + 2]
    norm = lax.rsqrt(square / width + epsilon)
    low = (low_ref[:, :rank] * norm).astype(bf16)
    raised = jnp.dot(low, up_ref[0], preferred_element_type=f32)
    q = (q_ref[...] * norm + adapter_scale * raised).astype(bf16)
    q = jnp.concatenate([q[:, h * HEAD_SIZE : (h + 1) * HEAD_SIZE] for h in range(heads)], axis=0)
    fresh = jnp.concatenate([refs[0][...], refs[1][...]], axis=1)
    for came in refs[2:-5]:
        fresh = fresh + came[...].astype(f32)
    fresh = (fresh * norm).astype(bf16)
    pieces = []
    for j in range(blocks):
        at = table[i, j]
        pieces += [near_ref[at], far_ref[at]]
    cached = jnp.concatenate(pieces, axis=0)
    context = cached.shape[0]
    nt = (((1,), (1,)), ((), ()))
    scale = HEAD_SIZE ** (-0.5)
    old = lax.dot_general(q, cached[:, :HEAD_SIZE], nt, preferred_element_type=f32) * scale
    new = lax.dot_general(q, fresh[:, :HEAD_SIZE], nt, preferred_element_type=f32) * scale
    lane = lax.broadcasted_iota(jnp.int32, old.shape, 1)
    inside = lane % (2 * part)
    far_side = jnp.where(inside >= part, 1, 0)
    half = jnp.where(core == 0, far_side, 1 - far_side)
    place = (lane // (2 * part)) * (2 * part) + half * part + inside % part
    old_seen = place < limit[i]
    token = lax.broadcasted_iota(jnp.int32, new.shape, 0) % length
    new_seen = lax.broadcasted_iota(jnp.int32, new.shape, 1) <= token
    old = jnp.where(old_seen, old, -jnp.inf)
    new = jnp.where(new_seen, new, -jnp.inf)
    top = jnp.maximum(jnp.max(old, axis=1, keepdims=True), jnp.max(new, axis=1, keepdims=True))
    old = jnp.where(old_seen, jnp.exp(old - top), 0.0)
    new = jnp.where(new_seen, jnp.exp(new - top), 0.0)
    share = 1.0 / (jnp.sum(old, axis=1, keepdims=True) + jnp.sum(new, axis=1, keepdims=True))
    out = jnp.dot((old * share).astype(bf16), cached[:, HEAD_SIZE:], preferred_element_type=f32)
    out += jnp.dot((new * share).astype(bf16), fresh[:, HEAD_SIZE:], preferred_element_type=f32)
    out = out.astype(bf16)
    own_rows = pl.ds(pl.multiple_of(i * length, length), length)
    for h in range(heads):
        o_ref[own_rows, h * HEAD_SIZE : (h + 1) * HEAD_SIZE] = out[h * length : (h + 1) * length]

    @pl.when(i == pl.num_programs(0) - 1)
    def _():
        copy.wait()
        first_messages(o_ref, held, None, left_ref, right_ref)


def attend(ring, width, table, limit, adapter, info, q, low, up, near, far, weight, kv, came):
    tenants = table.shape[0]
    length = q.shape[0] // tenants

    def rows(a):
        return pl.BlockSpec((length, a.shape[1]), lambda i, *s: (i, 0))

    def whole(a):
        return pl.BlockSpec(a.shape, lambda i, *s: (0,) * a.ndim)

    message = (q.shape[0] // 2, weight.shape[1] // ring.n)

    def fixed(shape):
        return pl.BlockSpec(shape, lambda i, *s: (0, 0))

    def own(base):
        return pl.BlockSpec(
            (length, HEAD_SIZE), lambda i, t, n, a, info: (i, base + info[ring.n])
        )

    return pl.pallas_call(
        functools.partial(attend_kernel, ring.half, width),
        grid_spec=pltpu.PrefetchScalarGridSpec(
            num_scalar_prefetch=4,
            grid=(tenants,),
            in_specs=[
                rows(q),
                rows(low),
                pl.BlockSpec((1, *up.shape[1:]), lambda i, t, n, a, info: (a[i], 0, 0)),
                whole(near),
                whole(far),
                pl.BlockSpec(memory_space=pl.ANY),
                own(0),
                own(KEY_HEADS),
            ]
            + [rows(a) for a in came],
            out_specs=[fixed(q.shape), fixed(message), fixed(message)],
            scratch_shapes=[
                pltpu.VMEM((weight.shape[0], message[1]), bf16),
                pltpu.SemaphoreType.DMA,
            ],
        ),
        out_shape=[
            jax.ShapeDtypeStruct(q.shape, bf16),
            jax.ShapeDtypeStruct(message, bf16),
            jax.ShapeDtypeStruct(message, bf16),
        ],
        compiler_params=pltpu.CompilerParams(vmem_limit_bytes=46 << 20),
        cost_estimate=pl.CostEstimate(
            flops=tenants * 4 * length * q.shape[1] * 288,
            bytes_accessed=near.size * 4 + q.size * 6 + up.size,
            transcendentals=0,
        ),
        name="attend",
    )(table, limit, adapter, info, q, low, up, near, far, weight, kv, kv, *came)


def pick_kernel(heads, info, pool_ref, o_ref):
    for d, head in enumerate(heads):
        for k in range(2):
            at = (head + k * KEY_HEADS) * HEAD_SIZE
            o_ref[d, :, :, k * HEAD_SIZE : (k + 1) * HEAD_SIZE] = pool_ref[:, :, at : at + HEAD_SIZE]


def pick_heads(info, pool, heads, pools):
    count, block_len, wide = pool.shape
    part = block_len // pools
    shape = (len(heads), count, part, 2 * HEAD_SIZE)
    return pl.pallas_call(
        functools.partial(pick_kernel, heads),
        grid_spec=pltpu.PrefetchScalarGridSpec(
            num_scalar_prefetch=1,
            grid=(1,),
            in_specs=[pl.BlockSpec((count, part, wide), lambda j, info: (0, info[info.shape[0] - 1], 0))],
            out_specs=pl.BlockSpec(shape, lambda j, info: (0, 0, 0, 0)),
        ),
        out_shape=jax.ShapeDtypeStruct(shape, bf16),
        compiler_params=pltpu.CompilerParams(vmem_limit_bytes=8 << 20),
        name="pick_heads",
    )(info, pool)


def fresh_kernel(kind, offsets, heads_at, info, kv_ref, *refs):
    outs = refs[-2:]
    got = refs[:-2]
    rows = kv_ref.shape[0]
    h = rows // 2
    sides = [slice(0, h), slice(h, rows)]
    for j in range(2):
        offset = offsets[0] if kind == "first" else offsets[j]
        head = info[heads_at + offset]
        for k in range(2):
            at = pl.ds(pl.multiple_of((head + k * KEY_HEADS) * HEAD_SIZE, HEAD_SIZE), HEAD_SIZE)
            to = slice(k * HEAD_SIZE, (k + 1) * HEAD_SIZE)
            if kind == "first":
                outs[j][:, to] = kv_ref[sides[j], at].astype(bf16)
            elif kind == "second":
                mine, other = sides[j], sides[1 - j]
                outs[j][mine, to] = (kv_ref[mine, at] + got[j][:, to].astype(f32)).astype(bf16)
                outs[j][other, to] = kv_ref[other, at].astype(bf16)
            else:
                outs[j][:, to] = (kv_ref[:, at] + got[j][:, to].astype(f32)).astype(bf16)


def fresh_join(info, kind, offsets, heads_at, kv, got):
    rows = kv.shape[0]
    shape = (rows // 2 if kind == "first" else rows, 2 * HEAD_SIZE)
    operands = [kv, *got]
    return pl.pallas_call(
        functools.partial(fresh_kernel, kind, offsets, heads_at),
        grid_spec=pltpu.PrefetchScalarGridSpec(
            num_scalar_prefetch=1,
            grid=(1,),
            in_specs=[pl.BlockSpec(a.shape, lambda j, info: (0, 0)) for a in operands],
            out_specs=[pl.BlockSpec(shape, lambda j, info: (0, 0))] * 2,
        ),
        out_shape=[jax.ShapeDtypeStruct(shape, bf16)] * 2,
        compiler_params=pltpu.CompilerParams(vmem_limit_bytes=8 << 20),
        name="fresh_join",
    )(info, *operands)


def per_device(
    ring,
    tokens,
    mamba_in_weight,
    state_projection,
    inner_taps,
    state_taps,
    inner_history,
    state_history,
    step_size_bias,
    log_decay_rate,
    skip_factor,
    gated_norm_gain,
    mamba_out_weight,
    saved_state_pool,
    tenant_state_slot,
    attention_gain,
    query_matrix,
    adapter_down,
    adapter_up,
    tenant_adapter,
    key_value_weight,
    key_value_pool,
    tenant_blocks,
    cached_length,
    attention_out_weight,
):
    n, half, pools = ring.n, ring.half, ring.pools
    tenants, length, depth = tokens.shape
    rows = tenants * length
    width = depth * n
    info = ring.info()
    own_tokens = tokens.reshape(rows, depth)
    heads = step_size_bias.shape[0]
    cols = mamba_in_weight.shape[2]
    swap = [(i, (i + 1) % pools) for i in range(pools)]

    slots = saved_state_pool.shape[0]
    flat_pool = saved_state_pool.reshape(slots, heads * HDIM, STATE)
    far_pool = lax.ppermute(flat_pool, "pool", swap)

    inner, kept, came, cache = ring.gather(
        own_tokens,
        lambda offsets, blocks, acc: in_product(info, offsets, blocks, mamba_in_weight, depth, acc),
        lambda x: partial_product(info, x, state_projection),
        pick_heads(info, key_value_pool, ring.heads, pools),
    )
    cache = cache.reshape(-1, *cache.shape[2:])

    gated, energy, final_state, a, b = state_pass(
        half,
        info,
        tenant_state_slot,
        inner,
        kept,
        came,
        mamba_out_weight,
        inner_history.astype(f32),
        state_history,
        inner_taps.astype(f32),
        state_taps.astype(f32),
        step_size_bias[None],
        log_decay_rate[None],
        skip_factor[None],
        gated_norm_gain[None],
        flat_pool,
        far_pool,
    )
    a, b, cache = lax.optimization_barrier((a, b, cache))
    far_cache = lax.ppermute(cache, "pool", swap)
    terms, got, far_cache = ring_sum(ring, info, a, b, gated, mamba_out_weight, depth, energy, far_cache)
    first, message = mixer_step(
        info,
        tenant_adapter,
        terms,
        got,
        energy,
        own_tokens,
        attention_gain[None],
        adapter_down.transpose(0, 2, 1),
        cols * n,
    )

    kv = jnp.dot(message[:, :depth], key_value_weight, preferred_element_type=f32)

    h = rows // 2
    a, b = message, message
    ka, kb = fresh_join(info, "first", [half], n, kv, [])
    accs, ready = None, ([0], [message])
    for s in range(1, half + 1):
        if s == half:
            a, b = a[:h], b[h:]
        a, b, ka, kb = ring.right(a), ring.left(b), ring.right(ka), ring.left(kb)
        accs = query_step(info, *ready, query_matrix, depth, accs)
        a, b, ka, kb, accs = lax.optimization_barrier((a, b, ka, kb, accs))
        ready = ([n - s, s], [a, b]) if s < half else ([half], [a, b])
        if s < half:
            kind = "second" if s == 1 else "later"
            ka, kb = fresh_join(info, kind, [half - s, n - half + s], n, kv, [ka, kb])
    kv_came = [ka, kb] if half > 1 else [jnp.concatenate([ka, kb], axis=0)]
    query, low = query_step(info, *ready, query_matrix, depth, accs)
    heads_out, a, b = attend(
        ring,
        width,
        tenant_blocks,
        cached_length,
        tenant_adapter,
        info,
        query,
        low,
        adapter_up,
        cache,
        far_cache,
        attention_out_weight,
        kv,
        kv_came,
    )
    terms, got, _ = ring_sum(ring, info, a, b, heads_out, attention_out_weight, depth)
    second = terms + first.astype(f32)
    for g in got:
        second = second + g.astype(f32)
    second = second.astype(bf16)
    return (
        second.reshape(tenants, length, depth),
        final_state.reshape(tenants, heads, HDIM, STATE),
    )


def solution(mesh):
    in_specs = (
        P(("groups", "pool"), None, "tensor"),
        P(None, None, "tensor"),
        P("tensor", None),
        P(None, "tensor"),
        P(),
        P(("groups", "pool"), None, "tensor"),
        P(("groups", "pool"), None, None),
        P("tensor"),
        P("tensor"),
        P("tensor"),
        P("tensor"),
        P("tensor", None),
        P(("groups", "pool"), "tensor", None, None),
        P(("groups", "pool")),
        P(),
        P(None, "tensor"),
        P(None, "tensor", None),
        P(None, None, "tensor"),
        P(("groups", "pool")),
        P("tensor", None),
        P(("groups", "tensor"), None, None),
        P(("groups", "pool"), None),
        P(("groups", "pool")),
        P("tensor", None),
    )
    out_specs = (P(("groups", "pool"), None, "tensor"), P(("groups", "pool"), "tensor", None, None))
    ring = Ring(mesh.shape["tensor"], mesh.shape["pool"])
    return jax.shard_map(
        functools.partial(per_device, ring),
        mesh=mesh,
        in_specs=in_specs,
        out_specs=out_specs,
        check_vma=False,
    )
```

```python
import functools

import jax
import jax.numpy as jnp
from jax import lax
from jax.experimental import pallas as pl
from jax.experimental.pallas import tpu as pltpu
from jax.sharding import PartitionSpec as P

HDIM = 64
STATE = 256
QUERY_HEADS = 64
KEY_HEADS = 8
HEAD_SIZE = 128

epsilon = 1e-05
adapter_scale = 2.0
highest = lax.Precision.HIGHEST
f32 = jnp.float32
bf16 = jnp.bfloat16


def ring_order(n):
    cols = 1
    for c in range(2, n):
        if n % c == 0 and (n // c) % 2 == 0 and c <= n // c:
            cols = c
    if cols == 1:
        return list(range(n))
    rows = n // cols
    order = [r * cols for r in range(rows)]
    for k, r in enumerate(reversed(range(rows))):
        across = list(range(1, cols))
        order += [r * cols + c for c in (across if k % 2 == 0 else across[::-1])]
    return order


class Ring:
    def __init__(self, n, pools):
        self.n = n
        heads = [d * QUERY_HEADS // n // (QUERY_HEADS // KEY_HEADS) for d in range(n)]
        self.half = n // 2
        self.pools = pools
        order = ring_order(n)
        place = {d: i for i, d in enumerate(order)}
        self.table = [
            [order[(place[d] + s) % n] for s in range(n)]
            + [heads[order[(place[d] + s) % n]] for s in range(n)]
            + [d, c]
            for d in range(n)
            for c in range(pools)
        ]
        self.heads = heads
        self.cw = [(order[i], order[(i + 1) % n]) for i in range(n)]
        self.ccw = [(order[i], order[(i - 1) % n]) for i in range(n)]

    def info(self):
        at = lax.axis_index("tensor") * self.pools + lax.axis_index("pool")
        return lax.dynamic_slice_in_dim(jnp.array(self.table, jnp.int32), at, 1, 0)[0]

    def right(self, x):
        return lax.ppermute(x, "tensor", self.cw)

    def left(self, x):
        return lax.ppermute(x, "tensor", self.ccw)

    def masks(self):
        found, m = [], 1
        while m < self.n:
            found.append([(i, i ^ m) for i in range(self.n)])
            m *= 2
        return found

    def gather(self, x, weigh, project, aside):
        n, half = self.n, self.half
        h = x.shape[0] // 2
        pairs = self.masks()
        exchange = pairs + pairs[:1]
        sums, ready = None, ([0], [x])
        a = b = x
        for s in range(1, max(half, len(exchange)) + 1):
            if s == half:
                a, b = a[:h], b[h:]
            if s <= half:
                a, b = self.right(a), self.left(b)
            if s == 1:
                sums = weigh(*ready, sums)
                x, sums = lax.optimization_barrier((x, sums))
                keep, give = project(x)
            if s <= len(exchange):
                came = lax.ppermute(give, "tensor", exchange[s - 1])
            if 1 < s <= half:
                sums = weigh(*ready, sums)
            if s <= len(exchange):
                a, b, sums, came = lax.optimization_barrier((a, b, sums, came))
            else:
                a, b, sums = lax.optimization_barrier((a, b, sums))
            if s < len(exchange):
                keep = keep + came.astype(f32)
                give = keep.astype(bf16)
            if s <= half:
                ready = ([n - s, s], [a, b]) if s < half else ([half], [a, b])
        x, aside, sums = lax.optimization_barrier((ready[1], aside, sums))
        aside = lax.all_to_all(aside, "tensor", 0, 0, tiled=True)
        return weigh(ready[0], x, sums), keep, came, aside


def split(x):
    high = x.astype(bf16)
    return high, (x - high.astype(f32)).astype(bf16)


def partial_kernel(info, x_ref, w_ref, keep_ref, give_ref, whole):
    whole[...] = jnp.dot(x_ref[...], w_ref[...], preferred_element_type=f32)
    h = keep_ref.shape[0]
    odd = lax.rem(info[info.shape[0] - 2], 2)
    keep_ref[...] = whole[pl.ds(pl.multiple_of(odd * h, 8), h), :]
    give_ref[...] = whole[pl.ds(pl.multiple_of((1 - odd) * h, 8), h), :].astype(bf16)


def partial_product(info, x, weight):
    shape = (x.shape[0] // 2, weight.shape[1])
    return pl.pallas_call(
        partial_kernel,
        grid_spec=pltpu.PrefetchScalarGridSpec(
            num_scalar_prefetch=1,
            grid=(1,),
            in_specs=[
                pl.BlockSpec(x.shape, lambda j, info: (0, 0)),
                pl.BlockSpec(weight.shape, lambda j, info: (0, 0)),
            ],
            out_specs=[pl.BlockSpec(shape, lambda j, info: (0, 0))] * 2,
            scratch_shapes=[pltpu.VMEM((x.shape[0], weight.shape[1]), f32)],
        ),
        out_shape=[jax.ShapeDtypeStruct(shape, f32), jax.ShapeDtypeStruct(shape, bf16)],
        compiler_params=pltpu.CompilerParams(vmem_limit_bytes=12 << 20),
        name="partial_product",
    )(info, x, weight)


def in_kernel(offsets, count, chunks, first_call, info, *refs):
    blocks = refs[:count]
    w_ref = refs[count]
    o_ref, spread, held, arrived = refs[-4:]
    depth = held.shape[1] * chunks
    rows = o_ref.shape[0] // 2
    part = depth // chunks
    copies = []
    for b, offset in enumerate(offsets):
        for c in range(chunks):
            at = pl.multiple_of(info[offset] * depth + c * part, part)
            slot = b * chunks + c
            copies.append(
                pltpu.make_async_copy(w_ref.at[pl.ds(at, part)], held.at[slot], arrived.at[slot])
            )
    for copy in copies:
        copy.start()

    lane = lax.broadcasted_iota(jnp.int32, (128, 512), 1)
    sub = lax.broadcasted_iota(jnp.int32, (128, 512), 0)
    target = jnp.where(lane < 256, 2 * sub, 2 * sub + 257)
    widen = jnp.where(lane == target, 1.0, 0.0).astype(bf16)
    for b in range(len(offsets)):
        base = 0
        for block in [blocks[b]] if count == len(offsets) else blocks:
            r = block.shape[0]
            for p in range(depth // 128):
                piece = block[:, p * 128 : (p + 1) * 128]
                both = jnp.dot(piece, widen, preferred_element_type=f32).astype(bf16)
                spread[b, base : base + r, p * 256 : (p + 1) * 256] = both[:, :256]
                spread[b, rows + base : rows + base + r, p * 256 : (p + 1) * 256] = both[:, 256:]
            base += r

    for slot, copy in enumerate(copies):
        b, c = slot // chunks, slot % chunks
        copy.wait()
        w = held[slot].reshape(2 * part, held.shape[3])
        x = spread[b, :, c * 2 * part : (c + 1) * 2 * part]
        term = jnp.dot(x, w, preferred_element_type=f32)
        if slot == 0:
            o_ref[...] = term if first_call else refs[count + 1][...] + term
        else:
            o_ref[...] += term


def in_product(info, offsets, blocks, weight, depth, acc):
    count = len(blocks)
    rows = sum(b.shape[0] for b in blocks) // len(offsets)
    cols = weight.shape[2]
    chunks = 2 if depth % 512 == 0 else 1
    slots = chunks * len(offsets)

    def fixed(shape):
        return pl.BlockSpec(shape, lambda j, info: (0, 0))

    in_specs = [fixed(b.shape) for b in blocks]
    in_specs.append(pl.BlockSpec(memory_space=pl.ANY))
    operands = [info, *blocks, weight]
    aliases = {}
    shape = (2 * rows, cols)
    if acc is not None:
        in_specs.append(fixed(shape))
        aliases = {len(operands): 0}
        operands.append(acc)
    return pl.pallas_call(
        functools.partial(in_kernel, offsets, count, chunks, acc is None),
        grid_spec=pltpu.PrefetchScalarGridSpec(
            num_scalar_prefetch=1,
            grid=(1,),
            in_specs=in_specs,
            out_specs=fixed(shape),
            scratch_shapes=[
                pltpu.VMEM((len(offsets), 2 * rows, 2 * depth), bf16),
                pltpu.VMEM((slots, depth // chunks, 2, cols), bf16),
                pltpu.SemaphoreType.DMA((slots,)),
            ],
        ),
        out_shape=jax.ShapeDtypeStruct(shape, f32),
        input_output_aliases=aliases,
        compiler_params=pltpu.CompilerParams(vmem_limit_bytes=30 << 20),
        cost_estimate=pl.CostEstimate(
            flops=len(offsets) * 8 * rows * depth * cols,
            bytes_accessed=len(offsets) * depth * cols * 8,
            transcendentals=0,
        ),
        name="in_product",
    )(*operands)


def lanes_of(columns, rows):
    lane = lax.broadcasted_iota(jnp.int32, (rows, 128), 1)
    out = jnp.zeros((rows, 128), f32)
    for at, value in columns:
        out = jnp.where(lane == at, value.astype(f32), out)
    return out.astype(bf16)


def energy_lanes(energy):
    high, low = split(energy)
    return lanes_of([(0, high), (1, low)], energy.shape[0])


def energy_of(lanes):
    wide = lanes.astype(f32)
    return wide[:, 0:1] + wide[:, 1:2]


def join_kernel(kind, depth, with_energy, *refs):
    refs = list(refs)
    e_ref = refs.pop(0) if with_energy else None
    term_ref = refs.pop(0)
    outs = refs[-2:]
    got = refs[:-2]
    rows = term_ref.shape[0] // 2
    h = rows // 2
    sides = [slice(0, h), slice(h, rows)]
    main, tail = slice(0, depth), slice(depth, depth + 128)
    for j in range(2):
        mine, other = sides[j], sides[1 - j]
        out = outs[j]
        base = j * rows
        if kind == "second":
            own = slice(base + mine.start, base + mine.stop)
            rest = slice(base + other.start, base + other.stop)
            out[mine, main] = (term_ref[own] + got[j][:, main].astype(f32)).astype(bf16)
            out[other, main] = term_ref[rest].astype(bf16)
            if with_energy:
                out[mine, tail] = energy_lanes(e_ref[mine] + energy_of(got[j][:, tail]))
                out[other, tail] = energy_lanes(e_ref[other])
        else:
            whole = slice(base, base + rows)
            out[:, main] = (term_ref[whole] + got[j][:, main].astype(f32)).astype(bf16)
            if with_energy:
                out[:, tail] = energy_lanes(e_ref[...] + energy_of(got[j][:, tail]))


def join(kind, rows, depth, energy, terms, got):
    wide = depth + (0 if energy is None else 128)
    operands = ([] if energy is None else [energy]) + [terms] + got
    return pl.pallas_call(
        functools.partial(join_kernel, kind, depth, energy is not None),
        out_shape=[jax.ShapeDtypeStruct((rows, wide), bf16)] * 2,
        compiler_params=pltpu.CompilerParams(vmem_limit_bytes=12 << 20),
        cost_estimate=pl.CostEstimate(flops=0, bytes_accessed=rows * wide * 8, transcendentals=0),
        name="join",
    )(*operands)


def term_kernel(info, lhs_ref, w_ref, o_ref):
    o_ref[...] = jnp.dot(lhs_ref[...], w_ref[...], preferred_element_type=f32)


def terms_of(info, offsets, lhs, weight, depth):
    rows = lhs.shape[0]
    return pl.pallas_call(
        term_kernel,
        grid_spec=pltpu.PrefetchScalarGridSpec(
            num_scalar_prefetch=1,
            grid=(len(offsets), 1),
            in_specs=[
                fixed_block(lhs.shape),
                pl.BlockSpec((weight.shape[0], depth), column_block(offsets, 1)),
            ],
            out_specs=pl.BlockSpec((rows, depth), lambda j, c, info: (j, 0)),
        ),
        out_shape=jax.ShapeDtypeStruct((len(offsets) * rows, depth), f32),
        compiler_params=pltpu.CompilerParams(vmem_limit_bytes=46 << 20),
        cost_estimate=pl.CostEstimate(
            flops=len(offsets) * 2 * rows * depth * weight.shape[0],
            bytes_accessed=len(offsets) * depth * weight.shape[0] * 2,
            transcendentals=0,
        ),
        name="terms",
    )(info, lhs, weight)


def tile_of(depth):
    return min(1024, depth)


def column_block(offsets, steps):
    def at(j, c, info, *more):
        device = info[offsets[0]]
        for b in range(1, len(offsets)):
            device = jnp.where(j == b, info[offsets[b]], device)
        return (0, device * steps + c)

    return at


def fixed_block(shape):
    return pl.BlockSpec(shape, lambda j, c, *s: (0,) * len(shape))


def ring_sum(ring, info, a, b, lhs, weight, depth, energy=None, aside=None):
    n, half = ring.n, ring.half
    rows = lhs.shape[0]
    for d in range(half - 1, -1, -1):
        lhs, a, b = lax.optimization_barrier((lhs, a, b))
        a, b = ring.right(a), ring.left(b)
        terms = terms_of(info, [d, n - d] if d > 0 else [0], lhs, weight, depth)
        if d == half - 1 and aside is not None:
            terms, a, b, aside = lax.optimization_barrier((terms, a, b, aside))
            swap = [(i, (i + 1) % ring.pools) for i in range(ring.pools)]
            aside = aside, lax.ppermute(aside, "pool", swap)
        else:
            terms, a, b = lax.optimization_barrier((terms, a, b))
        if d > 0:
            kind = "second" if d == half - 1 else "later"
            a, b = join(kind, rows, depth, energy, terms, [a, b])
    return terms, ([a, b] if half > 1 else [jnp.concatenate([a, b], axis=0)]), aside


def mixer_kernel(arrived, tenants, inner_size, info, adapter, term_ref, *refs):
    got = refs[:arrived]
    e_ref, tok_ref, gain_ref = refs[arrived : arrived + 3]
    downs = refs[arrived + 3 : arrived + 3 + tenants]
    first_ref, message_ref = refs[-2:]
    rows, depth = term_ref.shape
    length = rows // tenants
    tail = slice(depth, depth + 128)
    energy = e_ref[...]
    total = term_ref[...]
    for g in got:
        energy = energy + energy_of(g[:, tail])
        total = total + g[:, :depth].astype(f32)
    scale = lax.rsqrt(energy / inner_size + epsilon)
    first = (tok_ref[...].astype(f32) + total * scale).astype(bf16)
    wide = first.astype(f32)
    high, low = split(jnp.sum(wide * wide, axis=1, keepdims=True))
    first_ref[...] = first
    attn = (wide * gain_ref[...]).astype(bf16)
    message_ref[:, :depth] = attn
    rank = downs[0].shape[1]
    parts = []
    for i in range(tenants):
        x = attn[i * length : (i + 1) * length]
        parts.append(
            lax.dot_general(x, downs[i][0], (((1,), (1,)), ((), ())), preferred_element_type=f32)
        )
    small = jnp.concatenate(parts, axis=0).astype(bf16)
    message_ref[:, tail] = lanes_of([(rank, high), (rank + 1, low)], rows)
    message_ref[:, depth : depth + rank] = small


def mixer_step(info, adapter, terms, got, energy, own_tokens, gain, down, inner_size):
    rows, depth = terms.shape
    tenants = adapter.shape[0]
    operands = [terms, *got, energy, own_tokens, gain] + [down] * tenants

    def whole(a):
        return pl.BlockSpec(a.shape, lambda j, *s: (0,) * a.ndim)

    in_specs = [whole(a) for a in operands]
    in_specs[3 + len(got)] = pl.BlockSpec(
        (1, depth), lambda j, info, adapter: (0, info[info.shape[0] - 2])
    )
    for i in range(tenants):
        in_specs[4 + len(got) + i] = pl.BlockSpec(
            (1, *down.shape[1:]), functools.partial(lambda i, j, info, adapter: (adapter[i], 0, 0), i)
        )
    shapes = [jax.ShapeDtypeStruct((rows, depth), bf16), jax.ShapeDtypeStruct((rows, depth + 128), bf16)]
    return pl.pallas_call(
        functools.partial(mixer_kernel, len(got), tenants, inner_size),
        grid_spec=pltpu.PrefetchScalarGridSpec(
            num_scalar_prefetch=2,
            grid=(1,),
            in_specs=in_specs,
            out_specs=[whole(s) for s in shapes],
        ),
        out_shape=shapes,
        compiler_params=pltpu.CompilerParams(vmem_limit_bytes=16 << 20),
        cost_estimate=pl.CostEstimate(
            flops=2 * rows * depth * 64, bytes_accessed=rows * depth * 16, transcendentals=0
        ),
        name="mixer_step",
    )(info, adapter, *operands)


def query_kernel(offsets, count, first_call, info, *refs):
    blocks = refs[:count]
    w_ref = refs[count]
    q_ref, l_ref = refs[-2:]
    j, k = pl.program_id(0), pl.program_id(1)
    kb = w_ref.shape[0]
    steps = pl.num_programs(1)
    depth = blocks[0].shape[1] - 128

    @pl.when((j == 0) & (k == 0))
    def _():
        if first_call:
            q_ref[...] = jnp.zeros_like(q_ref)
            l_ref[...] = jnp.zeros_like(l_ref)
        else:
            q_ref[...] = refs[count + 1][...]
            l_ref[...] = refs[count + 2][...]

    for b in range(len(offsets)):
        for kk in range(depth // kb):

            @pl.when((j == b) & (k == kk))
            def _():
                pieces = [blocks[b]] if count == len(offsets) else blocks
                base = 0
                for block in pieces:
                    at = slice(base, base + block.shape[0])
                    q_ref[at] += jnp.dot(
                        block[:, kk * kb : (kk + 1) * kb], w_ref[...], preferred_element_type=f32
                    )
                    if kk == 0:
                        l_ref[at] += block[:, depth:].astype(f32)
                    base += block.shape[0]


def query_step(info, offsets, blocks, weight, depth, accs):
    count = len(blocks)
    rows = sum(b.shape[0] for b in blocks) // len(offsets)
    cols = weight.shape[1]
    kb = tile_of(depth)
    steps = depth // kb

    def row_block(j, k, info):
        at = info[offsets[0]]
        for b in range(1, len(offsets)):
            at = jnp.where(j == b, info[offsets[b]], at)
        return (at * steps + k, 0)

    shapes = [(rows, cols), (rows, 128)]
    in_specs = [fixed_block(b.shape) for b in blocks] + [pl.BlockSpec((kb, cols), row_block)]
    operands = [info, *blocks, weight]
    aliases = {}
    if accs is not None:
        in_specs += [fixed_block(s) for s in shapes]
        aliases = {len(operands): 0, len(operands) + 1: 1}
        operands += accs
    return pl.pallas_call(
        functools.partial(query_kernel, offsets, count, accs is None),
        grid_spec=pltpu.PrefetchScalarGridSpec(
            num_scalar_prefetch=1,
            grid=(len(offsets), steps),
            in_specs=in_specs,
            out_specs=[fixed_block(s) for s in shapes],
        ),
        out_shape=[jax.ShapeDtypeStruct(s, f32) for s in shapes],
        input_output_aliases=aliases,
        compiler_params=pltpu.CompilerParams(vmem_limit_bytes=46 << 20),
        cost_estimate=pl.CostEstimate(
            flops=len(offsets) * 2 * rows * depth * cols,
            bytes_accessed=len(offsets) * depth * cols * 2,
            transcendentals=0,
        ),
        name="query_step",
    )(*operands)


def shifted(history, x, k):
    if k == 3:
        return x
    return jnp.concatenate([history[k:3], x[: x.shape[0] - 3 + k]], axis=0)


def conv_silu(history, x, taps):
    total = taps[0:1] * shifted(history, x, 0)
    for k in range(1, 4):
        total = total + taps[k : k + 1] * shifted(history, x, k)
    return total * jax.nn.sigmoid(total)


def spans(heads, width):
    lane = lax.broadcasted_iota(jnp.int32, (heads, heads * width), 1)
    row = lax.broadcasted_iota(jnp.int32, (heads, heads * width), 0)
    return jnp.where(lane // width == row, 1.0, 0.0).astype(f32)


def far_columns(info, half, w_ref, held, arrived):
    depth = held.shape[1]
    at = pl.multiple_of(info[half] * depth, 128)
    return pltpu.make_async_copy(w_ref.at[:, pl.ds(at, depth)], held, arrived)


def first_messages(lhs_ref, held, energy_ref, left_ref, right_ref):
    term = jnp.dot(lhs_ref[...], held[...], preferred_element_type=f32)
    h, depth = left_ref.shape[0], held.shape[1]
    for j, out in enumerate((left_ref, right_ref)):
        side = slice(j * h, (j + 1) * h)
        out[:, :depth] = term[side].astype(bf16)
        if energy_ref is not None:
            out[:, depth : depth + 128] = energy_lanes(energy_ref[side])


def state_kernel(
    slot,
    info,
    x_ref,
    z_ref,
    kept_ref,
    came_ref,
    w_ref,
    hx_ref,
    hbc_ref,
    tx_ref,
    tbc_ref,
    bias_ref,
    rate_ref,
    skip_ref,
    gain_ref,
    own_ref,
    far_ref,
    gated_ref,
    energy_ref,
    final_ref,
    left_ref,
    right_ref,
    initial,
    held,
    arrived,
    *,
    slots,
    half,
):
    i = pl.program_id(0)
    count = info.shape[0]
    copy = far_columns(info, half, w_ref, held, arrived)

    @pl.when(i == 0)
    def _():
        copy.start()

    is_own = slot[i] // slots == info[count - 1]

    @pl.when(is_own)
    def _():
        initial[...] = own_ref[0]

    @pl.when(jnp.logical_not(is_own))
    def _():
        initial[...] = far_ref[0]

    length = x_ref.shape[0]
    heads = bias_ref.shape[1]
    values = conv_silu(hx_ref[0], x_ref[...].astype(bf16).astype(f32), tx_ref[...])
    shared = i // (pl.num_programs(0) // 2) == lax.rem(info[count - 2], 2)
    projected = jnp.where(shared, kept_ref[...], came_ref[...].astype(f32))
    bc = conv_silu(hbc_ref[0], projected[:, : 2 * STATE], tbc_ref[...])
    all_raw = projected[:, 2 * STATE :]
    pick = (all_raw.shape[1], heads)
    chosen = lax.broadcasted_iota(jnp.int32, pick, 0) == (
        lax.broadcasted_iota(jnp.int32, pick, 1) + info[count - 2] * heads
    )
    chosen = jnp.where(chosen, 1.0, 0.0).astype(f32)
    in_state = bc[:, :STATE].astype(bf16)
    out_state = bc[:, STATE:].astype(bf16)
    raw = jnp.dot(all_raw, chosen, precision=highest, preferred_element_type=f32) + bias_ref[...]
    steps = jnp.maximum(raw, 0.0) + jnp.log1p(jnp.exp(-jnp.abs(raw)))
    log_decay = -steps * jnp.exp(rate_ref[...])
    row = lax.broadcasted_iota(jnp.int32, (length, length), 0)
    col = lax.broadcasted_iota(jnp.int32, (length, length), 1)
    lower = jnp.where(row >= col, 1.0, 0.0).astype(f32)
    running = jnp.dot(lower, log_decay, precision=highest, preferred_element_type=f32)
    last = running[length - 1 : length]

    wide = spans(heads, length)
    both = jnp.dot(
        jnp.concatenate([running, steps], axis=0), wide, precision=highest, preferred_element_type=f32
    )
    run_t, step_t = both[:length], both[length:]
    lane = lax.broadcasted_iota(jnp.int32, (length, heads * length), 1) % length
    place = lax.broadcasted_iota(jnp.int32, (length, heads * length), 0)
    diagonal = lane == place
    run_s = jnp.sum(jnp.where(diagonal, run_t, 0.0), axis=0, keepdims=True)
    step_s = jnp.sum(jnp.where(diagonal, step_t, 0.0), axis=0, keepdims=True)
    seen = place >= lane
    decays = jnp.where(seen, jnp.exp(jnp.where(seen, run_t - run_s, 0.0)), 0.0)
    overlap = lax.dot_general(
        out_state,
        jnp.concatenate([in_state] * heads, axis=0),
        (((1,), (1,)), ((), ())),
        preferred_element_type=f32,
    )
    mixing = (overlap * decays * step_s).astype(bf16)
    short = values.astype(bf16)
    group = min(4, heads)
    gl, gw = group * length, group * HDIM
    own_block = (
        lax.broadcasted_iota(jnp.int32, (gl, gw), 0) // length
        == lax.broadcasted_iota(jnp.int32, (gl, gw), 1) // HDIM
    )
    within = []
    for g in range(heads // group):
        v = jnp.concatenate([values[:, g * gw : (g + 1) * gw]] * group, axis=0)
        v = jnp.where(own_block, v, 0.0).astype(bf16)
        within.append(jnp.dot(mixing[:, g * gl : (g + 1) * gl], v, preferred_element_type=f32))
    within = within[0] if len(within) == 1 else jnp.concatenate(within, axis=1)

    narrow = spans(heads, HDIM)
    scales = jnp.dot(
        jnp.concatenate(
            [
                jnp.exp(running),
                jnp.exp(last - running) * steps,
                jnp.broadcast_to(skip_ref[...], (8, heads)),
            ],
            axis=0,
        ),
        narrow,
        precision=highest,
        preferred_element_type=f32,
    )
    start = initial[...]
    carried = lax.dot_general(
        out_state, start.astype(bf16), (((1,), (1,)), ((), ())), preferred_element_type=f32
    )
    result = within + carried * scales[:length] + scales[2 * length : 2 * length + 1] * values
    z = z_ref[...].astype(bf16).astype(f32)
    gated = result * (z * jax.nn.sigmoid(z))
    at = pl.ds(pl.multiple_of(i * length, length), length)
    energy_ref[at, :] = jnp.sum(gated * gated, axis=1, keepdims=True)
    gated_ref[at, :] = (gated * gain_ref[...]).astype(bf16)

    kept = jnp.exp(
        lax.dot_general(
            log_decay,
            jnp.ones((length, STATE), f32),
            (((0,), (0,)), ((), ())),
            precision=highest,
            preferred_element_type=f32,
        )
    )
    update = lax.dot_general(
        (values * scales[length : 2 * length]).astype(bf16),
        in_state,
        (((0,), (0,)), ((), ())),
        preferred_element_type=f32,
    )
    for h in range(heads):
        at = slice(h * HDIM, (h + 1) * HDIM)
        final_ref[0, at, :] = update[at] + start[at] * kept[h : h + 1]

    @pl.when(i == pl.num_programs(0) - 1)
    def _():
        copy.wait()
        first_messages(gated_ref, held, energy_ref, left_ref, right_ref)


def state_pass(
    half, info, slot, inner, kept, came, weight, hx, hbc, tx, tbc, bias, rate, skip, gain, own_pool, far_pool
):
    tenants = slot.shape[0]
    length = inner.shape[0] // 2 // tenants
    cols = inner.shape[1]
    slots = own_pool.shape[0]

    def rows(width):
        return pl.BlockSpec((length, width), lambda i, *s: (i, 0))

    def whole(a):
        return pl.BlockSpec(a.shape, lambda i, *s: (0,) * a.ndim)

    def own_slot(i, slot, info):
        return (jnp.clip(slot[i] - info[info.shape[0] - 1] * slots, 0, slots - 1), 0, 0)

    def far_slot(i, slot, info):
        return (jnp.clip(slot[i] - (1 - info[info.shape[0] - 1]) * slots, 0, slots - 1), 0, 0)

    pooled = (1, cols, STATE)
    message = (tenants * length // 2, weight.shape[1] // (2 * half) + 128)

    def fixed(shape):
        return pl.BlockSpec(shape, lambda i, *s: (0, 0))

    return pl.pallas_call(
        functools.partial(state_kernel, slots=slots, half=half),
        grid_spec=pltpu.PrefetchScalarGridSpec(
            num_scalar_prefetch=2,
            grid=(tenants,),
            in_specs=[
                rows(cols),
                pl.BlockSpec((length, cols), lambda i, *s: (tenants + i, 0)),
                pl.BlockSpec((length, kept.shape[1]), lambda i, *s: (i % (tenants // 2), 0)),
                pl.BlockSpec((length, kept.shape[1]), lambda i, *s: (i % (tenants // 2), 0)),
                pl.BlockSpec(memory_space=pl.ANY),
                pl.BlockSpec((1, 3, cols), lambda i, *s: (i, 0, 0)),
                pl.BlockSpec((1, 3, 2 * STATE), lambda i, *s: (i, 0, 0)),
                whole(tx),
                whole(tbc),
                whole(bias),
                whole(rate),
                whole(skip),
                whole(gain),
                pl.BlockSpec(pooled, own_slot),
                pl.BlockSpec(pooled, far_slot),
            ],
            out_specs=[
                fixed((tenants * length, cols)),
                fixed((tenants * length, 1)),
                pl.BlockSpec(pooled, lambda i, *s: (i, 0, 0)),
                fixed(message),
                fixed(message),
            ],
            scratch_shapes=[
                pltpu.VMEM((cols, STATE), f32),
                pltpu.VMEM((weight.shape[0], message[1] - 128), bf16),
                pltpu.SemaphoreType.DMA,
            ],
        ),
        out_shape=[
            jax.ShapeDtypeStruct((tenants * length, cols), bf16),
            jax.ShapeDtypeStruct((tenants * length, 1), f32),
            jax.ShapeDtypeStruct((tenants, cols, STATE), f32),
            jax.ShapeDtypeStruct(message, bf16),
            jax.ShapeDtypeStruct(message, bf16),
        ],
        compiler_params=pltpu.CompilerParams(vmem_limit_bytes=48 << 20),
        cost_estimate=pl.CostEstimate(
            flops=tenants * 6 * length * cols * STATE,
            bytes_accessed=tenants * cols * STATE * 10,
            transcendentals=0,
        ),
        name="state_pass",
    )(slot, info, inner, inner, kept, came, weight, hx, hbc, tx, tbc, bias, rate, skip, gain, own_pool, far_pool)


def attend_kernel(
    half, width, table, limit, adapter, info, q_ref, low_ref, up_ref, near_ref, far_ref, w_ref, *refs
):
    o_ref, left_ref, right_ref, held, arrived = refs[-5:]
    copy = far_columns(info, half, w_ref, held, arrived)

    @pl.when(pl.program_id(0) == 0)
    def _():
        copy.start()

    i = pl.program_id(0)
    length = q_ref.shape[0]
    heads = q_ref.shape[1] // HEAD_SIZE
    blocks = table.shape[1]
    part = near_ref.shape[1]
    core = info[info.shape[0] - 1]
    rank = up_ref.shape[1]
    square = low_ref[:, rank : rank + 1] + low_ref[:, rank + 1 : rank + 2]
    norm = lax.rsqrt(square / width + epsilon)
    low = (low_ref[:, :rank] * norm).astype(bf16)
    raised = jnp.dot(low, up_ref[0], preferred_element_type=f32)
    q = (q_ref[...] * norm + adapter_scale * raised).astype(bf16)
    q = jnp.concatenate([q[:, h * HEAD_SIZE : (h + 1) * HEAD_SIZE] for h in range(heads)], axis=0)
    fresh = jnp.concatenate([refs[0][...], refs[1][...]], axis=1)
    for came in refs[2:-5]:
        fresh = fresh + came[...].astype(f32)
    fresh = (fresh * norm).astype(bf16)
    pieces = []
    for j in range(blocks):
        at = table[i, j]
        pieces += [near_ref[at], far_ref[at]]
    cached = jnp.concatenate(pieces, axis=0)
    context = cached.shape[0]
    nt = (((1,), (1,)), ((), ()))
    scale = HEAD_SIZE ** (-0.5)
    old = lax.dot_general(q, cached[:, :HEAD_SIZE], nt, preferred_element_type=f32) * scale
    new = lax.dot_general(q, fresh[:, :HEAD_SIZE], nt, preferred_element_type=f32) * scale
    lane = lax.broadcasted_iota(jnp.int32, old.shape, 1)
    inside = lane % (2 * part)
    far_side = jnp.where(inside >= part, 1, 0)
    half = jnp.where(core == 0, far_side, 1 - far_side)
    place = (lane // (2 * part)) * (2 * part) + half * part + inside % part
    old_seen = place < limit[i]
    token = lax.broadcasted_iota(jnp.int32, new.shape, 0) % length
    new_seen = lax.broadcasted_iota(jnp.int32, new.shape, 1) <= token
    old = jnp.where(old_seen, old, -jnp.inf)
    new = jnp.where(new_seen, new, -jnp.inf)
    top = jnp.maximum(jnp.max(old, axis=1, keepdims=True), jnp.max(new, axis=1, keepdims=True))
    old = jnp.where(old_seen, jnp.exp(old - top), 0.0)
    new = jnp.where(new_seen, jnp.exp(new - top), 0.0)
    share = 1.0 / (jnp.sum(old, axis=1, keepdims=True) + jnp.sum(new, axis=1, keepdims=True))
    out = jnp.dot((old * share).astype(bf16), cached[:, HEAD_SIZE:], preferred_element_type=f32)
    out += jnp.dot((new * share).astype(bf16), fresh[:, HEAD_SIZE:], preferred_element_type=f32)
    out = out.astype(bf16)
    own_rows = pl.ds(pl.multiple_of(i * length, length), length)
    for h in range(heads):
        o_ref[own_rows, h * HEAD_SIZE : (h + 1) * HEAD_SIZE] = out[h * length : (h + 1) * length]

    @pl.when(i == pl.num_programs(0) - 1)
    def _():
        copy.wait()
        first_messages(o_ref, held, None, left_ref, right_ref)


def attend(ring, width, table, limit, adapter, info, q, low, up, near, far, weight, kv, came):
    tenants = table.shape[0]
    length = q.shape[0] // tenants

    def rows(a):
        return pl.BlockSpec((length, a.shape[1]), lambda i, *s: (i, 0))

    def whole(a):
        return pl.BlockSpec(a.shape, lambda i, *s: (0,) * a.ndim)

    message = (q.shape[0] // 2, weight.shape[1] // ring.n)

    def fixed(shape):
        return pl.BlockSpec(shape, lambda i, *s: (0, 0))

    def own(base):
        return pl.BlockSpec(
            (length, HEAD_SIZE), lambda i, t, n, a, info: (i, base + info[ring.n])
        )

    return pl.pallas_call(
        functools.partial(attend_kernel, ring.half, width),
        grid_spec=pltpu.PrefetchScalarGridSpec(
            num_scalar_prefetch=4,
            grid=(tenants,),
            in_specs=[
                rows(q),
                rows(low),
                pl.BlockSpec((1, *up.shape[1:]), lambda i, t, n, a, info: (a[i], 0, 0)),
                whole(near),
                whole(far),
                pl.BlockSpec(memory_space=pl.ANY),
                own(0),
                own(KEY_HEADS),
            ]
            + [rows(a) for a in came],
            out_specs=[fixed(q.shape), fixed(message), fixed(message)],
            scratch_shapes=[
                pltpu.VMEM((weight.shape[0], message[1]), bf16),
                pltpu.SemaphoreType.DMA,
            ],
        ),
        out_shape=[
            jax.ShapeDtypeStruct(q.shape, bf16),
            jax.ShapeDtypeStruct(message, bf16),
            jax.ShapeDtypeStruct(message, bf16),
        ],
        compiler_params=pltpu.CompilerParams(vmem_limit_bytes=46 << 20),
        cost_estimate=pl.CostEstimate(
            flops=tenants * 4 * length * q.shape[1] * 288,
            bytes_accessed=near.size * 4 + q.size * 6 + up.size,
            transcendentals=0,
        ),
        name="attend",
    )(table, limit, adapter, info, q, low, up, near, far, weight, kv, kv, *came)


def pick_kernel(heads, info, pool_ref, o_ref):
    for d, head in enumerate(heads):
        for k in range(2):
            at = (head + k * KEY_HEADS) * HEAD_SIZE
            o_ref[d, :, :, k * HEAD_SIZE : (k + 1) * HEAD_SIZE] = pool_ref[:, :, at : at + HEAD_SIZE]


def pick_heads(info, pool, heads, pools):
    count, block_len, wide = pool.shape
    part = block_len // pools
    shape = (len(heads), count, part, 2 * HEAD_SIZE)
    return pl.pallas_call(
        functools.partial(pick_kernel, heads),
        grid_spec=pltpu.PrefetchScalarGridSpec(
            num_scalar_prefetch=1,
            grid=(1,),
            in_specs=[pl.BlockSpec((count, part, wide), lambda j, info: (0, info[info.shape[0] - 1], 0))],
            out_specs=pl.BlockSpec(shape, lambda j, info: (0, 0, 0, 0)),
        ),
        out_shape=jax.ShapeDtypeStruct(shape, bf16),
        compiler_params=pltpu.CompilerParams(vmem_limit_bytes=8 << 20),
        name="pick_heads",
    )(info, pool)


def fresh_kernel(kind, offsets, heads_at, info, kv_ref, *refs):
    outs = refs[-2:]
    got = refs[:-2]
    rows = kv_ref.shape[0]
    h = rows // 2
    sides = [slice(0, h), slice(h, rows)]
    for j in range(2):
        offset = offsets[0] if kind == "first" else offsets[j]
        head = info[heads_at + offset]
        for k in range(2):
            at = pl.ds(pl.multiple_of((head + k * KEY_HEADS) * HEAD_SIZE, HEAD_SIZE), HEAD_SIZE)
            to = slice(k * HEAD_SIZE, (k + 1) * HEAD_SIZE)
            if kind == "first":
                outs[j][:, to] = kv_ref[sides[j], at].astype(bf16)
            elif kind == "second":
                mine, other = sides[j], sides[1 - j]
                outs[j][mine, to] = (kv_ref[mine, at] + got[j][:, to].astype(f32)).astype(bf16)
                outs[j][other, to] = kv_ref[other, at].astype(bf16)
            else:
                outs[j][:, to] = (kv_ref[:, at] + got[j][:, to].astype(f32)).astype(bf16)


def fresh_join(info, kind, offsets, heads_at, kv, got):
    rows = kv.shape[0]
    shape = (rows // 2 if kind == "first" else rows, 2 * HEAD_SIZE)
    operands = [kv, *got]
    return pl.pallas_call(
        functools.partial(fresh_kernel, kind, offsets, heads_at),
        grid_spec=pltpu.PrefetchScalarGridSpec(
            num_scalar_prefetch=1,
            grid=(1,),
            in_specs=[pl.BlockSpec(a.shape, lambda j, info: (0, 0)) for a in operands],
            out_specs=[pl.BlockSpec(shape, lambda j, info: (0, 0))] * 2,
        ),
        out_shape=[jax.ShapeDtypeStruct(shape, bf16)] * 2,
        compiler_params=pltpu.CompilerParams(vmem_limit_bytes=8 << 20),
        name="fresh_join",
    )(info, *operands)


def per_device(
    ring,
    tokens,
    mamba_in_weight,
    state_projection,
    inner_taps,
    state_taps,
    inner_history,
    state_history,
    step_size_bias,
    log_decay_rate,
    skip_factor,
    gated_norm_gain,
    mamba_out_weight,
    saved_state_pool,
    tenant_state_slot,
    attention_gain,
    query_matrix,
    adapter_down,
    adapter_up,
    tenant_adapter,
    key_value_weight,
    key_value_pool,
    tenant_blocks,
    cached_length,
    attention_out_weight,
):
    n, half, pools = ring.n, ring.half, ring.pools
    tenants, length, depth = tokens.shape
    rows = tenants * length
    width = depth * n
    info = ring.info()
    own_tokens = tokens.reshape(rows, depth)
    heads = step_size_bias.shape[0]
    cols = mamba_in_weight.shape[2]
    swap = [(i, (i + 1) % pools) for i in range(pools)]

    slots = saved_state_pool.shape[0]
    flat_pool = saved_state_pool.reshape(slots, heads * HDIM, STATE)
    far_pool = lax.ppermute(flat_pool, "pool", swap)

    inner, kept, came, cache = ring.gather(
        own_tokens,
        lambda offsets, blocks, acc: in_product(info, offsets, blocks, mamba_in_weight, depth, acc),
        lambda x: partial_product(info, x, state_projection),
        pick_heads(info, key_value_pool, ring.heads, pools),
    )
    cache = cache.reshape(-1, *cache.shape[2:])

    gated, energy, final_state, a, b = state_pass(
        half,
        info,
        tenant_state_slot,
        inner,
        kept,
        came,
        mamba_out_weight,
        inner_history.astype(f32),
        state_history,
        inner_taps.astype(f32),
        state_taps.astype(f32),
        step_size_bias[None],
        log_decay_rate[None],
        skip_factor[None],
        gated_norm_gain[None],
        flat_pool,
        far_pool,
    )
    terms, got, (cache, far_cache) = ring_sum(ring, info, a, b, gated, mamba_out_weight, depth, energy, cache)
    first, message = mixer_step(
        info,
        tenant_adapter,
        terms,
        got,
        energy,
        own_tokens,
        attention_gain[None],
        adapter_down.transpose(0, 2, 1),
        cols * n,
    )

    kv = jnp.dot(message[:, :depth], key_value_weight, preferred_element_type=f32)

    h = rows // 2
    a, b = message, message
    ka, kb = fresh_join(info, "first", [half], n, kv, [])
    accs, ready = None, ([0], [message])
    for s in range(1, half + 1):
        if s == half:
            a, b = a[:h], b[h:]
        a, b, ka, kb = ring.right(a), ring.left(b), ring.right(ka), ring.left(kb)
        accs = query_step(info, *ready, query_matrix, depth, accs)
        a, b, ka, kb, accs = lax.optimization_barrier((a, b, ka, kb, accs))
        ready = ([n - s, s], [a, b]) if s < half else ([half], [a, b])
        if s < half:
            kind = "second" if s == 1 else "later"
            ka, kb = fresh_join(info, kind, [half - s, n - half + s], n, kv, [ka, kb])
    kv_came = [ka, kb] if half > 1 else [jnp.concatenate([ka, kb], axis=0)]
    query, low = query_step(info, *ready, query_matrix, depth, accs)
    heads_out, a, b = attend(
        ring,
        width,
        tenant_blocks,
        cached_length,
        tenant_adapter,
        info,
        query,
        low,
        adapter_up,
        cache,
        far_cache,
        attention_out_weight,
        kv,
        kv_came,
    )
    terms, got, _ = ring_sum(ring, info, a, b, heads_out, attention_out_weight, depth)
    second = terms + first.astype(f32)
    for g in got:
        second = second + g.astype(f32)
    second = second.astype(bf16)
    return (
        second.reshape(tenants, length, depth),
        final_state.reshape(tenants, heads, HDIM, STATE),
    )


def solution(mesh):
    in_specs = (
        P(("groups", "pool"), None, "tensor"),
        P(None, None, "tensor"),
        P("tensor", None),
        P(None, "tensor"),
        P(),
        P(("groups", "pool"), None, "tensor"),
        P(("groups", "pool"), None, None),
        P("tensor"),
        P("tensor"),
        P("tensor"),
        P("tensor"),
        P("tensor", None),
        P(("groups", "pool"), "tensor", None, None),
        P(("groups", "pool")),
        P(),
        P(None, "tensor"),
        P(None, "tensor", None),
        P(None, None, "tensor"),
        P(("groups", "pool")),
        P("tensor", None),
        P(("groups", "tensor"), None, None),
        P(("groups", "pool"), None),
        P(("groups", "pool")),
        P("tensor", None),
    )
    out_specs = (P(("groups", "pool"), None, "tensor"), P(("groups", "pool"), "tensor", None, None))
    ring = Ring(mesh.shape["tensor"], mesh.shape["pool"])
    return jax.shard_map(
        functools.partial(per_device, ring),
        mesh=mesh,
        in_specs=in_specs,
        out_specs=out_specs,
        check_vma=False,
    )
```

```python
import functools

import jax
import jax.numpy as jnp
from jax import lax
from jax.experimental import pallas as pl
from jax.experimental.pallas import tpu as pltpu
from jax.sharding import PartitionSpec as P

HDIM = 64
STATE = 256
QUERY_HEADS = 64
KEY_HEADS = 8
HEAD_SIZE = 128

epsilon = 1e-05
adapter_scale = 2.0
highest = lax.Precision.HIGHEST
f32 = jnp.float32
bf16 = jnp.bfloat16


def ring_order(n):
    cols = 1
    for c in range(2, n):
        if n % c == 0 and (n // c) % 2 == 0 and c <= n // c:
            cols = c
    if cols == 1:
        return list(range(n))
    rows = n // cols
    order = [r * cols for r in range(rows)]
    for k, r in enumerate(reversed(range(rows))):
        across = list(range(1, cols))
        order += [r * cols + c for c in (across if k % 2 == 0 else across[::-1])]
    return order


class Ring:
    def __init__(self, n, pools):
        self.n = n
        heads = [d * QUERY_HEADS // n // (QUERY_HEADS // KEY_HEADS) for d in range(n)]
        self.half = n // 2
        self.pools = pools
        order = ring_order(n)
        place = {d: i for i, d in enumerate(order)}
        self.table = [
            [order[(place[d] + s) % n] for s in range(n)]
            + [heads[order[(place[d] + s) % n]] for s in range(n)]
            + [d, c]
            for d in range(n)
            for c in range(pools)
        ]
        self.heads = heads
        self.cw = [(order[i], order[(i + 1) % n]) for i in range(n)]
        self.ccw = [(order[i], order[(i - 1) % n]) for i in range(n)]

    def info(self):
        at = lax.axis_index("tensor") * self.pools + lax.axis_index("pool")
        return lax.dynamic_slice_in_dim(jnp.array(self.table, jnp.int32), at, 1, 0)[0]

    def right(self, x):
        return lax.ppermute(x, "tensor", self.cw)

    def left(self, x):
        return lax.ppermute(x, "tensor", self.ccw)

    def masks(self):
        found, m = [], 1
        while m < self.n:
            found.append([(i, i ^ m) for i in range(self.n)])
            m *= 2
        return found

    def gather(self, x, weigh, project, aside):
        n, half = self.n, self.half
        h = x.shape[0] // 2
        pairs = self.masks()
        exchange = pairs + pairs[:1]
        sums, ready = None, ([0], [x])
        a = b = x
        for s in range(1, max(half, len(exchange)) + 1):
            if s == half:
                a, b = a[:h], b[h:]
            if s <= half:
                a, b = self.right(a), self.left(b)
            if s == 1:
                sums = weigh(*ready, sums)
                x, sums = lax.optimization_barrier((x, sums))
                keep, give = project(x)
            if s <= len(exchange):
                came = lax.ppermute(give, "tensor", exchange[s - 1])
            if 1 < s <= half:
                sums = weigh(*ready, sums)
            if s <= len(exchange):
                a, b, sums, came = lax.optimization_barrier((a, b, sums, came))
            else:
                a, b, sums = lax.optimization_barrier((a, b, sums))
            if s < len(exchange):
                keep = keep + came.astype(f32)
                give = keep.astype(bf16)
            if s <= half:
                ready = ([n - s, s], [a, b]) if s < half else ([half], [a, b])
        x, aside, sums = lax.optimization_barrier((ready[1], aside, sums))
        aside = lax.all_to_all(aside, "tensor", 0, 0, tiled=True)
        return weigh(ready[0], x, sums), keep, came, aside


def split(x):
    high = x.astype(bf16)
    return high, (x - high.astype(f32)).astype(bf16)


def partial_kernel(info, x_ref, w_ref, keep_ref, give_ref, whole):
    whole[...] = jnp.dot(x_ref[...], w_ref[...], preferred_element_type=f32)
    h = keep_ref.shape[0]
    odd = lax.rem(info[info.shape[0] - 2], 2)
    keep_ref[...] = whole[pl.ds(pl.multiple_of(odd * h, 8), h), :]
    give_ref[...] = whole[pl.ds(pl.multiple_of((1 - odd) * h, 8), h), :].astype(bf16)


def partial_product(info, x, weight):
    shape = (x.shape[0] // 2, weight.shape[1])
    return pl.pallas_call(
        partial_kernel,
        grid_spec=pltpu.PrefetchScalarGridSpec(
            num_scalar_prefetch=1,
            grid=(1,),
            in_specs=[
                pl.BlockSpec(x.shape, lambda j, info: (0, 0)),
                pl.BlockSpec(weight.shape, lambda j, info: (0, 0)),
            ],
            out_specs=[pl.BlockSpec(shape, lambda j, info: (0, 0))] * 2,
            scratch_shapes=[pltpu.VMEM((x.shape[0], weight.shape[1]), f32)],
        ),
        out_shape=[jax.ShapeDtypeStruct(shape, f32), jax.ShapeDtypeStruct(shape, bf16)],
        compiler_params=pltpu.CompilerParams(vmem_limit_bytes=12 << 20),
        name="partial_product",
    )(info, x, weight)


def in_kernel(offsets, count, chunks, first_call, info, *refs):
    blocks = refs[:count]
    w_ref = refs[count]
    o_ref, spread, held, arrived = refs[-4:]
    depth = held.shape[1] * chunks
    rows = o_ref.shape[0] // 2
    part = depth // chunks
    copies = []
    for b, offset in enumerate(offsets):
        for c in range(chunks):
            at = pl.multiple_of(info[offset] * depth + c * part, part)
            slot = b * chunks + c
            copies.append(
                pltpu.make_async_copy(w_ref.at[pl.ds(at, part)], held.at[slot], arrived.at[slot])
            )
    for copy in copies:
        copy.start()

    lane = lax.broadcasted_iota(jnp.int32, (128, 512), 1)
    sub = lax.broadcasted_iota(jnp.int32, (128, 512), 0)
    target = jnp.where(lane < 256, 2 * sub, 2 * sub + 257)
    widen = jnp.where(lane == target, 1.0, 0.0).astype(bf16)
    for b in range(len(offsets)):
        base = 0
        for block in [blocks[b]] if count == len(offsets) else blocks:
            r = block.shape[0]
            for p in range(depth // 128):
                piece = block[:, p * 128 : (p + 1) * 128]
                both = jnp.dot(piece, widen, preferred_element_type=f32).astype(bf16)
                spread[b, base : base + r, p * 256 : (p + 1) * 256] = both[:, :256]
                spread[b, rows + base : rows + base + r, p * 256 : (p + 1) * 256] = both[:, 256:]
            base += r

    for slot, copy in enumerate(copies):
        b, c = slot // chunks, slot % chunks
        copy.wait()
        w = held[slot].reshape(2 * part, held.shape[3])
        x = spread[b, :, c * 2 * part : (c + 1) * 2 * part]
        term = jnp.dot(x, w, preferred_element_type=f32)
        if slot == 0:
            o_ref[...] = term if first_call else refs[count + 1][...] + term
        else:
            o_ref[...] += term


def in_product(info, offsets, blocks, weight, depth, acc):
    count = len(blocks)
    rows = sum(b.shape[0] for b in blocks) // len(offsets)
    cols = weight.shape[2]
    chunks = 4 if depth % 1024 == 0 else 1
    slots = chunks * len(offsets)

    def fixed(shape):
        return pl.BlockSpec(shape, lambda j, info: (0, 0))

    in_specs = [fixed(b.shape) for b in blocks]
    in_specs.append(pl.BlockSpec(memory_space=pl.ANY))
    operands = [info, *blocks, weight]
    aliases = {}
    shape = (2 * rows, cols)
    if acc is not None:
        in_specs.append(fixed(shape))
        aliases = {len(operands): 0}
        operands.append(acc)
    return pl.pallas_call(
        functools.partial(in_kernel, offsets, count, chunks, acc is None),
        grid_spec=pltpu.PrefetchScalarGridSpec(
            num_scalar_prefetch=1,
            grid=(1,),
            in_specs=in_specs,
            out_specs=fixed(shape),
            scratch_shapes=[
                pltpu.VMEM((len(offsets), 2 * rows, 2 * depth), bf16),
                pltpu.VMEM((slots, depth // chunks, 2, cols), bf16),
                pltpu.SemaphoreType.DMA((slots,)),
            ],
        ),
        out_shape=jax.ShapeDtypeStruct(shape, f32),
        input_output_aliases=aliases,
        compiler_params=pltpu.CompilerParams(vmem_limit_bytes=30 << 20),
        cost_estimate=pl.CostEstimate(
            flops=len(offsets) * 8 * rows * depth * cols,
            bytes_accessed=len(offsets) * depth * cols * 8,
            transcendentals=0,
        ),
        name="in_product",
    )(*operands)


def lanes_of(columns, rows):
    lane = lax.broadcasted_iota(jnp.int32, (rows, 128), 1)
    out = jnp.zeros((rows, 128), f32)
    for at, value in columns:
        out = jnp.where(lane == at, value.astype(f32), out)
    return out.astype(bf16)


def energy_lanes(energy):
    high, low = split(energy)
    return lanes_of([(0, high), (1, low)], energy.shape[0])


def energy_of(lanes):
    wide = lanes.astype(f32)
    return wide[:, 0:1] + wide[:, 1:2]


def join_kernel(kind, depth, with_energy, *refs):
    refs = list(refs)
    e_ref = refs.pop(0) if with_energy else None
    term_ref = refs.pop(0)
    outs = refs[-2:]
    got = refs[:-2]
    rows = term_ref.shape[0] // 2
    h = rows // 2
    sides = [slice(0, h), slice(h, rows)]
    main, tail = slice(0, depth), slice(depth, depth + 128)
    for j in range(2):
        mine, other = sides[j], sides[1 - j]
        out = outs[j]
        base = j * rows
        if kind == "second":
            own = slice(base + mine.start, base + mine.stop)
            rest = slice(base + other.start, base + other.stop)
            out[mine, main] = (term_ref[own] + got[j][:, main].astype(f32)).astype(bf16)
            out[other, main] = term_ref[rest].astype(bf16)
            if with_energy:
                out[mine, tail] = energy_lanes(e_ref[mine] + energy_of(got[j][:, tail]))
                out[other, tail] = energy_lanes(e_ref[other])
        else:
            whole = slice(base, base + rows)
            out[:, main] = (term_ref[whole] + got[j][:, main].astype(f32)).astype(bf16)
            if with_energy:
                out[:, tail] = energy_lanes(e_ref[...] + energy_of(got[j][:, tail]))


def join(kind, rows, depth, energy, terms, got):
    wide = depth + (0 if energy is None else 128)
    operands = ([] if energy is None else [energy]) + [terms] + got
    return pl.pallas_call(
        functools.partial(join_kernel, kind, depth, energy is not None),
        out_shape=[jax.ShapeDtypeStruct((rows, wide), bf16)] * 2,
        compiler_params=pltpu.CompilerParams(vmem_limit_bytes=12 << 20),
        cost_estimate=pl.CostEstimate(flops=0, bytes_accessed=rows * wide * 8, transcendentals=0),
        name="join",
    )(*operands)


def term_kernel(info, lhs_ref, w_ref, o_ref):
    o_ref[...] = jnp.dot(lhs_ref[...], w_ref[...], preferred_element_type=f32)


def terms_of(info, offsets, lhs, weight, depth):
    rows = lhs.shape[0]
    return pl.pallas_call(
        term_kernel,
        grid_spec=pltpu.PrefetchScalarGridSpec(
            num_scalar_prefetch=1,
            grid=(len(offsets), 1),
            in_specs=[
                fixed_block(lhs.shape),
                pl.BlockSpec((weight.shape[0], depth), column_block(offsets, 1)),
            ],
            out_specs=pl.BlockSpec((rows, depth), lambda j, c, info: (j, 0)),
        ),
        out_shape=jax.ShapeDtypeStruct((len(offsets) * rows, depth), f32),
        compiler_params=pltpu.CompilerParams(vmem_limit_bytes=46 << 20),
        cost_estimate=pl.CostEstimate(
            flops=len(offsets) * 2 * rows * depth * weight.shape[0],
            bytes_accessed=len(offsets) * depth * weight.shape[0] * 2,
            transcendentals=0,
        ),
        name="terms",
    )(info, lhs, weight)


def tile_of(depth):
    return min(1024, depth)


def column_block(offsets, steps):
    def at(j, c, info, *more):
        device = info[offsets[0]]
        for b in range(1, len(offsets)):
            device = jnp.where(j == b, info[offsets[b]], device)
        return (0, device * steps + c)

    return at


def fixed_block(shape):
    return pl.BlockSpec(shape, lambda j, c, *s: (0,) * len(shape))


def ring_sum(ring, info, a, b, lhs, weight, depth, energy=None, aside=None):
    n, half = ring.n, ring.half
    rows = lhs.shape[0]
    for d in range(half - 1, -1, -1):
        lhs, a, b = lax.optimization_barrier((lhs, a, b))
        a, b = ring.right(a), ring.left(b)
        terms = terms_of(info, [d, n - d] if d > 0 else [0], lhs, weight, depth)
        if d == half - 1 and aside is not None:
            terms, a, b, aside = lax.optimization_barrier((terms, a, b, aside))
            swap = [(i, (i + 1) % ring.pools) for i in range(ring.pools)]
            aside = aside, lax.ppermute(aside, "pool", swap)
        else:
            terms, a, b = lax.optimization_barrier((terms, a, b))
        if d > 0:
            kind = "second" if d == half - 1 else "later"
            a, b = join(kind, rows, depth, energy, terms, [a, b])
    return terms, ([a, b] if half > 1 else [jnp.concatenate([a, b], axis=0)]), aside


def mixer_kernel(arrived, tenants, inner_size, info, adapter, term_ref, *refs):
    got = refs[:arrived]
    e_ref, tok_ref, gain_ref = refs[arrived : arrived + 3]
    downs = refs[arrived + 3 : arrived + 3 + tenants]
    first_ref, message_ref = refs[-2:]
    rows, depth = term_ref.shape
    length = rows // tenants
    tail = slice(depth, depth + 128)
    energy = e_ref[...]
    total = term_ref[...]
    for g in got:
        energy = energy + energy_of(g[:, tail])
        total = total + g[:, :depth].astype(f32)
    scale = lax.rsqrt(energy / inner_size + epsilon)
    first = (tok_ref[...].astype(f32) + total * scale).astype(bf16)
    wide = first.astype(f32)
    high, low = split(jnp.sum(wide * wide, axis=1, keepdims=True))
    first_ref[...] = first
    attn = (wide * gain_ref[...]).astype(bf16)
    message_ref[:, :depth] = attn
    rank = downs[0].shape[1]
    parts = []
    for i in range(tenants):
        x = attn[i * length : (i + 1) * length]
        parts.append(
            lax.dot_general(x, downs[i][0], (((1,), (1,)), ((), ())), preferred_element_type=f32)
        )
    small = jnp.concatenate(parts, axis=0).astype(bf16)
    message_ref[:, tail] = lanes_of([(rank, high), (rank + 1, low)], rows)
    message_ref[:, depth : depth + rank] = small


def mixer_step(info, adapter, terms, got, energy, own_tokens, gain, down, inner_size):
    rows, depth = terms.shape
    tenants = adapter.shape[0]
    operands = [terms, *got, energy, own_tokens, gain] + [down] * tenants

    def whole(a):
        return pl.BlockSpec(a.shape, lambda j, *s: (0,) * a.ndim)

    in_specs = [whole(a) for a in operands]
    in_specs[3 + len(got)] = pl.BlockSpec(
        (1, depth), lambda j, info, adapter: (0, info[info.shape[0] - 2])
    )
    for i in range(tenants):
        in_specs[4 + len(got) + i] = pl.BlockSpec(
            (1, *down.shape[1:]), functools.partial(lambda i, j, info, adapter: (adapter[i], 0, 0), i)
        )
    shapes = [jax.ShapeDtypeStruct((rows, depth), bf16), jax.ShapeDtypeStruct((rows, depth + 128), bf16)]
    return pl.pallas_call(
        functools.partial(mixer_kernel, len(got), tenants, inner_size),
        grid_spec=pltpu.PrefetchScalarGridSpec(
            num_scalar_prefetch=2,
            grid=(1,),
            in_specs=in_specs,
            out_specs=[whole(s) for s in shapes],
        ),
        out_shape=shapes,
        compiler_params=pltpu.CompilerParams(vmem_limit_bytes=16 << 20),
        cost_estimate=pl.CostEstimate(
            flops=2 * rows * depth * 64, bytes_accessed=rows * depth * 16, transcendentals=0
        ),
        name="mixer_step",
    )(info, adapter, *operands)


def query_kernel(offsets, count, first_call, info, *refs):
    blocks = refs[:count]
    w_ref = refs[count]
    q_ref, l_ref = refs[-2:]
    j, k = pl.program_id(0), pl.program_id(1)
    kb = w_ref.shape[0]
    steps = pl.num_programs(1)
    depth = blocks[0].shape[1] - 128

    @pl.when((j == 0) & (k == 0))
    def _():
        if first_call:
            q_ref[...] = jnp.zeros_like(q_ref)
            l_ref[...] = jnp.zeros_like(l_ref)
        else:
            q_ref[...] = refs[count + 1][...]
            l_ref[...] = refs[count + 2][...]

    for b in range(len(offsets)):
        for kk in range(depth // kb):

            @pl.when((j == b) & (k == kk))
            def _():
                pieces = [blocks[b]] if count == len(offsets) else blocks
                base = 0
                for block in pieces:
                    at = slice(base, base + block.shape[0])
                    q_ref[at] += jnp.dot(
                        block[:, kk * kb : (kk + 1) * kb], w_ref[...], preferred_element_type=f32
                    )
                    if kk == 0:
                        l_ref[at] += block[:, depth:].astype(f32)
                    base += block.shape[0]


def query_step(info, offsets, blocks, weight, depth, accs):
    count = len(blocks)
    rows = sum(b.shape[0] for b in blocks) // len(offsets)
    cols = weight.shape[1]
    kb = tile_of(depth)
    steps = depth // kb

    def row_block(j, k, info):
        at = info[offsets[0]]
        for b in range(1, len(offsets)):
            at = jnp.where(j == b, info[offsets[b]], at)
        return (at * steps + k, 0)

    shapes = [(rows, cols), (rows, 128)]
    in_specs = [fixed_block(b.shape) for b in blocks] + [pl.BlockSpec((kb, cols), row_block)]
    operands = [info, *blocks, weight]
    aliases = {}
    if accs is not None:
        in_specs += [fixed_block(s) for s in shapes]
        aliases = {len(operands): 0, len(operands) + 1: 1}
        operands += accs
    return pl.pallas_call(
        functools.partial(query_kernel, offsets, count, accs is None),
        grid_spec=pltpu.PrefetchScalarGridSpec(
            num_scalar_prefetch=1,
            grid=(len(offsets), steps),
            in_specs=in_specs,
            out_specs=[fixed_block(s) for s in shapes],
        ),
        out_shape=[jax.ShapeDtypeStruct(s, f32) for s in shapes],
        input_output_aliases=aliases,
        compiler_params=pltpu.CompilerParams(vmem_limit_bytes=46 << 20),
        cost_estimate=pl.CostEstimate(
            flops=len(offsets) * 2 * rows * depth * cols,
            bytes_accessed=len(offsets) * depth * cols * 2,
            transcendentals=0,
        ),
        name="query_step",
    )(*operands)


def shifted(history, x, k):
    if k == 3:
        return x
    return jnp.concatenate([history[k:3], x[: x.shape[0] - 3 + k]], axis=0)


def conv_silu(history, x, taps):
    total = taps[0:1] * shifted(history, x, 0)
    for k in range(1, 4):
        total = total + taps[k : k + 1] * shifted(history, x, k)
    return total * jax.nn.sigmoid(total)


def spans(heads, width):
    lane = lax.broadcasted_iota(jnp.int32, (heads, heads * width), 1)
    row = lax.broadcasted_iota(jnp.int32, (heads, heads * width), 0)
    return jnp.where(lane // width == row, 1.0, 0.0).astype(f32)


def far_columns(info, half, w_ref, held, arrived):
    depth = held.shape[1]
    at = pl.multiple_of(info[half] * depth, 128)
    return pltpu.make_async_copy(w_ref.at[:, pl.ds(at, depth)], held, arrived)


def first_messages(lhs_ref, held, energy_ref, left_ref, right_ref):
    term = jnp.dot(lhs_ref[...], held[...], preferred_element_type=f32)
    h, depth = left_ref.shape[0], held.shape[1]
    for j, out in enumerate((left_ref, right_ref)):
        side = slice(j * h, (j + 1) * h)
        out[:, :depth] = term[side].astype(bf16)
        if energy_ref is not None:
            out[:, depth : depth + 128] = energy_lanes(energy_ref[side])


def state_kernel(
    slot,
    info,
    x_ref,
    z_ref,
    kept_ref,
    came_ref,
    w_ref,
    hx_ref,
    hbc_ref,
    tx_ref,
    tbc_ref,
    bias_ref,
    rate_ref,
    skip_ref,
    gain_ref,
    own_ref,
    far_ref,
    gated_ref,
    energy_ref,
    final_ref,
    left_ref,
    right_ref,
    initial,
    held,
    arrived,
    *,
    slots,
    half,
):
    i = pl.program_id(0)
    count = info.shape[0]
    copy = far_columns(info, half, w_ref, held, arrived)

    @pl.when(i == 0)
    def _():
        copy.start()

    is_own = slot[i] // slots == info[count - 1]

    @pl.when(is_own)
    def _():
        initial[...] = own_ref[0]

    @pl.when(jnp.logical_not(is_own))
    def _():
        initial[...] = far_ref[0]

    length = x_ref.shape[0]
    heads = bias_ref.shape[1]
    values = conv_silu(hx_ref[0], x_ref[...].astype(bf16).astype(f32), tx_ref[...])
    shared = i // (pl.num_programs(0) // 2) == lax.rem(info[count - 2], 2)
    projected = jnp.where(shared, kept_ref[...], came_ref[...].astype(f32))
    bc = conv_silu(hbc_ref[0], projected[:, : 2 * STATE], tbc_ref[...])
    all_raw = projected[:, 2 * STATE :]
    pick = (all_raw.shape[1], heads)
    chosen = lax.broadcasted_iota(jnp.int32, pick, 0) == (
        lax.broadcasted_iota(jnp.int32, pick, 1) + info[count - 2] * heads
    )
    chosen = jnp.where(chosen, 1.0, 0.0).astype(f32)
    in_state = bc[:, :STATE].astype(bf16)
    out_state = bc[:, STATE:].astype(bf16)
    raw = jnp.dot(all_raw, chosen, precision=highest, preferred_element_type=f32) + bias_ref[...]
    steps = jnp.maximum(raw, 0.0) + jnp.log1p(jnp.exp(-jnp.abs(raw)))
    log_decay = -steps * jnp.exp(rate_ref[...])
    row = lax.broadcasted_iota(jnp.int32, (length, length), 0)
    col = lax.broadcasted_iota(jnp.int32, (length, length), 1)
    lower = jnp.where(row >= col, 1.0, 0.0).astype(f32)
    running = jnp.dot(lower, log_decay, precision=highest, preferred_element_type=f32)
    last = running[length - 1 : length]

    wide = spans(heads, length)
    both = jnp.dot(
        jnp.concatenate([running, steps], axis=0), wide, precision=highest, preferred_element_type=f32
    )
    run_t, step_t = both[:length], both[length:]
    lane = lax.broadcasted_iota(jnp.int32, (length, heads * length), 1) % length
    place = lax.broadcasted_iota(jnp.int32, (length, heads * length), 0)
    diagonal = lane == place
    run_s = jnp.sum(jnp.where(diagonal, run_t, 0.0), axis=0, keepdims=True)
    step_s = jnp.sum(jnp.where(diagonal, step_t, 0.0), axis=0, keepdims=True)
    seen = place >= lane
    decays = jnp.where(seen, jnp.exp(jnp.where(seen, run_t - run_s, 0.0)), 0.0)
    overlap = lax.dot_general(
        out_state,
        jnp.concatenate([in_state] * heads, axis=0),
        (((1,), (1,)), ((), ())),
        preferred_element_type=f32,
    )
    mixing = (overlap * decays * step_s).astype(bf16)
    short = values.astype(bf16)
    group = min(4, heads)
    gl, gw = group * length, group * HDIM
    own_block = (
        lax.broadcasted_iota(jnp.int32, (gl, gw), 0) // length
        == lax.broadcasted_iota(jnp.int32, (gl, gw), 1) // HDIM
    )
    within = []
    for g in range(heads // group):
        v = jnp.concatenate([values[:, g * gw : (g + 1) * gw]] * group, axis=0)
        v = jnp.where(own_block, v, 0.0).astype(bf16)
        within.append(jnp.dot(mixing[:, g * gl : (g + 1) * gl], v, preferred_element_type=f32))
    within = within[0] if len(within) == 1 else jnp.concatenate(within, axis=1)

    narrow = spans(heads, HDIM)
    scales = jnp.dot(
        jnp.concatenate(
            [
                jnp.exp(running),
                jnp.exp(last - running) * steps,
                jnp.broadcast_to(skip_ref[...], (8, heads)),
            ],
            axis=0,
        ),
        narrow,
        precision=highest,
        preferred_element_type=f32,
    )
    start = initial[...]
    carried = lax.dot_general(
        out_state, start.astype(bf16), (((1,), (1,)), ((), ())), preferred_element_type=f32
    )
    result = within + carried * scales[:length] + scales[2 * length : 2 * length + 1] * values
    z = z_ref[...].astype(bf16).astype(f32)
    gated = result * (z * jax.nn.sigmoid(z))
    at = pl.ds(pl.multiple_of(i * length, length), length)
    energy_ref[at, :] = jnp.sum(gated * gated, axis=1, keepdims=True)
    gated_ref[at, :] = (gated * gain_ref[...]).astype(bf16)

    kept = jnp.exp(
        lax.dot_general(
            log_decay,
            jnp.ones((length, STATE), f32),
            (((0,), (0,)), ((), ())),
            precision=highest,
            preferred_element_type=f32,
        )
    )
    update = lax.dot_general(
        (values * scales[length : 2 * length]).astype(bf16),
        in_state,
        (((0,), (0,)), ((), ())),
        preferred_element_type=f32,
    )
    for h in range(heads):
        at = slice(h * HDIM, (h + 1) * HDIM)
        final_ref[0, at, :] = update[at] + start[at] * kept[h : h + 1]

    @pl.when(i == pl.num_programs(0) - 1)
    def _():
        copy.wait()
        first_messages(gated_ref, held, energy_ref, left_ref, right_ref)


def state_pass(
    half, info, slot, inner, kept, came, weight, hx, hbc, tx, tbc, bias, rate, skip, gain, own_pool, far_pool
):
    tenants = slot.shape[0]
    length = inner.shape[0] // 2 // tenants
    cols = inner.shape[1]
    slots = own_pool.shape[0]

    def rows(width):
        return pl.BlockSpec((length, width), lambda i, *s: (i, 0))

    def whole(a):
        return pl.BlockSpec(a.shape, lambda i, *s: (0,) * a.ndim)

    def own_slot(i, slot, info):
        return (jnp.clip(slot[i] - info[info.shape[0] - 1] * slots, 0, slots - 1), 0, 0)

    def far_slot(i, slot, info):
        return (jnp.clip(slot[i] - (1 - info[info.shape[0] - 1]) * slots, 0, slots - 1), 0, 0)

    pooled = (1, cols, STATE)
    message = (tenants * length // 2, weight.shape[1] // (2 * half) + 128)

    def fixed(shape):
        return pl.BlockSpec(shape, lambda i, *s: (0, 0))

    return pl.pallas_call(
        functools.partial(state_kernel, slots=slots, half=half),
        grid_spec=pltpu.PrefetchScalarGridSpec(
            num_scalar_prefetch=2,
            grid=(tenants,),
            in_specs=[
                rows(cols),
                pl.BlockSpec((length, cols), lambda i, *s: (tenants + i, 0)),
                pl.BlockSpec((length, kept.shape[1]), lambda i, *s: (i % (tenants // 2), 0)),
                pl.BlockSpec((length, kept.shape[1]), lambda i, *s: (i % (tenants // 2), 0)),
                pl.BlockSpec(memory_space=pl.ANY),
                pl.BlockSpec((1, 3, cols), lambda i, *s: (i, 0, 0)),
                pl.BlockSpec((1, 3, 2 * STATE), lambda i, *s: (i, 0, 0)),
                whole(tx),
                whole(tbc),
                whole(bias),
                whole(rate),
                whole(skip),
                whole(gain),
                pl.BlockSpec(pooled, own_slot),
                pl.BlockSpec(pooled, far_slot),
            ],
            out_specs=[
                fixed((tenants * length, cols)),
                fixed((tenants * length, 1)),
                pl.BlockSpec(pooled, lambda i, *s: (i, 0, 0)),
                fixed(message),
                fixed(message),
            ],
            scratch_shapes=[
                pltpu.VMEM((cols, STATE), f32),
                pltpu.VMEM((weight.shape[0], message[1] - 128), bf16),
                pltpu.SemaphoreType.DMA,
            ],
        ),
        out_shape=[
            jax.ShapeDtypeStruct((tenants * length, cols), bf16),
            jax.ShapeDtypeStruct((tenants * length, 1), f32),
            jax.ShapeDtypeStruct((tenants, cols, STATE), f32),
            jax.ShapeDtypeStruct(message, bf16),
            jax.ShapeDtypeStruct(message, bf16),
        ],
        compiler_params=pltpu.CompilerParams(vmem_limit_bytes=48 << 20),
        cost_estimate=pl.CostEstimate(
            flops=tenants * 6 * length * cols * STATE,
            bytes_accessed=tenants * cols * STATE * 10,
            transcendentals=0,
        ),
        name="state_pass",
    )(slot, info, inner, inner, kept, came, weight, hx, hbc, tx, tbc, bias, rate, skip, gain, own_pool, far_pool)


def attend_kernel(
    half, width, table, limit, adapter, info, q_ref, low_ref, up_ref, near_ref, far_ref, w_ref, *refs
):
    o_ref, left_ref, right_ref, held, arrived = refs[-5:]
    copy = far_columns(info, half, w_ref, held, arrived)

    @pl.when(pl.program_id(0) == 0)
    def _():
        copy.start()

    i = pl.program_id(0)
    length = q_ref.shape[0]
    heads = q_ref.shape[1] // HEAD_SIZE
    blocks = table.shape[1]
    part = near_ref.shape[1]
    core = info[info.shape[0] - 1]
    rank = up_ref.shape[1]
    square = low_ref[:, rank : rank + 1] + low_ref[:, rank + 1 : rank + 2]
    norm = lax.rsqrt(square / width + epsilon)
    low = (low_ref[:, :rank] * norm).astype(bf16)
    raised = jnp.dot(low, up_ref[0], preferred_element_type=f32)
    q = (q_ref[...] * norm + adapter_scale * raised).astype(bf16)
    q = jnp.concatenate([q[:, h * HEAD_SIZE : (h + 1) * HEAD_SIZE] for h in range(heads)], axis=0)
    fresh = jnp.concatenate([refs[0][...], refs[1][...]], axis=1)
    for came in refs[2:-5]:
        fresh = fresh + came[...].astype(f32)
    fresh = (fresh * norm).astype(bf16)
    pieces = []
    for j in range(blocks):
        at = table[i, j]
        pieces += [near_ref[at], far_ref[at]]
    cached = jnp.concatenate(pieces, axis=0)
    context = cached.shape[0]
    nt = (((1,), (1,)), ((), ()))
    scale = HEAD_SIZE ** (-0.5)
    old = lax.dot_general(q, cached[:, :HEAD_SIZE], nt, preferred_element_type=f32) * scale
    new = lax.dot_general(q, fresh[:, :HEAD_SIZE], nt, preferred_element_type=f32) * scale
    lane = lax.broadcasted_iota(jnp.int32, old.shape, 1)
    inside = lane % (2 * part)
    far_side = jnp.where(inside >= part, 1, 0)
    half = jnp.where(core == 0, far_side, 1 - far_side)
    place = (lane // (2 * part)) * (2 * part) + half * part + inside % part
    old_seen = place < limit[i]
    token = lax.broadcasted_iota(jnp.int32, new.shape, 0) % length
    new_seen = lax.broadcasted_iota(jnp.int32, new.shape, 1) <= token
    old = jnp.where(old_seen, old, -jnp.inf)
    new = jnp.where(new_seen, new, -jnp.inf)
    top = jnp.maximum(jnp.max(old, axis=1, keepdims=True), jnp.max(new, axis=1, keepdims=True))
    old = jnp.where(old_seen, jnp.exp(old - top), 0.0)
    new = jnp.where(new_seen, jnp.exp(new - top), 0.0)
    share = 1.0 / (jnp.sum(old, axis=1, keepdims=True) + jnp.sum(new, axis=1, keepdims=True))
    out = jnp.dot((old * share).astype(bf16), cached[:, HEAD_SIZE:], preferred_element_type=f32)
    out += jnp.dot((new * share).astype(bf16), fresh[:, HEAD_SIZE:], preferred_element_type=f32)
    out = out.astype(bf16)
    own_rows = pl.ds(pl.multiple_of(i * length, length), length)
    for h in range(heads):
        o_ref[own_rows, h * HEAD_SIZE : (h + 1) * HEAD_SIZE] = out[h * length : (h + 1) * length]

    @pl.when(i == pl.num_programs(0) - 1)
    def _():
        copy.wait()
        first_messages(o_ref, held, None, left_ref, right_ref)


def attend(ring, width, table, limit, adapter, info, q, low, up, near, far, weight, kv, came):
    tenants = table.shape[0]
    length = q.shape[0] // tenants

    def rows(a):
        return pl.BlockSpec((length, a.shape[1]), lambda i, *s: (i, 0))

    def whole(a):
        return pl.BlockSpec(a.shape, lambda i, *s: (0,) * a.ndim)

    message = (q.shape[0] // 2, weight.shape[1] // ring.n)

    def fixed(shape):
        return pl.BlockSpec(shape, lambda i, *s: (0, 0))

    def own(base):
        return pl.BlockSpec(
            (length, HEAD_SIZE), lambda i, t, n, a, info: (i, base + info[ring.n])
        )

    return pl.pallas_call(
        functools.partial(attend_kernel, ring.half, width),
        grid_spec=pltpu.PrefetchScalarGridSpec(
            num_scalar_prefetch=4,
            grid=(tenants,),
            in_specs=[
                rows(q),
                rows(low),
                pl.BlockSpec((1, *up.shape[1:]), lambda i, t, n, a, info: (a[i], 0, 0)),
                whole(near),
                whole(far),
                pl.BlockSpec(memory_space=pl.ANY),
                own(0),
                own(KEY_HEADS),
            ]
            + [rows(a) for a in came],
            out_specs=[fixed(q.shape), fixed(message), fixed(message)],
            scratch_shapes=[
                pltpu.VMEM((weight.shape[0], message[1]), bf16),
                pltpu.SemaphoreType.DMA,
            ],
        ),
        out_shape=[
            jax.ShapeDtypeStruct(q.shape, bf16),
            jax.ShapeDtypeStruct(message, bf16),
            jax.ShapeDtypeStruct(message, bf16),
        ],
        compiler_params=pltpu.CompilerParams(vmem_limit_bytes=46 << 20),
        cost_estimate=pl.CostEstimate(
            flops=tenants * 4 * length * q.shape[1] * 288,
            bytes_accessed=near.size * 4 + q.size * 6 + up.size,
            transcendentals=0,
        ),
        name="attend",
    )(table, limit, adapter, info, q, low, up, near, far, weight, kv, kv, *came)


def pick_kernel(heads, info, pool_ref, o_ref):
    for d, head in enumerate(heads):
        for k in range(2):
            at = (head + k * KEY_HEADS) * HEAD_SIZE
            o_ref[d, :, :, k * HEAD_SIZE : (k + 1) * HEAD_SIZE] = pool_ref[:, :, at : at + HEAD_SIZE]


def pick_heads(info, pool, heads, pools):
    count, block_len, wide = pool.shape
    part = block_len // pools
    shape = (len(heads), count, part, 2 * HEAD_SIZE)
    return pl.pallas_call(
        functools.partial(pick_kernel, heads),
        grid_spec=pltpu.PrefetchScalarGridSpec(
            num_scalar_prefetch=1,
            grid=(1,),
            in_specs=[pl.BlockSpec((count, part, wide), lambda j, info: (0, info[info.shape[0] - 1], 0))],
            out_specs=pl.BlockSpec(shape, lambda j, info: (0, 0, 0, 0)),
        ),
        out_shape=jax.ShapeDtypeStruct(shape, bf16),
        compiler_params=pltpu.CompilerParams(vmem_limit_bytes=8 << 20),
        name="pick_heads",
    )(info, pool)


def fresh_kernel(kind, offsets, heads_at, info, kv_ref, *refs):
    outs = refs[-2:]
    got = refs[:-2]
    rows = kv_ref.shape[0]
    h = rows // 2
    sides = [slice(0, h), slice(h, rows)]
    for j in range(2):
        offset = offsets[0] if kind == "first" else offsets[j]
        head = info[heads_at + offset]
        for k in range(2):
            at = pl.ds(pl.multiple_of((head + k * KEY_HEADS) * HEAD_SIZE, HEAD_SIZE), HEAD_SIZE)
            to = slice(k * HEAD_SIZE, (k + 1) * HEAD_SIZE)
            if kind == "first":
                outs[j][:, to] = kv_ref[sides[j], at].astype(bf16)
            elif kind == "second":
                mine, other = sides[j], sides[1 - j]
                outs[j][mine, to] = (kv_ref[mine, at] + got[j][:, to].astype(f32)).astype(bf16)
                outs[j][other, to] = kv_ref[other, at].astype(bf16)
            else:
                outs[j][:, to] = (kv_ref[:, at] + got[j][:, to].astype(f32)).astype(bf16)


def fresh_join(info, kind, offsets, heads_at, kv, got):
    rows = kv.shape[0]
    shape = (rows // 2 if kind == "first" else rows, 2 * HEAD_SIZE)
    operands = [kv, *got]
    return pl.pallas_call(
        functools.partial(fresh_kernel, kind, offsets, heads_at),
        grid_spec=pltpu.PrefetchScalarGridSpec(
            num_scalar_prefetch=1,
            grid=(1,),
            in_specs=[pl.BlockSpec(a.shape, lambda j, info: (0, 0)) for a in operands],
            out_specs=[pl.BlockSpec(shape, lambda j, info: (0, 0))] * 2,
        ),
        out_shape=[jax.ShapeDtypeStruct(shape, bf16)] * 2,
        compiler_params=pltpu.CompilerParams(vmem_limit_bytes=8 << 20),
        name="fresh_join",
    )(info, *operands)


def per_device(
    ring,
    tokens,
    mamba_in_weight,
    state_projection,
    inner_taps,
    state_taps,
    inner_history,
    state_history,
    step_size_bias,
    log_decay_rate,
    skip_factor,
    gated_norm_gain,
    mamba_out_weight,
    saved_state_pool,
    tenant_state_slot,
    attention_gain,
    query_matrix,
    adapter_down,
    adapter_up,
    tenant_adapter,
    key_value_weight,
    key_value_pool,
    tenant_blocks,
    cached_length,
    attention_out_weight,
):
    n, half, pools = ring.n, ring.half, ring.pools
    tenants, length, depth = tokens.shape
    rows = tenants * length
    width = depth * n
    info = ring.info()
    own_tokens = tokens.reshape(rows, depth)
    heads = step_size_bias.shape[0]
    cols = mamba_in_weight.shape[2]
    swap = [(i, (i + 1) % pools) for i in range(pools)]

    slots = saved_state_pool.shape[0]
    flat_pool = saved_state_pool.reshape(slots, heads * HDIM, STATE)
    far_pool = lax.ppermute(flat_pool, "pool", swap)

    inner, kept, came, cache = ring.gather(
        own_tokens,
        lambda offsets, blocks, acc: in_product(info, offsets, blocks, mamba_in_weight, depth, acc),
        lambda x: partial_product(info, x, state_projection),
        pick_heads(info, key_value_pool, ring.heads, pools),
    )
    cache = cache.reshape(-1, *cache.shape[2:])

    gated, energy, final_state, a, b = state_pass(
        half,
        info,
        tenant_state_slot,
        inner,
        kept,
        came,
        mamba_out_weight,
        inner_history.astype(f32),
        state_history,
        inner_taps.astype(f32),
        state_taps.astype(f32),
        step_size_bias[None],
        log_decay_rate[None],
        skip_factor[None],
        gated_norm_gain[None],
        flat_pool,
        far_pool,
    )
    terms, got, (cache, far_cache) = ring_sum(ring, info, a, b, gated, mamba_out_weight, depth, energy, cache)
    first, message = mixer_step(
        info,
        tenant_adapter,
        terms,
        got,
        energy,
        own_tokens,
        attention_gain[None],
        adapter_down.transpose(0, 2, 1),
        cols * n,
    )

    kv = jnp.dot(message[:, :depth], key_value_weight, preferred_element_type=f32)

    h = rows // 2
    a, b = message, message
    ka, kb = fresh_join(info, "first", [half], n, kv, [])
    accs, ready = None, ([0], [message])
    for s in range(1, half + 1):
        if s == half:
            a, b = a[:h], b[h:]
        a, b, ka, kb = ring.right(a), ring.left(b), ring.right(ka), ring.left(kb)
        accs = query_step(info, *ready, query_matrix, depth, accs)
        a, b, ka, kb, accs = lax.optimization_barrier((a, b, ka, kb, accs))
        ready = ([n - s, s], [a, b]) if s < half else ([half], [a, b])
        if s < half:
            kind = "second" if s == 1 else "later"
            ka, kb = fresh_join(info, kind, [half - s, n - half + s], n, kv, [ka, kb])
    kv_came = [ka, kb] if half > 1 else [jnp.concatenate([ka, kb], axis=0)]
    query, low = query_step(info, *ready, query_matrix, depth, accs)
    heads_out, a, b = attend(
        ring,
        width,
        tenant_blocks,
        cached_length,
        tenant_adapter,
        info,
        query,
        low,
        adapter_up,
        cache,
        far_cache,
        attention_out_weight,
        kv,
        kv_came,
    )
    terms, got, _ = ring_sum(ring, info, a, b, heads_out, attention_out_weight, depth)
    second = terms + first.astype(f32)
    for g in got:
        second = second + g.astype(f32)
    second = second.astype(bf16)
    return (
        second.reshape(tenants, length, depth),
        final_state.reshape(tenants, heads, HDIM, STATE),
    )


def solution(mesh):
    in_specs = (
        P(("groups", "pool"), None, "tensor"),
        P(None, None, "tensor"),
        P("tensor", None),
        P(None, "tensor"),
        P(),
        P(("groups", "pool"), None, "tensor"),
        P(("groups", "pool"), None, None),
        P("tensor"),
        P("tensor"),
        P("tensor"),
        P("tensor"),
        P("tensor", None),
        P(("groups", "pool"), "tensor", None, None),
        P(("groups", "pool")),
        P(),
        P(None, "tensor"),
        P(None, "tensor", None),
        P(None, None, "tensor"),
        P(("groups", "pool")),
        P("tensor", None),
        P(("groups", "tensor"), None, None),
        P(("groups", "pool"), None),
        P(("groups", "pool")),
        P("tensor", None),
    )
    out_specs = (P(("groups", "pool"), None, "tensor"), P(("groups", "pool"), "tensor", None, None))
    ring = Ring(mesh.shape["tensor"], mesh.shape["pool"])
    return jax.shard_map(
        functools.partial(per_device, ring),
        mesh=mesh,
        in_specs=in_specs,
        out_specs=out_specs,
        check_vma=False,
    )
```
